32 devices in a mesh: seq: 8 (over y, x, core), tp: 4 (over z).
Axes of the slice: x: 2, y: 2, z: 4, core: 2. Of those that a mesh axis runs over, the one named last changes fastest.
Arguments:
- tokens: bfloat16 [4096, 1024], P('seq', 'tp'), may hold values from -6 to 6
- variate: int32 [4096], P('seq'), may hold values from 0 to 3
- positions: int32 [4096], P('seq'), may hold values from 0 to 511
- lengths: int32 [4], replicated, may hold values from 1 to 2048, 4096 in all
- page_table: int32 [72], replicated, may hold values from 0 to 71, each once
- gain_attn: bfloat16 [1024], replicated, may hold values from 0.099609375 to 1.8984375
- w_query: bfloat16 [1024, 512], P(None, 'tp'), may hold values from -1 to 1
- w_key: bfloat16 [1024, 512], P(None, 'tp'), may hold values from -1 to 1
- w_value: bfloat16 [1024, 512], P(None, 'tp'), may hold values from -0.1875 to 0.1875
- var_bias: float32 [2, 8], P(None, 'tp'), may hold values from -2 to 2
- w_out: bfloat16 [512, 1024], P('tp'), may hold values from -0.25 to 0.25
- gain_ffn: bfloat16 [1024], replicated, may hold values from 0.099609375 to 1.8984375
- w_gate: bfloat16 [1024, 4096], P(None, 'tp'), may hold values from -0.1875 to 0.1875
- w_up: bfloat16 [1024, 4096], P(None, 'tp'), may hold values from -0.1875 to 0.1875
- w_down: bfloat16 [4096, 1024], P('tp'), may hold values from -0.09375 to 0.09375
Outputs:
- mixed: bfloat16 [4096, 1024], P('seq', 'tp')
- cache: bfloat16 [4608, 2, 512], P('seq', None, 'tp')
The draws below stay inside these ranges and needn't reach their ends.
Inputs may be any that keep to these rules, and one draw needn't show every extreme that they name: The lengths fill all 4096 token positions in order; some request has exactly 2048 tokens. `page_table`: each physical page appears once.
All inputs are finite; a program needn't handle non-finite values.
Results may differ from the reference program's by a relative error of at most 0.018.
Values may be sent and summed in bfloat16 or wider, within the bound.
No kernel may reach another device: no remote copies, remote signals or barrier semaphores. Data moves between devices by JAX's collectives and lax.ppermute only.
A program may use at most 64 MiB of HBM per device.

```python
import math
import jax
import jax.numpy as jnp
import numpy as np
from jax import lax

D = 1024
HD = 64
FF = 4096
TOK_DEV = 512
PAGE = 64
VARS = 4
TIMES = 512
HEADS = 8
TOKENS = 4096
LEN_MAX = 2048
REQS = 4
PAGES = 72
CACHE_ROWS = 4608


def query_key_pair(key):
    own_query = jax.random.normal(jax.random.fold_in(key, 11), (D, HEADS * HD), jnp.float32)
    own_key = jax.random.normal(jax.random.fold_in(key, 13), (D, HEADS * HD), jnp.float32)
    scale = D ** (-0.5)
    query_part = own_query * scale
    key_part = own_key * scale
    limit = 32.0 * scale
    return (jnp.clip(query_part, -limit, limit), jnp.clip(key_part, -limit, limit))


def draw_w_query(key, part):
    return query_key_pair(key)[0].astype(jnp.bfloat16)


def draw_w_key(key, part):
    return query_key_pair(key)[1].astype(jnp.bfloat16)


def touch_ends(drawn, key, smallest, high):
    shape = drawn.shape
    spot = [jax.random.randint(jax.random.fold_in(key, axis), (), 0, shape[axis]) for axis in range(len(shape))]
    drawn = drawn.at[tuple(spot)].set(smallest)
    longest = shape.index(max(shape))
    spot[longest] = (spot[longest] + 1) % shape[longest]
    return drawn.at[tuple(spot)].set(high)


def levels(key, dims, shards, least, high):
    def one(axis_at, shards_of):
        steps = jax.random.uniform(jax.random.fold_in(jax.random.fold_in(key, 6), axis_at), (shards_of,), jnp.float32, least / len(shards), high / len(shards))
        return jnp.repeat(jnp.exp(steps), dims[axis_at] // shards_of).reshape((-1,) + (1,) * (len(dims) - axis_at - 1))

    level = one(*shards[0])
    for cut in shards[1:]:
        level = level * one(*cut)
    return level


def length_profile(amount, total, most, slope):
    portions = [(1 << 20) // math.isqrt(rank ** slope) + 1 for rank in range(2, amount + 1)]
    rest, counts = total - most - (amount - 1), [1] * (amount - 1)
    while rest > 0:
        free = [i for i in range(amount - 1) if counts[i] < most]
        whole, left = sum([portions[i] for i in free]), rest
        for i in free:
            more = min(most - counts[i], max(1, left * portions[i] // whole), rest)
            counts[i] = counts[i] + more
            rest = rest - more
    return np.array([most] + counts)


def ragged_sizes(key, number_of, total, most, lean):
    if number_of == 2:
        one = jax.random.randint(key, (), max(1, total - most), min(most, total - 1) + 1)
        return jnp.stack([one, total - one])
    sizes = jnp.asarray(length_profile(number_of, total, most, lean), jnp.int32)
    twos = (number_of - 1) // 2
    donor, receiver = sizes[1:1 + 2 * twos:2], sizes[2:2 + 2 * twos:2]
    margin = jnp.minimum(donor - 1, most - receiver)
    shifted = jax.random.randint(jax.random.fold_in(key, 1), (twos,), 0, 1 << 20) % (margin + 1)
    sizes = sizes.at[1:1 + 2 * twos:2].set(donor - shifted).at[2:2 + 2 * twos:2].set(receiver + shifted)
    return sizes[jax.random.permutation(jax.random.fold_in(key, 2), number_of)]


def bell_draw(stream_key, shape, width, reach, pieces=(), kind=jnp.bfloat16):
    loudness = levels(stream_key, shape, pieces, -0.22, 0.18) if pieces else 1.0
    drawn = jax.random.normal(stream_key, shape, jnp.float32) * width * loudness
    return jnp.minimum(jnp.maximum(drawn, -reach), reach).astype(kind)


def setup_inputs(seed: int = 0) -> dict:
    seeds = jax.random.split(jax.random.key(seed), 16)
    return {
        "tokens": bell_draw(seeds[0], (TOKENS, D), 1.0, 6.0, ((0, 8), (1, 4))),
        "variate": touch_ends(jax.random.randint(seeds[1], (TOKENS,), 0, VARS), jax.random.fold_in(seeds[1], 1), 0, VARS - 1).astype(jnp.int32),
        "positions": touch_ends(jax.random.randint(seeds[2], (TOKENS,), 0, TIMES), jax.random.fold_in(seeds[2], 1), 0, TIMES - 1).astype(jnp.int32),
        "lengths": ragged_sizes(seeds[3], REQS, TOKENS, LEN_MAX, 2).astype(jnp.int32),
        "page_table": jax.random.permutation(seeds[4], PAGES).astype(jnp.int32),
        "gain_attn": jnp.clip(1.0 + 0.18 * jax.random.normal(seeds[5], (D,), jnp.float32), 0.099609375, 1.8984375).astype(jnp.bfloat16),
        "w_query": draw_w_query(jax.random.fold_in(seeds[15], 71), 0),
        "w_key": draw_w_key(jax.random.fold_in(seeds[15], 71), 0),
        "w_value": bell_draw(seeds[8], (D, HEADS * HD), D ** -0.5, 0.1875, ((1, 4),)),
        "var_bias": jnp.clip(jax.random.uniform(seeds[9], (2, HEADS), jnp.float32, -2.0, 2.0) * levels(seeds[9], (2, HEADS), ((1, 4),), -0.4, 0.0), -2.0, 2.0),
        "w_out": bell_draw(seeds[10], (HEADS * HD, D), (HEADS * HD) ** -0.5, 0.25, ((0, 4),)),
        "gain_ffn": jnp.clip(1.0 + 0.18 * jax.random.normal(seeds[11], (D,), jnp.float32), 0.099609375, 1.8984375).astype(jnp.bfloat16),
        "w_gate": bell_draw(seeds[12], (D, FF), D ** -0.5, 0.1875, ((1, 4),)),
        "w_up": bell_draw(seeds[13], (D, FF), D ** -0.5, 0.1875, ((1, 4),)),
        "w_down": bell_draw(seeds[14], (FF, D), FF ** -0.5, 0.09375, ((0, 4),)),
    }


def root_mean_norm(values, gain):
    values = values.astype(jnp.float32)
    scale = lax.rsqrt(lax.optimization_barrier(jnp.mean(values * values, axis=-1, keepdims=True)) + 1e-06)
    return values * scale * gain.astype(jnp.float32)

def rotate(vectors, positions):
    half_dim = vectors.shape[-1] // 2
    frequency = 10000.0 ** (-jnp.arange(half_dim, dtype=jnp.float32) / half_dim)
    angles = positions.astype(jnp.float32)[:, None] * frequency[None, :]
    cosine = jnp.cos(angles)[:, None, :]
    sine_part = jnp.sin(angles)[:, None, :]
    first_half = vectors[..., :half_dim]
    second_half = vectors[..., half_dim:]
    return jnp.concatenate([first_half * cosine - second_half * sine_part, second_half * cosine + first_half * sine_part], axis=-1)

def segment_of(index, request_ends):
    return lax.optimization_barrier(jnp.sum((index[:, None] >= request_ends[None, :]).astype(jnp.int32), axis=1)).astype(jnp.int32)

def cache_slots(lengths, page_table, index):
    request_ends = jnp.cumsum(lengths).astype(jnp.int32)
    request_starts = request_ends - lengths
    page_counts = (lengths + PAGE - 1) // PAGE
    page_bases = jnp.cumsum(page_counts).astype(jnp.int32) - page_counts
    segment = segment_of(index, request_ends)
    chosen = segment[:, None] == jnp.arange(lengths.shape[0], dtype=jnp.int32)[None, :]
    offset_in = index - lax.optimization_barrier(jnp.sum(jnp.where(chosen, request_starts[None, :], 0), axis=1)).astype(jnp.int32)
    logical = lax.optimization_barrier(jnp.sum(jnp.where(chosen, page_bases[None, :], 0), axis=1)).astype(jnp.int32) + offset_in // PAGE
    page_ids = jnp.arange(page_table.shape[0], dtype=jnp.int32)
    physical = lax.optimization_barrier(jnp.sum(jnp.where(logical[:, None] == page_ids[None, :], page_table[None, :], 0), axis=1)).astype(jnp.int32)
    return physical * PAGE + offset_in % PAGE

def reference(tokens, variate, positions, lengths, page_table, gain_attn, w_query, w_key, w_value, var_bias, w_out, gain_ffn, w_gate, w_up, w_down):
    index = jnp.arange(TOKENS, dtype=jnp.int32)
    normed = root_mean_norm(tokens, gain_attn).astype(jnp.bfloat16)
    query_rows = rotate(jnp.dot(normed, w_query, preferred_element_type=jnp.float32).reshape(TOKENS, HEADS, HD), positions).astype(jnp.bfloat16)
    key_rows = rotate(jnp.dot(normed, w_key, preferred_element_type=jnp.float32).reshape(TOKENS, HEADS, HD), positions).astype(jnp.bfloat16)
    value_rows = jnp.dot(normed, w_value, preferred_element_type=jnp.float32).astype(jnp.bfloat16).reshape(TOKENS, HEADS, HD)
    request_ends = jnp.cumsum(lengths).astype(jnp.int32)
    segment = segment_of(index, request_ends)
    window = min(LEN_MAX + TOK_DEV, TOKENS)

    def one_block(block):
        first = (block * TOK_DEV).astype(jnp.int32)
        key_first = jnp.clip(first + TOK_DEV - window, 0, TOKENS - window).astype(jnp.int32)
        query_block = lax.dynamic_slice_in_dim(query_rows, first, TOK_DEV, 0).astype(jnp.float32)
        key_block = lax.dynamic_slice_in_dim(key_rows, key_first, window, 0).astype(jnp.float32)
        value_block = lax.dynamic_slice_in_dim(value_rows, key_first, window, 0).astype(jnp.float32)
        query_index = first + jnp.arange(TOK_DEV, dtype=jnp.int32)
        key_index = key_first + jnp.arange(window, dtype=jnp.int32)
        query_segment = lax.dynamic_slice_in_dim(segment, first, TOK_DEV, 0)
        key_segment = lax.dynamic_slice_in_dim(segment, key_first, window, 0)
        query_variate = lax.dynamic_slice_in_dim(variate, first, TOK_DEV, 0)
        key_variate = lax.dynamic_slice_in_dim(variate, key_first, window, 0)
        scores = jnp.einsum('qhd,khd->hqk', query_block, key_block) * HD ** (-0.5)
        same = query_variate[:, None] == key_variate[None, :]
        scores = scores + jnp.where(same[None], var_bias[0][:, None, None], var_bias[1][:, None, None])
        visible = (query_segment[:, None] == key_segment[None, :]) & (query_index[:, None] >= key_index[None, :])
        scores = jnp.where(visible[None], scores, -1e+30)
        peak = lax.optimization_barrier(jnp.max(scores, axis=-1, keepdims=True))
        weights = jnp.where(visible[None], jnp.exp(scores - peak), 0.0)
        totals = lax.optimization_barrier(jnp.sum(weights, axis=-1))
        rounded = lax.optimization_barrier(weights.astype(jnp.bfloat16)).astype(jnp.float32)
        summed = jnp.einsum('hqk,khd->qhd', rounded, value_block) / jnp.transpose(totals)[:, :, None]
        return summed.reshape(TOK_DEV, HEADS * HD).astype(jnp.bfloat16)
    attended = lax.map(one_block, jnp.arange(TOKENS // TOK_DEV, dtype=jnp.int32)).reshape(TOKENS, HEADS * HD)
    projected = jnp.dot(attended, w_out, preferred_element_type=jnp.float32)
    residual = (tokens.astype(jnp.float32) + projected).astype(jnp.bfloat16)
    normed_mid = root_mean_norm(residual, gain_ffn).astype(jnp.bfloat16)
    gate_part = jnp.dot(normed_mid, w_gate, preferred_element_type=jnp.float32)
    up_part = jnp.dot(normed_mid, w_up, preferred_element_type=jnp.float32)
    hidden = (jax.nn.silu(gate_part) * up_part).astype(jnp.bfloat16)
    mixed = (residual.astype(jnp.float32) + jnp.dot(hidden, w_down, preferred_element_type=jnp.float32)).astype(jnp.bfloat16)
    stacked = jnp.stack([key_rows.reshape(TOKENS, HEADS * HD), value_rows.reshape(TOKENS, HEADS * HD)], axis=1)
    slots = cache_slots(lengths, page_table, index)
    cache = jnp.zeros((CACHE_ROWS, 2, HEADS * HD), jnp.bfloat16).at[slots].set(stacked)
    return (mixed, cache)
```

```python
import functools

import jax
import jax.numpy as jnp
from jax import lax
from jax.experimental import pallas as pl
from jax.experimental.pallas import tpu as pltpu
from jax.sharding import PartitionSpec as P

HD = 64
PAGE = 64
VARS = 4
BIAS_PARTS = 3
LANES = 128
HIDDEN_SCORE = -1e30
EPS = 1e-06

VMEM = pl.BlockSpec(memory_space=pltpu.VMEM)
SMEM = pl.BlockSpec(memory_space=pltpu.SMEM)
ANY = pl.BlockSpec(memory_space=pl.ANY)


def params(mib):
    return pltpu.CompilerParams(vmem_limit_bytes=mib << 20)


def cost(flops, nbytes, exps=0):
    return pl.CostEstimate(flops=flops, bytes_accessed=nbytes, transcendentals=exps)


def dot_f32(left, right):
    return jnp.dot(left, right, preferred_element_type=jnp.float32)


def line_gather(shard):
    far = lax.ppermute(shard, "tp", [(0, 2), (1, 3), (2, 0), (3, 1)])
    left = lax.ppermute(shard, "tp", [(0, 1), (1, 2), (2, 3)])
    right = lax.ppermute(shard, "tp", [(3, 2), (2, 1), (1, 0)])
    ends = lax.ppermute(far, "tp", [(2, 3), (1, 0)])
    return [shard, left, right, far, ends]


def gather_pieces(shard):
    if lax.axis_size("tp") == 4:
        return line_gather(shard)
    whole = lax.all_gather(shard, "tp", axis=0)
    return [whole[i] for i in range(whole.shape[0])]


def piece_count():
    return 5 if lax.axis_size("tp") == 4 else lax.axis_size("tp")


def assemble(pieces, place, target, on_line):
    width = pieces[0].shape[1]

    def put(block, value):
        target[:, pl.ds(pl.multiple_of(block * width, width), width)] = value

    if not on_line:
        for i, piece in enumerate(pieces):
            target[:, i * width : (i + 1) * width] = piece[...]
        return
    own, left, right, far, ends = pieces
    put(place, own[...])
    put(lax.rem(place + 2, 4), far[...])
    put(lax.rem(place + 3, 4), jnp.where(place == 0, ends[...], left[...]))
    put(lax.rem(place + 1, 4), jnp.where(place == 3, ends[...], right[...]))


def rotate_lanes(vectors, cosine, signed_sine):
    lane = lax.broadcasted_iota(jnp.int32, vectors.shape, 1)
    half = HD // 2
    ahead = pltpu.roll(vectors, vectors.shape[1] - half, 1)
    behind = pltpu.roll(vectors, half, 1)
    partner = jnp.where(lane % HD < half, ahead, behind)
    return vectors * cosine + partner * signed_sine


def norm_rows(values, gain):
    scale = lax.rsqrt(jnp.mean(values * values, axis=-1, keepdims=True) + EPS)
    return (values * scale * gain).astype(jnp.bfloat16)


def project_kernel(count, on_line, place_ref, *refs):
    pieces = refs[:count]
    gain, w_q, w_k, w_v, cosine, sine, tokens, queries, pairs = refs[count:]
    assemble(pieces, place_ref[0], tokens, on_line)
    rows = tokens.shape[0]
    width = w_q.shape[1]
    step = min(rows, 256)
    gain_row = gain[...].astype(jnp.float32)
    for first in range(0, rows, step):
        part = pl.ds(first, step)
        normed = norm_rows(tokens[part, :].astype(jnp.float32), gain_row)
        cos_part, sin_part = cosine[part, :], sine[part, :]
        query = rotate_lanes(dot_f32(normed, w_q[...]), cos_part, sin_part)
        queries[part, :] = query.astype(jnp.bfloat16) * jnp.bfloat16(HD**-0.5)
        key = rotate_lanes(dot_f32(normed, w_k[...]), cos_part, sin_part)
        pairs[part, :width] = key.astype(jnp.bfloat16)
        pairs[part, width:] = dot_f32(normed, w_v[...]).astype(jnp.bfloat16)


def project(pieces, place, gain, w_query, w_key, w_value, cosine, sine):
    rows, part = pieces[0].shape
    width = w_query.shape[1]
    features = w_query.shape[0]
    on_line = lax.axis_size("tp") == 4
    return pl.pallas_call(
        functools.partial(project_kernel, len(pieces), on_line),
        out_shape=[
            jax.ShapeDtypeStruct((rows, features), jnp.bfloat16),
            jax.ShapeDtypeStruct((rows, width), jnp.bfloat16),
            jax.ShapeDtypeStruct((rows, 2 * width), jnp.bfloat16),
        ],
        in_specs=[SMEM] + [VMEM] * (len(pieces) + 6),
        out_specs=[VMEM] * 3,
        compiler_params=params(24),
        cost_estimate=cost(6 * rows * features * width, 4 << 20),
        name="project",
    )(place, *pieces, gain, w_query, w_key, w_value, cosine, sine)


def seq_xor(value, mask):
    return lax.ppermute(value, "seq", [(i, i ^ mask) for i in range(lax.axis_size("seq"))])


def seq_pieces(pairs):
    if lax.axis_size("seq") == 8:
        across = seq_xor(pairs, 2)
        down = seq_xor(pairs, 4)
        twin = seq_xor(pairs, 1)
        diagonal = seq_xor(across, 4)
        across_twin = seq_xor(across, 1)
        down_twin = seq_xor(down, 1)
        diagonal_twin = seq_xor(diagonal, 1)
        return [pairs, twin, across, across_twin, down, down_twin, diagonal, diagonal_twin]
    return [lax.all_gather(pairs, "seq", axis=0)]


def piece_copies(pieces, me, wanted):
    if len(pieces) > 1:
        for m, piece in enumerate(pieces):
            wanted(piece, me ^ m)
    else:
        for j in range(pieces[0].shape[0]):
            wanted(pieces[0].at[j], j)


def attend_kernel(count, heads, reach, info, queries, query_marks, key_marks, *refs):
    pieces = refs[:count]
    out, q_buf, k_buf, v_buf, scores, peak, total, sems = refs[count:]
    me, last = info[0], info[1]
    rows = queries.shape[0]
    width = queries.shape[1]

    def copies(source, block, slot):
        return [
            pltpu.make_async_copy(
                source.at[:, pl.ds(0, width)], k_buf.at[slot, :, pl.ds(0, width)], sems.at[slot, 0]
            ),
            pltpu.make_async_copy(
                source.at[:, pl.ds(width, width)],
                v_buf.at[slot, :, pl.ds(0, width)],
                sems.at[slot, 1],
            ),
            pltpu.make_async_copy(
                key_marks.at[pl.ds(pl.multiple_of(block * rows, rows), rows), :],
                k_buf.at[slot, :, pl.ds(width, LANES)],
                sems.at[slot, 2],
            ),
        ]

    def begin(source, block):
        distance = me - block

        @pl.when((distance >= 0) & (distance <= last))
        def _():
            for copy in copies(source, block, distance):
                copy.start()

    piece_copies(pieces, me, begin)
    example = pieces[0] if count > 1 else pieces[0].at[0]

    def finish(slot):
        for copy in copies(example, 0, slot):
            copy.wait()

    lane = lax.broadcasted_iota(jnp.int32, (rows, width), 1)
    for h in range(heads):
        part = pl.ds(h * rows, rows)
        q_buf[part, :width] = jnp.where(lane // HD == h, queries[...], jnp.bfloat16(0))
        q_buf[part, width:] = query_marks[h]
    for slot in range(reach + 1):
        v_buf[slot, :, width:] = jnp.ones((rows, LANES), jnp.bfloat16)

    def narrow(tile):
        best = tile[:, :LANES]
        for first in range(LANES, rows, LANES):
            best = jnp.maximum(best, tile[:, first : first + LANES])
        return best

    def score(h, slot):
        return lax.dot_general(
            q_buf[pl.ds(h * rows, rows), :],
            k_buf[slot],
            (((1,), (1,)), ((), ())),
            preferred_element_type=jnp.float32,
        )

    finish(0)
    q_at = lax.broadcasted_iota(jnp.int32, (rows, rows), 0)
    k_at = lax.broadcasted_iota(jnp.int32, (rows, rows), 1)
    for h in range(heads):
        tile = jnp.where(k_at <= q_at, score(h, 0), HIDDEN_SCORE)
        scores[h, 0] = tile
        peak[h] = narrow(tile)

    def first_pass(slot, carry):
        finish(slot)
        for h in range(heads):
            tile = score(h, slot)
            scores[h, slot] = tile
            peak[h] = jnp.maximum(peak[h], narrow(tile))
        return carry

    lax.fori_loop(1, last + 1, first_pass, 0)
    for h in range(heads):
        best = jnp.max(peak[h], axis=1, keepdims=True)
        peak[h] = jnp.broadcast_to(best, (rows, LANES))
        total[h] = jnp.zeros_like(total[h])

    def second_pass(slot, carry):
        for h in range(heads):
            best = peak[h]
            wide = jnp.concatenate([best] * (rows // LANES), axis=1)
            weight = jnp.exp(scores[h, slot] - wide).astype(jnp.bfloat16)
            total[h] += dot_f32(weight, v_buf[slot])
        return carry

    lax.fori_loop(0, last + 1, second_pass, 0)
    result = total[0, :, :width] / total[0, :, width:]
    for h in range(1, heads):
        result = jnp.where(lane // HD == h, total[h, :, :width] / total[h, :, width:], result)
    out[...] = result.astype(jnp.bfloat16)


def attend(info, queries, query_marks, key_marks, pieces, heads, reach):
    rows, width = queries.shape
    slots = reach + 1
    return pl.pallas_call(
        functools.partial(attend_kernel, len(pieces), heads, reach),
        out_shape=jax.ShapeDtypeStruct((rows, width), jnp.bfloat16),
        in_specs=[SMEM, VMEM, VMEM, ANY] + [ANY] * len(pieces),
        out_specs=VMEM,
        scratch_shapes=[
            pltpu.VMEM((heads * rows, width + LANES), jnp.bfloat16),
            pltpu.VMEM((slots, rows, width + LANES), jnp.bfloat16),
            pltpu.VMEM((slots, rows, width + LANES), jnp.bfloat16),
            pltpu.VMEM((heads, slots, rows, rows), jnp.float32),
            pltpu.VMEM((heads, rows, LANES), jnp.float32),
            pltpu.VMEM((heads, rows, width + LANES), jnp.float32),
            pltpu.SemaphoreType.DMA((slots, 3)),
        ],
        compiler_params=params(48),
        cost_estimate=cost(
            4 * heads * rows * rows * slots * 256, 4 << 20, heads * rows * rows * slots
        ),
        name="attend",
    )(info, queries, query_marks, key_marks, *pieces)


def bias_marks(variate, segment, var_bias, requests):
    lane = jnp.arange(LANES, dtype=jnp.int32)
    chosen = variate[None, :, None] == (lane % VARS)[None, None, :]
    bias = jnp.where(chosen, var_bias[0][:, None, None], var_bias[1][:, None, None])
    high = lax.reduce_precision(bias, 8, 7)
    middle = lax.reduce_precision(bias - high, 8, 7)
    low = bias - high - middle
    part = (lane // VARS)[None, None, :]
    marks = jnp.where(part == 0, high, jnp.where(part == 1, middle, low))
    other = segment[None, :, None] != (lane - BIAS_PARTS * VARS)[None, None, :]
    marks = jnp.where(part < BIAS_PARTS, marks, jnp.where(other, HIDDEN_SCORE, 0.0))
    used = lane < BIAS_PARTS * VARS + requests
    return jnp.where(used[None, None, :], marks, 0.0).astype(jnp.bfloat16)


def key_marks_of(variate, segment, requests):
    lane = jnp.arange(LANES, dtype=jnp.int32)[None, :]
    same_variate = variate[:, None] == lane % VARS
    same_segment = segment[:, None] == lane - BIAS_PARTS * VARS
    marked = jnp.where(lane < BIAS_PARTS * VARS, same_variate, same_segment)
    used = lane < BIAS_PARTS * VARS + requests
    return (marked & used).astype(jnp.bfloat16)


def cache_kernel(count, window, me_ref, first_token, amounts, *refs):
    pieces = refs[:count]
    out, rows_buf, sems = refs[count:]
    rows = rows_buf.shape[1]
    blocks = rows_buf.shape[0]
    flat = rows_buf.shape[0] * rows
    me = me_ref[0]
    started = []

    def begin(source, block):
        copy = pltpu.make_async_copy(source, rows_buf.at[block], sems.at[len(started)])
        copy.start()
        started.append(copy)

    piece_copies(pieces, me, begin)
    for copy in started:
        copy.wait()
    row = lax.broadcasted_iota(jnp.int32, (PAGE, window), 0)
    column = lax.broadcasted_iota(jnp.int32, (PAGE, window), 1)

    def one_page(page, carry):
        first = first_token[page]
        block = first // rows
        total = None
        for ahead in range(2):
            at = jnp.minimum(block + ahead, blocks - 1)
            inside = first - block * rows
            if ahead == 0:
                start = jnp.minimum(inside // 16 * 16, rows - window)
                offset = inside - start
            else:
                start = 0
                offset = inside - rows
            wanted = (row + offset == column) & (row < amounts[page])
            if ahead == 1:
                wanted = wanted & (block + 1 < blocks)
            chooser = jnp.where(wanted, 1.0, 0.0).astype(jnp.bfloat16)
            found = dot_f32(chooser, rows_buf[at, pl.ds(pl.multiple_of(start, 16), window), :])
            total = found if total is None else total + found
        out[pl.ds(pl.multiple_of(page * PAGE, PAGE), PAGE), :] = total.astype(jnp.bfloat16)
        return carry

    lax.fori_loop(0, out.shape[0] // PAGE, one_page, 0)


def fill_cache(me, first_token, amounts, pieces):
    rows, width = pieces[0].shape[-2:]
    blocks = lax.axis_size("seq")
    pages = first_token.shape[0]
    return pl.pallas_call(
        functools.partial(cache_kernel, len(pieces), 2 * PAGE),
        out_shape=jax.ShapeDtypeStruct((pages * PAGE, width), jnp.bfloat16),
        in_specs=[SMEM] * 3 + [ANY] * len(pieces),
        out_specs=VMEM,
        scratch_shapes=[
            pltpu.VMEM((blocks, rows, width), jnp.bfloat16),
            pltpu.SemaphoreType.DMA((blocks,)),
        ],
        compiler_params=params(24),
        cost_estimate=cost(4 * pages * PAGE * 2 * PAGE * width, 3 << 20),
        name="fill_cache",
    )(me, first_token, amounts, *pieces)


def page_sources(lengths, page_table, me, devices):
    ends = jnp.cumsum(lengths)
    starts = ends - lengths
    counts = (lengths + PAGE - 1) // PAGE
    bases = jnp.cumsum(counts) - counts
    pages = page_table.shape[0] // devices
    mine = me * pages + jnp.arange(pages, dtype=jnp.int32)
    order = jnp.arange(page_table.shape[0], dtype=jnp.int32)
    logical = jnp.sum(jnp.where(page_table[None, :] == mine[:, None], order[None, :], 0), axis=1)
    within = (logical[:, None] >= bases[None, :]) & (logical[:, None] < (bases + counts)[None, :])
    first = starts[None, :] + (logical[:, None] - bases[None, :]) * PAGE
    amount = jnp.minimum(ends[None, :] - first, PAGE)
    return (
        jnp.sum(jnp.where(within, first, 0), axis=1),
        jnp.sum(jnp.where(within, amount, 0), axis=1),
    )


def hidden_kernel(count, on_line, place_ref, *refs):
    pieces = refs[:count]
    tokens, gain, w_out, w_gate, w_up, w_down = refs[count : count + 6]
    if on_line:
        hidden, kept, first_out, second_out = refs[count + 6 : count + 10]
    else:
        hidden, kept = refs[count + 6 : count + 8]
    attended, out_buf, gate_buf, up_buf, down_buf, sems = refs[-6:]
    place = place_ref[0]
    loads = [
        pltpu.make_async_copy(source, target, sems.at[i])
        for i, (source, target) in enumerate(
            [(w_out, out_buf), (w_gate, gate_buf), (w_up, up_buf), (w_down, down_buf)]
        )
    ]
    for load in loads:
        load.start()
    assemble(pieces, place, attended, on_line)
    rows, features = tokens.shape
    width = kept.shape[1]
    step = min(rows, 256)
    gain_row = gain[...].astype(jnp.float32)
    loads[0].wait()
    normed = []
    for first in range(0, rows, step):
        part = pl.ds(first, step)
        projected = dot_f32(attended[part, :], out_buf[...])
        residual = (tokens[part, :].astype(jnp.float32) + projected).astype(jnp.bfloat16)
        tokens_now = residual.astype(jnp.float32)
        normed.append(norm_rows(tokens_now, gain_row))
        gather = residual[:, :width]
        for i in range(1, features // width):
            gather = jnp.where(place == i, residual[:, i * width : (i + 1) * width], gather)
        kept[part, :] = gather
    loads[1].wait()
    loads[2].wait()
    for i, first in enumerate(range(0, rows, step)):
        part = pl.ds(first, step)
        gate = dot_f32(normed[i], gate_buf[...])
        up = dot_f32(normed[i], up_buf[...])
        hidden[part, :] = (jax.nn.silu(gate) * up).astype(jnp.bfloat16)
    loads[3].wait()
    if not on_line:
        return

    def block(index):
        return down_buf[:, pl.ds(pl.multiple_of(index * width, width), width)]

    toward_end = jnp.where(place == 3, 0, jnp.where(place == 0, 3, place))
    first_out[...] = dot_f32(hidden[...], block(toward_end)).astype(jnp.bfloat16)
    second_out[...] = dot_f32(hidden[...], block(lax.rem(place + 2, 4)))


def hidden_of(place, pieces, tokens, gain, w_out, w_gate, w_up, w_down):
    rows, features = tokens.shape
    width = features // lax.axis_size("tp")
    units = w_gate.shape[1]
    on_line = lax.axis_size("tp") == 4
    shapes = [
        jax.ShapeDtypeStruct((rows, units), jnp.bfloat16),
        jax.ShapeDtypeStruct((rows, width), jnp.bfloat16),
    ]
    if on_line:
        shapes += [
            jax.ShapeDtypeStruct((rows, width), jnp.bfloat16),
            jax.ShapeDtypeStruct((rows, width), jnp.float32),
        ]
    return pl.pallas_call(
        functools.partial(hidden_kernel, len(pieces), on_line),
        out_shape=shapes,
        in_specs=[SMEM] + [VMEM] * len(pieces) + [VMEM, VMEM] + [ANY] * 4,
        out_specs=[VMEM] * len(shapes),
        scratch_shapes=[
            pltpu.VMEM((rows, w_out.shape[0]), jnp.bfloat16),
            pltpu.VMEM(w_out.shape, jnp.bfloat16),
            pltpu.VMEM(w_gate.shape, jnp.bfloat16),
            pltpu.VMEM(w_up.shape, jnp.bfloat16),
            pltpu.VMEM(w_down.shape, jnp.bfloat16),
            pltpu.SemaphoreType.DMA((4,)),
        ],
        compiler_params=params(40),
        cost_estimate=cost(6 * rows * features * units, 10 << 20),
        name="hidden",
    )(place, *pieces, tokens, gain, w_out, w_gate, w_up, w_down)


def down_kernel(place_ref, hidden, kept, w_down, to_right, to_left, own):
    place = place_ref[0]
    width = own.shape[1]

    def product(index):
        weights = w_down[:, pl.ds(pl.multiple_of(index * width, width), width)]
        return dot_f32(hidden[...], weights)

    to_right[...] = product(lax.rem(place + 1, 4)).astype(jnp.bfloat16)
    to_left[...] = product(lax.rem(place + 3, 4)).astype(jnp.bfloat16)
    own[...] = product(place) + kept[...].astype(jnp.float32)


def down_blocks(place, hidden, kept, w_down):
    rows, width = kept.shape
    return pl.pallas_call(
        down_kernel,
        out_shape=[
            jax.ShapeDtypeStruct((rows, width), jnp.bfloat16),
            jax.ShapeDtypeStruct((rows, width), jnp.bfloat16),
            jax.ShapeDtypeStruct((rows, width), jnp.float32),
        ],
        in_specs=[SMEM, VMEM, VMEM, VMEM],
        out_specs=[VMEM] * 3,
        compiler_params=params(24),
        cost_estimate=cost(2 * rows * w_down.shape[0] * width * 3, 5 << 20),
        name="down_blocks",
    )(place, hidden, kept, w_down)


def feed_forward(place, pieces, tokens, gain, w_out, w_gate, w_up, w_down):
    outs = hidden_of(place, pieces, tokens, gain, w_out, w_gate, w_up, w_down)
    if lax.axis_size("tp") != 4:
        hidden, kept = outs
        share = lax.psum_scatter(
            dot_f32(hidden, w_down).astype(jnp.bfloat16), "tp", scatter_dimension=1, tiled=True
        )
        return (kept.astype(jnp.float32) + share.astype(jnp.float32)).astype(jnp.bfloat16)
    hidden, kept, toward_end, two_away = outs
    from_end = lax.ppermute(toward_end, "tp", [(3, 2), (0, 1)])
    to_right, to_left, own = down_blocks(place, hidden, kept, w_down)
    from_left = lax.ppermute(to_right, "tp", [(0, 1), (1, 2), (2, 3)])
    from_right = lax.ppermute(to_left, "tp", [(3, 2), (2, 1), (1, 0)])
    joined = (two_away + from_end.astype(jnp.float32)).astype(jnp.bfloat16)
    from_far = lax.ppermute(joined, "tp", [(0, 2), (1, 3), (2, 0), (3, 1)])
    arrived = from_left.astype(jnp.float32) + from_right.astype(jnp.float32)
    return (own + arrived + from_far.astype(jnp.float32)).astype(jnp.bfloat16)


def rope_tables(positions, width):
    half = HD // 2
    frequency = 10000.0 ** (-jnp.arange(half, dtype=jnp.float32) / half)
    angles = positions.astype(jnp.float32)[:, None] * frequency[None, :]
    cosine, sine = jnp.cos(angles), jnp.sin(angles)
    heads = width // HD
    return (
        jnp.concatenate([cosine, cosine] * heads, axis=1),
        jnp.concatenate([-sine, sine] * heads, axis=1),
    )


def segment_of(index, request_ends):
    return jnp.sum((index[:, None] >= request_ends[None, :]).astype(jnp.int32), axis=1)


def per_device(
    tokens,
    variate,
    positions,
    lengths,
    page_table,
    gain_attn,
    w_query,
    w_key,
    w_value,
    var_bias,
    w_out,
    gain_ffn,
    w_gate,
    w_up,
    w_down,
):
    devices = lax.axis_size("seq")
    me = lax.axis_index("seq").astype(jnp.int32)
    place = lax.axis_index("tp").astype(jnp.int32).reshape(1)
    rows = tokens.shape[0]
    width = w_query.shape[1]
    heads = width // HD
    requests = lengths.shape[0]
    reach = devices // 2

    pieces = gather_pieces(tokens)
    all_variates = lax.all_gather(variate, "seq", axis=0, tiled=True)
    slice_rows = w_out.shape[0] // devices
    w_out_slice = lax.dynamic_slice_in_dim(w_out, me * slice_rows, slice_rows, 0)
    w_out_all = lax.all_gather(w_out_slice, ("tp", "seq"), axis=0, tiled=True)

    cosine, sine = rope_tables(positions, width)
    ends = jnp.cumsum(lengths)
    row_first = me * rows
    segment = segment_of(row_first + jnp.arange(rows, dtype=jnp.int32), ends)
    query_marks = bias_marks(variate, segment, var_bias, requests)
    all_index = jnp.arange(rows * devices, dtype=jnp.int32)
    key_marks = key_marks_of(all_variates, segment_of(all_index, ends), requests)
    request_start = jnp.sum(jnp.where(ends <= row_first, lengths, 0))
    info = jnp.stack([me, me - request_start // rows]).astype(jnp.int32)
    first_token, amounts = page_sources(lengths, page_table, me, devices)

    token_rows, queries, pairs = project(
        pieces, place, gain_attn.reshape(1, -1), w_query, w_key, w_value, cosine, sine
    )
    row_pieces = seq_pieces(pairs)
    attended = attend(info, queries, query_marks, key_marks, row_pieces, heads, reach)
    attended_pieces = gather_pieces(attended)
    cache = fill_cache(me.reshape(1), first_token, amounts, row_pieces)
    mixed = feed_forward(
        place,
        attended_pieces,
        token_rows,
        gain_ffn.reshape(1, -1),
        w_out_all,
        w_gate,
        w_up,
        w_down,
    )
    return (mixed, cache.reshape(cache.shape[0], 2, width))


def solution(mesh):
    placed = (
        P("seq", "tp"),
        P("seq"),
        P("seq"),
        P(),
        P(),
        P(),
        P(None, "tp"),
        P(None, "tp"),
        P(None, "tp"),
        P(None, "tp"),
        P("tp", None),
        P(),
        P(None, "tp"),
        P(None, "tp"),
        P("tp", None),
    )
    return jax.shard_map(
        per_device,
        mesh=mesh,
        in_specs=placed,
        out_specs=(P("seq", "tp"), P("seq", None, "tp")),
        check_vma=False,
    )
```

```python
import functools

import jax
import jax.numpy as jnp
from jax import lax
from jax.experimental import pallas as pl
from jax.experimental.pallas import tpu as pltpu
from jax.sharding import PartitionSpec as P

HD = 64
PAGE = 64
VARS = 4
BIAS_PARTS = 3
LANES = 128
HIDDEN_SCORE = -1e30
EPS = 1e-06

VMEM = pl.BlockSpec(memory_space=pltpu.VMEM)
SMEM = pl.BlockSpec(memory_space=pltpu.SMEM)
ANY = pl.BlockSpec(memory_space=pl.ANY)


def params(mib):
    return pltpu.CompilerParams(vmem_limit_bytes=mib << 20)


def cost(flops, nbytes, exps=0):
    return pl.CostEstimate(flops=flops, bytes_accessed=nbytes, transcendentals=exps)


def dot_f32(left, right):
    return jnp.dot(left, right, preferred_element_type=jnp.float32)


def line_gather(shard):
    far = lax.ppermute(shard, "tp", [(0, 2), (1, 3), (2, 0), (3, 1)])
    left = lax.ppermute(shard, "tp", [(0, 1), (1, 2), (2, 3)])
    right = lax.ppermute(shard, "tp", [(3, 2), (2, 1), (1, 0)])
    ends = lax.ppermute(far, "tp", [(2, 3), (1, 0)])
    return [shard, left, right, far, ends]


def turn_gather(shard):
    count = lax.axis_size("tp")
    turns = [2, 1, 3] if count == 4 else list(range(1, count))
    moved = {
        turn: lax.ppermute(shard, "tp", [(i, (i + turn) % count) for i in range(count)])
        for turn in turns
    }
    return [shard] + [moved[turn] for turn in range(1, count)]


def gather_pieces(shard):
    if lax.axis_size("tp") == 4:
        return line_gather(shard)
    return turn_gather(shard)


def assemble(pieces, place, count, target):
    width = pieces[0].shape[1]

    def put(block, value):
        target[:, pl.ds(pl.multiple_of(block * width, width), width)] = value

    if len(pieces) == count:
        for turn, piece in enumerate(pieces):
            put(lax.rem(place + count - turn, count), piece[...])
        return
    own, left, right, far, ends = pieces
    put(place, own[...])
    put(lax.rem(place + 2, 4), far[...])
    put(lax.rem(place + 3, 4), jnp.where(place == 0, ends[...], left[...]))
    put(lax.rem(place + 1, 4), jnp.where(place == 3, ends[...], right[...]))


def rotate_lanes(vectors, cosine, signed_sine):
    lane = lax.broadcasted_iota(jnp.int32, vectors.shape, 1)
    half = HD // 2
    ahead = pltpu.roll(vectors, vectors.shape[1] - half, 1)
    behind = pltpu.roll(vectors, half, 1)
    partner = jnp.where(lane % HD < half, ahead, behind)
    return vectors * cosine + partner * signed_sine


def norm_rows(values, gain):
    scale = lax.rsqrt(jnp.mean(values * values, axis=-1, keepdims=True) + EPS)
    return (values * scale * gain).astype(jnp.bfloat16)


def project_kernel(places, count, place_ref, *refs):
    pieces = refs[:count]
    gain, w_q, w_k, w_v, cosine, sine, tokens, queries, pairs = refs[count:]
    assemble(pieces, place_ref[0], places, tokens)
    rows = tokens.shape[0]
    width = w_q.shape[1]
    step = min(rows, 256)
    gain_row = gain[...].astype(jnp.float32)
    for first in range(0, rows, step):
        part = pl.ds(first, step)
        normed = norm_rows(tokens[part, :].astype(jnp.float32), gain_row)
        cos_part, sin_part = cosine[part, :], sine[part, :]
        query = rotate_lanes(dot_f32(normed, w_q[...]), cos_part, sin_part)
        queries[part, :] = query.astype(jnp.bfloat16) * jnp.bfloat16(HD**-0.5)
        key = rotate_lanes(dot_f32(normed, w_k[...]), cos_part, sin_part)
        pairs[part, :width] = key.astype(jnp.bfloat16)
        pairs[part, width:] = dot_f32(normed, w_v[...]).astype(jnp.bfloat16)


def project(pieces, place, gain, w_query, w_key, w_value, cosine, sine):
    rows, part = pieces[0].shape
    width = w_query.shape[1]
    features = w_query.shape[0]
    return pl.pallas_call(
        functools.partial(project_kernel, lax.axis_size("tp"), len(pieces)),
        out_shape=[
            jax.ShapeDtypeStruct((rows, features), jnp.bfloat16),
            jax.ShapeDtypeStruct((rows, width), jnp.bfloat16),
            jax.ShapeDtypeStruct((rows, 2 * width), jnp.bfloat16),
        ],
        in_specs=[SMEM] + [VMEM] * (len(pieces) + 6),
        out_specs=[VMEM] * 3,
        compiler_params=params(12),
        cost_estimate=cost(6 * rows * features * width, 4 << 20),
        name="project",
    )(place, *pieces, gain, w_query, w_key, w_value, cosine, sine)


def seq_xor(value, mask):
    return lax.ppermute(value, "seq", [(i, i ^ mask) for i in range(lax.axis_size("seq"))])


def seq_pieces(pairs):
    if lax.axis_size("seq") == 8:
        across = seq_xor(pairs, 2)
        down = seq_xor(pairs, 4)
        twin = seq_xor(pairs, 1)
        diagonal = seq_xor(across, 4)
        across_twin = seq_xor(across, 1)
        down_twin = seq_xor(down, 1)
        diagonal_twin = seq_xor(diagonal, 1)
        return [pairs, twin, across, across_twin, down, down_twin, diagonal, diagonal_twin]
    return [lax.all_gather(pairs, "seq", axis=0)]


def piece_copies(pieces, me, wanted):
    if len(pieces) > 1:
        for m, piece in enumerate(pieces):
            wanted(piece, me ^ m)
    else:
        for j in range(pieces[0].shape[0]):
            wanted(pieces[0].at[j], j)


def attend_kernel(count, heads, reach, info, queries, query_marks, key_marks, *refs):
    pieces = refs[:count]
    out, q_buf, k_buf, v_buf, scores, peak, total, sems = refs[count:]
    me, last = info[0], info[1]
    rows = queries.shape[0]
    width = queries.shape[1]

    def copies(source, block, slot):
        return [
            pltpu.make_async_copy(
                source.at[:, pl.ds(0, width)], k_buf.at[slot, :, pl.ds(0, width)], sems.at[slot, 0]
            ),
            pltpu.make_async_copy(
                source.at[:, pl.ds(width, width)],
                v_buf.at[slot, :, pl.ds(0, width)],
                sems.at[slot, 1],
            ),
            pltpu.make_async_copy(
                key_marks.at[pl.ds(pl.multiple_of(block * rows, rows), rows), :],
                k_buf.at[slot, :, pl.ds(width, LANES)],
                sems.at[slot, 2],
            ),
        ]

    def begin(source, block):
        distance = me - block

        @pl.when((distance >= 0) & (distance <= last))
        def _():
            for copy in copies(source, block, distance):
                copy.start()

    piece_copies(pieces, me, begin)
    example = pieces[0] if count > 1 else pieces[0].at[0]

    def finish(slot):
        for copy in copies(example, 0, slot):
            copy.wait()

    lane = lax.broadcasted_iota(jnp.int32, (rows, width), 1)
    for h in range(heads):
        part = pl.ds(h * rows, rows)
        q_buf[part, :width] = jnp.where(lane // HD == h, queries[...], jnp.bfloat16(0))
        q_buf[part, width:] = query_marks[h]
    for slot in range(reach + 1):
        v_buf[slot, :, width:] = jnp.ones((rows, LANES), jnp.bfloat16)

    def narrow(tile):
        best = tile[:, :LANES]
        for first in range(LANES, rows, LANES):
            best = jnp.maximum(best, tile[:, first : first + LANES])
        return best

    def score(h, slot):
        return lax.dot_general(
            q_buf[pl.ds(h * rows, rows), :],
            k_buf[slot],
            (((1,), (1,)), ((), ())),
            preferred_element_type=jnp.float32,
        )

    finish(0)
    q_at = lax.broadcasted_iota(jnp.int32, (rows, rows), 0)
    k_at = lax.broadcasted_iota(jnp.int32, (rows, rows), 1)
    for h in range(heads):
        tile = jnp.where(k_at <= q_at, score(h, 0), HIDDEN_SCORE)
        scores[h, 0] = tile
        peak[h] = narrow(tile)

    def first_pass(slot, carry):
        finish(slot)
        for h in range(heads):
            tile = score(h, slot)
            scores[h, slot] = tile
            peak[h] = jnp.maximum(peak[h], narrow(tile))
        return carry

    lax.fori_loop(1, last + 1, first_pass, 0)
    for h in range(heads):
        best = jnp.max(peak[h], axis=1, keepdims=True)
        peak[h] = jnp.broadcast_to(best, (rows, LANES))
        total[h] = jnp.zeros_like(total[h])

    def second_pass(slot, carry):
        for h in range(heads):
            best = peak[h]
            wide = jnp.concatenate([best] * (rows // LANES), axis=1)
            weight = jnp.exp(scores[h, slot] - wide).astype(jnp.bfloat16)
            total[h] += dot_f32(weight, v_buf[slot])
        return carry

    lax.fori_loop(0, last + 1, second_pass, 0)
    result = total[0, :, :width] / total[0, :, width:]
    for h in range(1, heads):
        result = jnp.where(lane // HD == h, total[h, :, :width] / total[h, :, width:], result)
    out[...] = result.astype(jnp.bfloat16)


def attend(info, queries, query_marks, key_marks, pieces, heads, reach):
    rows, width = queries.shape
    slots = reach + 1
    return pl.pallas_call(
        functools.partial(attend_kernel, len(pieces), heads, reach),
        out_shape=jax.ShapeDtypeStruct((rows, width), jnp.bfloat16),
        in_specs=[SMEM, VMEM, VMEM, ANY] + [ANY] * len(pieces),
        out_specs=VMEM,
        scratch_shapes=[
            pltpu.VMEM((heads * rows, width + LANES), jnp.bfloat16),
            pltpu.VMEM((slots, rows, width + LANES), jnp.bfloat16),
            pltpu.VMEM((slots, rows, width + LANES), jnp.bfloat16),
            pltpu.VMEM((heads, slots, rows, rows), jnp.float32),
            pltpu.VMEM((heads, rows, LANES), jnp.float32),
            pltpu.VMEM((heads, rows, width + LANES), jnp.float32),
            pltpu.SemaphoreType.DMA((slots, 3)),
        ],
        compiler_params=params(12 + 2 * slots),
        cost_estimate=cost(
            4 * heads * rows * rows * slots * 256, 4 << 20, heads * rows * rows * slots
        ),
        name="attend",
    )(info, queries, query_marks, key_marks, *pieces)


def bias_marks(variate, segment, var_bias, requests):
    lane = jnp.arange(LANES, dtype=jnp.int32)
    high = lax.reduce_precision(var_bias, 8, 7)
    middle = lax.reduce_precision(var_bias - high, 8, 7)
    parts = jnp.stack([high, middle, var_bias - high - middle], axis=2)
    by_lane = jnp.repeat(parts, VARS, axis=2)
    by_lane = jnp.pad(by_lane, ((0, 0), (0, 0), (0, LANES - by_lane.shape[2])))
    by_lane = by_lane.astype(jnp.bfloat16)
    same = variate[None, :, None] == (lane % VARS)[None, None, :]
    marks = jnp.where(same, by_lane[0][:, None, :], by_lane[1][:, None, :])
    request = lane - BIAS_PARTS * VARS
    other = segment[None, :, None] != request[None, None, :]
    hidden = other & ((request >= 0) & (request < requests))[None, None, :]
    return jnp.where(hidden, jnp.bfloat16(HIDDEN_SCORE), marks)


def key_marks_of(variate, segment, requests):
    lane = jnp.arange(LANES, dtype=jnp.int32)[None, :]
    same_variate = variate[:, None] == lane % VARS
    same_segment = segment[:, None] == lane - BIAS_PARTS * VARS
    marked = jnp.where(lane < BIAS_PARTS * VARS, same_variate, same_segment)
    used = lane < BIAS_PARTS * VARS + requests
    return (marked & used).astype(jnp.bfloat16)


def cache_kernel(count, window, me_ref, first_token, amounts, *refs):
    pieces = refs[:count]
    out, rows_buf, sems = refs[count:]
    rows = rows_buf.shape[1]
    blocks = rows_buf.shape[0]
    flat = rows_buf.shape[0] * rows
    me = me_ref[0]
    started = []

    def begin(source, block):
        copy = pltpu.make_async_copy(source, rows_buf.at[block], sems.at[len(started)])
        copy.start()
        started.append(copy)

    piece_copies(pieces, me, begin)
    for copy in started:
        copy.wait()
    row = lax.broadcasted_iota(jnp.int32, (PAGE, window), 0)
    column = lax.broadcasted_iota(jnp.int32, (PAGE, window), 1)

    def one_page(page, carry):
        first = first_token[page]
        block = first // rows
        total = None
        for ahead in range(2):
            at = jnp.minimum(block + ahead, blocks - 1)
            inside = first - block * rows
            if ahead == 0:
                start = jnp.minimum(inside // 16 * 16, rows - window)
                offset = inside - start
            else:
                start = 0
                offset = inside - rows
            wanted = (row + offset == column) & (row < amounts[page])
            if ahead == 1:
                wanted = wanted & (block + 1 < blocks)
            chooser = jnp.where(wanted, 1.0, 0.0).astype(jnp.bfloat16)
            found = dot_f32(chooser, rows_buf[at, pl.ds(pl.multiple_of(start, 16), window), :])
            total = found if total is None else total + found
        out[pl.ds(pl.multiple_of(page * PAGE, PAGE), PAGE), :] = total.astype(jnp.bfloat16)
        return carry

    lax.fori_loop(0, out.shape[0] // PAGE, one_page, 0)


def fill_cache(me, first_token, amounts, pieces):
    rows, width = pieces[0].shape[-2:]
    blocks = lax.axis_size("seq")
    pages = first_token.shape[0]
    return pl.pallas_call(
        functools.partial(cache_kernel, len(pieces), 2 * PAGE),
        out_shape=jax.ShapeDtypeStruct((pages * PAGE, width), jnp.bfloat16),
        in_specs=[SMEM] * 3 + [ANY] * len(pieces),
        out_specs=VMEM,
        scratch_shapes=[
            pltpu.VMEM((blocks, rows, width), jnp.bfloat16),
            pltpu.SemaphoreType.DMA((blocks,)),
        ],
        compiler_params=params(8),
        cost_estimate=cost(4 * pages * PAGE * 2 * PAGE * width, 3 << 20),
        name="fill_cache",
    )(me, first_token, amounts, *pieces)


def running_sum(values):
    at = jnp.arange(values.shape[0], dtype=jnp.int32)
    return jnp.sum(jnp.where(at[None, :] <= at[:, None], values[None, :], 0), axis=1)


def page_sources(lengths, page_table, me, devices):
    ends = running_sum(lengths)
    starts = ends - lengths
    counts = (lengths + PAGE - 1) // PAGE
    bases = running_sum(counts) - counts
    pages = page_table.shape[0] // devices
    mine = me * pages + jnp.arange(pages, dtype=jnp.int32)
    order = jnp.arange(page_table.shape[0], dtype=jnp.int32)
    logical = jnp.sum(jnp.where(page_table[None, :] == mine[:, None], order[None, :], 0), axis=1)
    within = (logical[:, None] >= bases[None, :]) & (logical[:, None] < (bases + counts)[None, :])
    first = starts[None, :] + (logical[:, None] - bases[None, :]) * PAGE
    amount = jnp.minimum(ends[None, :] - first, PAGE)
    return (
        jnp.sum(jnp.where(within, first, 0), axis=1),
        jnp.sum(jnp.where(within, amount, 0), axis=1),
    )


def feed_kernel(places, count, on_line, place_ref, *refs):
    pieces = refs[:count]
    tokens, gain, w_out, w_gate, w_up, w_down = refs[count : count + 6]
    outs, attended = refs[count + 6 : -1], refs[-1]
    place = place_ref[0]
    assemble(pieces, place, places, attended)
    features = tokens.shape[1]
    width = features // places
    columns = w_out.shape[2]
    projected = jnp.concatenate(
        [dot_f32(attended[...], w_out[i, : attended.shape[1], :]) for i in range(w_out.shape[0])],
        axis=1,
    )
    residual = (tokens[...].astype(jnp.float32) + projected).astype(jnp.bfloat16)
    normed = norm_rows(residual.astype(jnp.float32), gain[...].astype(jnp.float32))
    kept = residual[:, :width]
    for i in range(1, places):
        kept = jnp.where(place == i, residual[:, i * width : (i + 1) * width], kept)
    gate = dot_f32(normed, w_gate[...])
    up = dot_f32(normed, w_up[...])
    hidden = (jax.nn.silu(gate) * up).astype(jnp.bfloat16)
    if not on_line:
        outs[0][...] = dot_f32(hidden, w_down[...]).astype(jnp.bfloat16)
        outs[1][...] = kept.astype(jnp.float32)
        return

    def product(index):
        return dot_f32(hidden, w_down[:, pl.ds(pl.multiple_of(index * width, width), width)])

    far, to_right, to_left, toward_end, own = outs
    far[...] = product(lax.rem(place + 2, 4))
    right = product(lax.rem(place + 1, 4)).astype(jnp.bfloat16)
    left = product(lax.rem(place + 3, 4)).astype(jnp.bfloat16)
    to_right[...] = right
    to_left[...] = left
    toward_end[...] = jnp.where(place == 3, right, left)
    own[...] = product(place) + kept.astype(jnp.float32)


def feed_share(place, pieces, tokens, gain, w_out, w_gate, w_up, w_down, part, parts):
    places = lax.axis_size("tp")
    rows, features = tokens.shape[0] // parts, tokens.shape[1]
    width = features // places
    on_line = places == 4
    if on_line:
        kinds = [jnp.float32, jnp.bfloat16, jnp.bfloat16, jnp.bfloat16, jnp.float32]
        shapes = [jax.ShapeDtypeStruct((rows, width), kind) for kind in kinds]
    else:
        shapes = [
            jax.ShapeDtypeStruct((rows, features), jnp.bfloat16),
            jax.ShapeDtypeStruct((rows, width), jnp.float32),
        ]

    def rows_of(array):
        return pl.BlockSpec((rows, array.shape[1]), lambda i: (part, 0))

    def whole(array):
        return pl.BlockSpec(array.shape, lambda i: (0,) * array.ndim)

    weights = [gain, w_out, w_gate, w_up, w_down]
    return pl.pallas_call(
        functools.partial(feed_kernel, places, len(pieces), on_line),
        grid=(1,),
        out_shape=shapes,
        in_specs=[SMEM]
        + [rows_of(piece) for piece in pieces]
        + [rows_of(tokens)]
        + [whole(weight) for weight in weights],
        out_specs=[whole(shape) for shape in shapes],
        scratch_shapes=[pltpu.VMEM((rows, places * pieces[0].shape[1]), jnp.bfloat16)],
        compiler_params=params(28),
        cost_estimate=cost(6 * rows * features * w_gate.shape[1], 10 << 20),
        name="feed",
    )(place, *pieces, tokens, *weights)


def feed_forward(place, pieces, tokens, gain, w_out, w_gate, w_up, w_down):
    parts = 2
    mixed = []
    for part in range(parts):
        outs = feed_share(place, pieces, tokens, gain, w_out, w_gate, w_up, w_down, part, parts)
        if lax.axis_size("tp") != 4:
            share = lax.psum_scatter(outs[0], "tp", scatter_dimension=1, tiled=True)
            mixed.append((outs[1] + share.astype(jnp.float32)).astype(jnp.bfloat16))
            continue
        far, to_right, to_left, toward_end, own = outs
        from_end = lax.ppermute(toward_end, "tp", [(3, 2), (0, 1)])
        from_left = lax.ppermute(to_right, "tp", [(0, 1), (1, 2), (2, 3)])
        from_right = lax.ppermute(to_left, "tp", [(3, 2), (2, 1), (1, 0)])
        joined = (far + from_end.astype(jnp.float32)).astype(jnp.bfloat16)
        from_far = lax.ppermute(joined, "tp", [(0, 2), (1, 3), (2, 0), (3, 1)])
        arrived = from_left.astype(jnp.float32) + from_right.astype(jnp.float32)
        mixed.append((own + arrived + from_far.astype(jnp.float32)).astype(jnp.bfloat16))
    return jnp.concatenate(mixed, axis=0)


def rope_tables(positions, width):
    half = HD // 2
    frequency = 10000.0 ** (-jnp.arange(half, dtype=jnp.float32) / half)
    angles = positions.astype(jnp.float32)[:, None] * frequency[None, :]
    cosine, sine = jnp.cos(angles), jnp.sin(angles)
    heads = width // HD
    return (
        jnp.concatenate([cosine, cosine] * heads, axis=1),
        jnp.concatenate([-sine, sine] * heads, axis=1),
    )


def gather_w_out(w_out, variate, me, devices):
    columns = w_out.shape[1] // devices
    block = lax.dynamic_slice_in_dim(w_out, me * columns, columns, 1)
    block = lax.all_gather(block, "tp", axis=0, tiled=True)
    extra = variate.astype(jnp.bfloat16).reshape(-1, columns)
    height = block.shape[0]
    pad = -extra.shape[0] % 16
    block = jnp.concatenate([block, jnp.pad(extra, ((0, pad), (0, 0)))], axis=0)
    blocks = lax.all_gather(block, "seq", axis=0)
    variates = blocks[:, height : height + extra.shape[0], :]
    return blocks, variates.reshape(-1).astype(jnp.int32)


def segment_of(index, request_ends):
    return jnp.sum((index[:, None] >= request_ends[None, :]).astype(jnp.int32), axis=1)


def per_device(
    tokens,
    variate,
    positions,
    lengths,
    page_table,
    gain_attn,
    w_query,
    w_key,
    w_value,
    var_bias,
    w_out,
    gain_ffn,
    w_gate,
    w_up,
    w_down,
):
    devices = lax.axis_size("seq")
    me = lax.axis_index("seq").astype(jnp.int32)
    place = lax.axis_index("tp").astype(jnp.int32).reshape(1)
    rows = tokens.shape[0]
    width = w_query.shape[1]
    heads = width // HD
    requests = lengths.shape[0]
    reach = devices // 2

    pieces = gather_pieces(tokens)
    w_out_all, all_variates = gather_w_out(w_out, variate, me, devices)

    cosine, sine = rope_tables(positions, width)
    ends = running_sum(lengths)
    row_first = me * rows
    segment = segment_of(row_first + jnp.arange(rows, dtype=jnp.int32), ends)
    query_marks = bias_marks(variate, segment, var_bias, requests)
    all_index = jnp.arange(rows * devices, dtype=jnp.int32)
    key_marks = key_marks_of(all_variates, segment_of(all_index, ends), requests)
    request_start = jnp.sum(jnp.where(ends <= row_first, lengths, 0))
    info = jnp.stack([me, me - request_start // rows]).astype(jnp.int32)
    first_token, amounts = page_sources(lengths, page_table, me, devices)

    token_rows, queries, pairs = project(
        pieces, place, gain_attn.reshape(1, -1), w_query, w_key, w_value, cosine, sine
    )
    row_pieces = seq_pieces(pairs)
    attended = attend(info, queries, query_marks, key_marks, row_pieces, heads, reach)
    attended_pieces = turn_gather(attended)
    cache = fill_cache(me.reshape(1), first_token, amounts, row_pieces)
    mixed = feed_forward(
        place,
        attended_pieces,
        token_rows,
        gain_ffn.reshape(1, -1),
        w_out_all,
        w_gate,
        w_up,
        w_down,
    )
    return (mixed, cache.reshape(cache.shape[0], 2, width))


def solution(mesh):
    placed = (
        P("seq", "tp"),
        P("seq"),
        P("seq"),
        P(),
        P(),
        P(),
        P(None, "tp"),
        P(None, "tp"),
        P(None, "tp"),
        P(None, "tp"),
        P("tp", None),
        P(),
        P(None, "tp"),
        P(None, "tp"),
        P("tp", None),
    )
    return jax.shard_map(
        per_device,
        mesh=mesh,
        in_specs=placed,
        out_specs=(P("seq", "tp"), P("seq", None, "tp")),
        check_vma=False,
    )
```

```python
import functools

import jax
import jax.numpy as jnp
from jax import lax
from jax.experimental import pallas as pl
from jax.experimental.pallas import tpu as pltpu
from jax.sharding import PartitionSpec as P

HD = 64
PAGE = 64
VARS = 4
BIAS_PARTS = 3
LANES = 128
HIDDEN_SCORE = -1e30
EPS = 1e-06

VMEM = pl.BlockSpec(memory_space=pltpu.VMEM)
SMEM = pl.BlockSpec(memory_space=pltpu.SMEM)
ANY = pl.BlockSpec(memory_space=pl.ANY)


def params(mib):
    return pltpu.CompilerParams(vmem_limit_bytes=mib << 20)


def cost(flops, nbytes, exps=0):
    return pl.CostEstimate(flops=flops, bytes_accessed=nbytes, transcendentals=exps)


def round_up(amount, unit):
    return (amount + unit - 1) // unit * unit


def dot_f32(left, right):
    return jnp.dot(left, right, preferred_element_type=jnp.float32)


def line_gather(shard):
    far = lax.ppermute(shard, "tp", [(0, 2), (1, 3), (2, 0), (3, 1)])
    left = lax.ppermute(shard, "tp", [(0, 1), (1, 2), (2, 3)])
    right = lax.ppermute(shard, "tp", [(3, 2), (2, 1), (1, 0)])
    ends = lax.ppermute(far, "tp", [(2, 3), (1, 0)])
    return [shard, left, right, far, ends]


def turn_gather(shard):
    count = lax.axis_size("tp")
    turns = [2, 1, 3] if count == 4 else list(range(1, count))
    moved = {
        turn: lax.ppermute(shard, "tp", [(i, (i + turn) % count) for i in range(count)])
        for turn in turns
    }
    return [shard] + [moved[turn] for turn in range(1, count)]


def gather_pieces(shard):
    if lax.axis_size("tp") == 4:
        return line_gather(shard)
    return turn_gather(shard)


def assemble(pieces, place, count, target):
    width = pieces[0].shape[1]

    def put(block, value):
        target[:, pl.ds(pl.multiple_of(block * width, width), width)] = value

    if len(pieces) == count:
        for turn, piece in enumerate(pieces):
            put(lax.rem(place + count - turn, count), piece[...])
        return
    own, left, right, far, ends = pieces
    put(place, own[...])
    put(lax.rem(place + 2, 4), far[...])
    put(lax.rem(place + 3, 4), jnp.where(place == 0, ends[...], left[...]))
    put(lax.rem(place + 1, 4), jnp.where(place == 3, ends[...], right[...]))


def rotate_lanes(vectors, cosine, signed_sine):
    lane = lax.broadcasted_iota(jnp.int32, vectors.shape, 1)
    half = HD // 2
    ahead = pltpu.roll(vectors, vectors.shape[1] - half, 1)
    behind = pltpu.roll(vectors, half, 1)
    partner = jnp.where(lane % HD < half, ahead, behind)
    return vectors * cosine + partner * signed_sine


def norm_rows(values, gain):
    scale = lax.rsqrt(jnp.mean(values * values, axis=-1, keepdims=True) + EPS)
    return (values * scale * gain).astype(jnp.bfloat16)


def project_kernel(places, count, place_ref, *refs):
    pieces = refs[:count]
    gain, w_q, w_k, w_v, cosine, sine, extra, tokens, queries, pairs = refs[count:]
    pairs[tokens.shape[0] :, :] = extra[...]
    assemble(pieces, place_ref[0], places, tokens)
    rows = tokens.shape[0]
    width = w_q.shape[1]
    step = min(rows, 256)
    gain_row = gain[...].astype(jnp.float32)
    for first in range(0, rows, step):
        part = pl.ds(first, step)
        normed = norm_rows(tokens[part, :].astype(jnp.float32), gain_row)
        cos_part, sin_part = cosine[part, :], sine[part, :]
        query = rotate_lanes(dot_f32(normed, w_q[...]), cos_part, sin_part)
        queries[part, :] = query.astype(jnp.bfloat16) * jnp.bfloat16(HD**-0.5)
        key = rotate_lanes(dot_f32(normed, w_k[...]), cos_part, sin_part)
        pairs[part, :width] = key.astype(jnp.bfloat16)
        pairs[part, width:] = dot_f32(normed, w_v[...]).astype(jnp.bfloat16)


def project(pieces, place, gain, w_query, w_key, w_value, cosine, sine, extra):
    rows, part = pieces[0].shape
    width = w_query.shape[1]
    features = w_query.shape[0]
    return pl.pallas_call(
        functools.partial(project_kernel, lax.axis_size("tp"), len(pieces)),
        out_shape=[
            jax.ShapeDtypeStruct((rows, features), jnp.bfloat16),
            jax.ShapeDtypeStruct((rows, width), jnp.bfloat16),
            jax.ShapeDtypeStruct((rows + extra.shape[0], 2 * width), jnp.bfloat16),
        ],
        in_specs=[SMEM] + [VMEM] * (len(pieces) + 7),
        out_specs=[VMEM] * 3,
        compiler_params=params(12),
        cost_estimate=cost(6 * rows * features * width, 4 << 20),
        name="project",
    )(place, *pieces, gain, w_query, w_key, w_value, cosine, sine, extra)


def seq_xor(value, mask):
    return lax.ppermute(value, "seq", [(i, i ^ mask) for i in range(lax.axis_size("seq"))])


def seq_pieces(pairs):
    if lax.axis_size("seq") == 8:
        diagonal = seq_xor(pairs, 6)
        across = seq_xor(pairs, 2)
        down = seq_xor(pairs, 4)
        twin = seq_xor(pairs, 1)
        across_twin = seq_xor(across, 1)
        down_twin = seq_xor(down, 1)
        diagonal_twin = seq_xor(diagonal, 1)
        return [pairs, twin, across, across_twin, down, down_twin, diagonal, diagonal_twin]
    return [lax.all_gather(pairs, "seq", axis=0)]


def piece_copies(pieces, me, wanted):
    if len(pieces) > 1:
        for m, piece in enumerate(pieces):
            wanted(piece, me ^ m)
    else:
        for j in range(pieces[0].shape[0]):
            wanted(pieces[0].at[j], j)


def attend_kernel(count, heads, reach, requests, info, queries, query_marks, *refs):
    pieces = refs[:count]
    out, q_buf, k_buf, v_buf, extra_buf, scores, peak, total, sems = refs[count:]
    me, last = info[0], info[1]
    rows = queries.shape[0]
    width = queries.shape[1]

    def copies(source, slot):
        return [
            pltpu.make_async_copy(
                source.at[pl.ds(0, rows), pl.ds(0, width)],
                k_buf.at[slot, :, pl.ds(0, width)],
                sems.at[slot, 0],
            ),
            pltpu.make_async_copy(
                source.at[pl.ds(0, rows), pl.ds(width, width)],
                v_buf.at[slot, :, pl.ds(0, width)],
                sems.at[slot, 1],
            ),
            pltpu.make_async_copy(
                source.at[pl.ds(rows, extra_buf.shape[1]), :], extra_buf.at[slot], sems.at[slot, 2]
            ),
        ]

    def begin(source, block):
        distance = me - block

        @pl.when((distance >= 0) & (distance <= last))
        def _():
            for copy in copies(source, distance):
                copy.start()

    piece_copies(pieces, me, begin)
    example = pieces[0] if count > 1 else pieces[0].at[0]

    mark_count = round_up(BIAS_PARTS * VARS + requests, 16)

    def finish(slot):
        for copy in copies(example, slot):
            copy.wait()
        extra = extra_buf[slot].astype(jnp.float32)
        pair_width = extra.shape[1]
        variates = jnp.concatenate([extra[i : i + 1] for i in range(rows // pair_width)], axis=1)
        mark = lax.broadcasted_iota(jnp.int32, (mark_count, rows), 0)
        key = lax.broadcasted_iota(jnp.int32, (mark_count, rows), 1) + (me - slot) * rows
        segment = jnp.zeros_like(key)
        for r in range(requests):
            segment += (key >= info[2 + r]).astype(jnp.int32)
        same_variate = (mark % VARS).astype(jnp.float32) == variates
        same_segment = mark - BIAS_PARTS * VARS == segment
        marked = (same_variate & (mark < BIAS_PARTS * VARS)) | (
            same_segment & (mark >= BIAS_PARTS * VARS)
        )
        columns = jnp.transpose(jnp.where(marked, 1.0, 0.0))
        k_buf[slot, :, width : width + mark_count] = columns.astype(jnp.bfloat16)

    lane = lax.broadcasted_iota(jnp.int32, (rows, width), 1)
    for h in range(heads):
        part = pl.ds(h * rows, rows)
        q_buf[part, :width] = jnp.where(lane // HD == h, queries[...], jnp.bfloat16(0))
        q_buf[part, width:] = query_marks[h]
    for slot in range(reach + 1):
        v_buf[slot, :, width:] = jnp.ones((rows, LANES), jnp.bfloat16)
        k_buf[slot, :, width:] = jnp.zeros((rows, LANES), jnp.bfloat16)

    def narrow(tile):
        best = tile[:, :LANES]
        for first in range(LANES, rows, LANES):
            best = jnp.maximum(best, tile[:, first : first + LANES])
        return best

    def score(h, slot):
        return lax.dot_general(
            q_buf[pl.ds(h * rows, rows), :],
            k_buf[slot],
            (((1,), (1,)), ((), ())),
            preferred_element_type=jnp.float32,
        )

    finish(0)
    q_at = lax.broadcasted_iota(jnp.int32, (rows, rows), 0)
    k_at = lax.broadcasted_iota(jnp.int32, (rows, rows), 1)
    for h in range(heads):
        tile = jnp.where(k_at <= q_at, score(h, 0), HIDDEN_SCORE)
        scores[h, 0] = tile
        peak[h] = narrow(tile)

    def first_pass(slot, carry):
        finish(slot)
        for h in range(heads):
            tile = score(h, slot)
            scores[h, slot] = tile
            peak[h] = jnp.maximum(peak[h], narrow(tile))
        return carry

    lax.fori_loop(1, last + 1, first_pass, 0)
    for h in range(heads):
        best = jnp.max(peak[h], axis=1, keepdims=True)
        peak[h] = jnp.broadcast_to(best, (rows, LANES))
        total[h] = jnp.zeros_like(total[h])

    def second_pass(slot, carry):
        for h in range(heads):
            best = peak[h]
            wide = jnp.concatenate([best] * (rows // LANES), axis=1)
            weight = jnp.exp(scores[h, slot] - wide).astype(jnp.bfloat16)
            total[h] += dot_f32(weight, v_buf[slot])
        return carry

    lax.fori_loop(0, last + 1, second_pass, 0)
    result = total[0, :, :width] / total[0, :, width:]
    for h in range(1, heads):
        result = jnp.where(lane // HD == h, total[h, :, :width] / total[h, :, width:], result)
    out[...] = result.astype(jnp.bfloat16)


def attend(info, queries, query_marks, pieces, heads, reach, requests):
    rows, width = queries.shape
    slots = reach + 1
    return pl.pallas_call(
        functools.partial(attend_kernel, len(pieces), heads, reach, requests),
        out_shape=jax.ShapeDtypeStruct((rows, width), jnp.bfloat16),
        in_specs=[SMEM, VMEM, VMEM] + [ANY] * len(pieces),
        out_specs=VMEM,
        scratch_shapes=[
            pltpu.VMEM((heads * rows, width + LANES), jnp.bfloat16),
            pltpu.VMEM((slots, rows, width + LANES), jnp.bfloat16),
            pltpu.VMEM((slots, rows, width + LANES), jnp.bfloat16),
            pltpu.VMEM((slots, pieces[0].shape[-2] - rows, pieces[0].shape[-1]), jnp.bfloat16),
            pltpu.VMEM((heads, slots, rows, rows), jnp.float32),
            pltpu.VMEM((heads, rows, LANES), jnp.float32),
            pltpu.VMEM((heads, rows, width + LANES), jnp.float32),
            pltpu.SemaphoreType.DMA((slots, 3)),
        ],
        compiler_params=params(12 + 2 * slots),
        cost_estimate=cost(
            4 * heads * rows * rows * slots * 256, 4 << 20, heads * rows * rows * slots
        ),
        name="attend",
    )(info, queries, query_marks, *pieces)


def bias_marks(variate, segment, var_bias, requests):
    lane = jnp.arange(LANES, dtype=jnp.int32)
    high = lax.reduce_precision(var_bias, 8, 7)
    middle = lax.reduce_precision(var_bias - high, 8, 7)
    parts = jnp.stack([high, middle, var_bias - high - middle], axis=2)
    by_lane = jnp.repeat(parts, VARS, axis=2)
    by_lane = jnp.pad(by_lane, ((0, 0), (0, 0), (0, LANES - by_lane.shape[2])))
    by_lane = by_lane.astype(jnp.bfloat16)
    same = variate[None, :, None] == (lane % VARS)[None, None, :]
    marks = jnp.where(same, by_lane[0][:, None, :], by_lane[1][:, None, :])
    request = lane - BIAS_PARTS * VARS
    other = segment[None, :, None] != request[None, None, :]
    hidden = other & ((request >= 0) & (request < requests))[None, None, :]
    return jnp.where(hidden, jnp.bfloat16(HIDDEN_SCORE), marks)


def extra_rows(variate, width):
    extra = variate.astype(jnp.bfloat16).reshape(-1, width)
    return jnp.pad(extra, ((0, round_up(extra.shape[0], 16) - extra.shape[0]), (0, 0)))


def cache_kernel(count, window, me_ref, first_token, amounts, *refs):
    pieces = refs[:count]
    out, rows_buf, sems = refs[count:]
    rows = rows_buf.shape[1]
    blocks = rows_buf.shape[0]
    flat = rows_buf.shape[0] * rows
    me = me_ref[0]
    started = []

    def begin(source, block):
        copy = pltpu.make_async_copy(
            source.at[pl.ds(0, rows), :], rows_buf.at[block], sems.at[len(started)]
        )
        copy.start()
        started.append(copy)

    piece_copies(pieces, me, begin)
    for copy in started:
        copy.wait()
    row = lax.broadcasted_iota(jnp.int32, (PAGE, window), 0)
    column = lax.broadcasted_iota(jnp.int32, (PAGE, window), 1)

    def one_page(page, carry):
        first = first_token[page]
        block = first // rows
        total = None
        for ahead in range(2):
            at = jnp.minimum(block + ahead, blocks - 1)
            inside = first - block * rows
            if ahead == 0:
                start = jnp.minimum(inside // 16 * 16, rows - window)
                offset = inside - start
            else:
                start = 0
                offset = inside - rows
            wanted = (row + offset == column) & (row < amounts[page])
            if ahead == 1:
                wanted = wanted & (block + 1 < blocks)
            chooser = jnp.where(wanted, 1.0, 0.0).astype(jnp.bfloat16)
            found = dot_f32(chooser, rows_buf[at, pl.ds(pl.multiple_of(start, 16), window), :])
            total = found if total is None else total + found
        out[pl.ds(pl.multiple_of(page * PAGE, PAGE), PAGE), :] = total.astype(jnp.bfloat16)
        return carry

    lax.fori_loop(0, out.shape[0] // PAGE, one_page, 0)


def fill_cache(me, first_token, amounts, pieces, rows):
    width = pieces[0].shape[-1]
    blocks = lax.axis_size("seq")
    pages = first_token.shape[0]
    return pl.pallas_call(
        functools.partial(cache_kernel, len(pieces), 2 * PAGE),
        out_shape=jax.ShapeDtypeStruct((pages * PAGE, width), jnp.bfloat16),
        in_specs=[SMEM] * 3 + [ANY] * len(pieces),
        out_specs=VMEM,
        scratch_shapes=[
            pltpu.VMEM((blocks, rows, width), jnp.bfloat16),
            pltpu.SemaphoreType.DMA((blocks,)),
        ],
        compiler_params=params(8),
        cost_estimate=cost(4 * pages * PAGE * 2 * PAGE * width, 3 << 20),
        name="fill_cache",
    )(me, first_token, amounts, *pieces)


def running_sum(values):
    at = jnp.arange(values.shape[0], dtype=jnp.int32)
    return jnp.sum(jnp.where(at[None, :] <= at[:, None], values[None, :], 0), axis=1)


def page_sources(lengths, page_table, me, devices):
    ends = running_sum(lengths)
    starts = ends - lengths
    counts = (lengths + PAGE - 1) // PAGE
    bases = running_sum(counts) - counts
    pages = page_table.shape[0] // devices
    mine = me * pages + jnp.arange(pages, dtype=jnp.int32)
    order = jnp.arange(page_table.shape[0], dtype=jnp.int32)
    logical = jnp.sum(jnp.where(page_table[None, :] == mine[:, None], order[None, :], 0), axis=1)
    within = (logical[:, None] >= bases[None, :]) & (logical[:, None] < (bases + counts)[None, :])
    first = starts[None, :] + (logical[:, None] - bases[None, :]) * PAGE
    amount = jnp.minimum(ends[None, :] - first, PAGE)
    return (
        jnp.sum(jnp.where(within, first, 0), axis=1),
        jnp.sum(jnp.where(within, amount, 0), axis=1),
    )


def hidden_kernel(places, count, on_line, place_ref, *refs):
    pieces = refs[:count]
    tokens, gain, w_out, w_gate, w_up, w_down = refs[count : count + 6]
    outs, attended = refs[count + 6 : -1], refs[-1]
    hidden, kept = outs[:2]
    place = place_ref[0]
    assemble(pieces, place, places, attended)
    rows, features = tokens.shape
    width = kept.shape[1]
    step = min(rows, 256)
    gain_row = gain[...].astype(jnp.float32)
    for first in range(0, rows, step):
        part = pl.ds(first, step)
        projected = dot_f32(attended[part, :], w_out[...])
        residual = (tokens[part, :].astype(jnp.float32) + projected).astype(jnp.bfloat16)
        mine = residual[:, :width]
        for i in range(1, places):
            mine = jnp.where(place == i, residual[:, i * width : (i + 1) * width], mine)
        kept[part, :] = mine
        normed = norm_rows(residual.astype(jnp.float32), gain_row)
        gate = dot_f32(normed, w_gate[...])
        up = dot_f32(normed, w_up[...])
        hidden[part, :] = (jax.nn.silu(gate) * up).astype(jnp.bfloat16)
    if not on_line:
        return

    def block(index):
        return w_down[:, pl.ds(pl.multiple_of(index * width, width), width)]

    toward_end = jnp.where(place == 3, 0, jnp.where(place == 0, 3, place))
    outs[2][...] = dot_f32(hidden[...], block(toward_end)).astype(jnp.bfloat16)


def hidden_of(place, pieces, tokens, gain, w_out, w_gate, w_up, w_down):
    rows, features = tokens.shape
    places = lax.axis_size("tp")
    width = features // places
    units = w_gate.shape[1]
    on_line = places == 4
    shapes = [
        jax.ShapeDtypeStruct((rows, units), jnp.bfloat16),
        jax.ShapeDtypeStruct((rows, width), jnp.bfloat16),
    ]
    if on_line:
        shapes.append(jax.ShapeDtypeStruct((rows, width), jnp.bfloat16))
    return pl.pallas_call(
        functools.partial(hidden_kernel, places, len(pieces), on_line),
        out_shape=shapes,
        in_specs=[SMEM] + [VMEM] * (len(pieces) + 6),
        out_specs=[VMEM] * len(shapes),
        scratch_shapes=[pltpu.VMEM((rows, w_out.shape[0]), jnp.bfloat16)],
        compiler_params=params(24),
        cost_estimate=cost(6 * rows * features * units, 10 << 20),
        name="hidden",
    )(place, *pieces, tokens, gain, w_out, w_gate, w_up, w_down)


def down_kernel(place_ref, hidden, kept, w_down, far, to_right, to_left, own):
    place = place_ref[0]
    width = own.shape[1]

    def product(index):
        weights = w_down[:, pl.ds(pl.multiple_of(index * width, width), width)]
        return dot_f32(hidden[...], weights)

    far[...] = product(lax.rem(place + 2, 4))
    to_right[...] = product(lax.rem(place + 1, 4)).astype(jnp.bfloat16)
    to_left[...] = product(lax.rem(place + 3, 4)).astype(jnp.bfloat16)
    own[...] = product(place) + kept[...].astype(jnp.float32)


def down_blocks(place, hidden, kept, w_down):
    rows, width = kept.shape
    kinds = [jnp.float32, jnp.bfloat16, jnp.bfloat16, jnp.float32]
    return pl.pallas_call(
        down_kernel,
        out_shape=[jax.ShapeDtypeStruct((rows, width), kind) for kind in kinds],
        in_specs=[SMEM, VMEM, VMEM, VMEM],
        out_specs=[VMEM] * 4,
        compiler_params=params(12),
        cost_estimate=cost(2 * rows * w_down.shape[0] * width * 4, 5 << 20),
        name="down_blocks",
    )(place, hidden, kept, w_down)


def add_kernel(*refs):
    total = refs[0][...].astype(jnp.float32)
    for ref in refs[1:-1]:
        total = total + ref[...].astype(jnp.float32)
    refs[-1][...] = total.astype(jnp.bfloat16)


def add_up(*terms):
    return pl.pallas_call(
        add_kernel,
        out_shape=jax.ShapeDtypeStruct(terms[0].shape, jnp.bfloat16),
        in_specs=[VMEM] * len(terms),
        out_specs=VMEM,
        compiler_params=params(6),
        cost_estimate=cost(terms[0].size * len(terms), 4 * terms[0].size * len(terms)),
        name="add_up",
    )(*terms)


def feed_forward(place, pieces, tokens, gain, w_out, w_gate, w_up, w_down):
    outs = hidden_of(place, pieces, tokens, gain, w_out, w_gate, w_up, w_down)
    hidden, kept = outs[:2]
    if lax.axis_size("tp") != 4:
        share = lax.psum_scatter(
            dot_f32(hidden, w_down).astype(jnp.bfloat16), "tp", scatter_dimension=1, tiled=True
        )
        return add_up(kept, share), hidden
    from_end = lax.ppermute(outs[2], "tp", [(3, 2), (0, 1)])
    far, to_right, to_left, own = down_blocks(place, hidden, kept, w_down)
    from_left = lax.ppermute(to_right, "tp", [(0, 1), (1, 2), (2, 3)])
    from_right = lax.ppermute(to_left, "tp", [(3, 2), (2, 1), (1, 0)])
    joined = add_up(far, from_end)
    from_far = lax.ppermute(joined, "tp", [(0, 2), (1, 3), (2, 0), (3, 1)])
    return add_up(own, from_left, from_right, from_far), joined


def rope_tables(positions, width):
    half = HD // 2
    frequency = 10000.0 ** (-jnp.arange(half, dtype=jnp.float32) / half)
    angles = positions.astype(jnp.float32)[:, None] * frequency[None, :]
    cosine, sine = jnp.cos(angles), jnp.sin(angles)
    heads = width // HD
    return (
        jnp.concatenate([cosine, cosine] * heads, axis=1),
        jnp.concatenate([-sine, sine] * heads, axis=1),
    )


def segment_of(index, request_ends):
    return jnp.sum((index[:, None] >= request_ends[None, :]).astype(jnp.int32), axis=1)


def per_device(
    tokens,
    variate,
    positions,
    lengths,
    page_table,
    gain_attn,
    w_query,
    w_key,
    w_value,
    var_bias,
    w_out,
    gain_ffn,
    w_gate,
    w_up,
    w_down,
):
    devices = lax.axis_size("seq")
    me = lax.axis_index("seq").astype(jnp.int32)
    place = lax.axis_index("tp").astype(jnp.int32).reshape(1)
    rows = tokens.shape[0]
    width = w_query.shape[1]
    heads = width // HD
    requests = lengths.shape[0]
    reach = devices // 2

    pieces = gather_pieces(tokens)
    cosine, sine = rope_tables(positions, width)
    ends = running_sum(lengths)
    row_first = me * rows
    segment = segment_of(row_first + jnp.arange(rows, dtype=jnp.int32), ends)
    query_marks = bias_marks(variate, segment, var_bias, requests)
    request_start = jnp.sum(jnp.where(ends <= row_first, lengths, 0))
    info = jnp.concatenate([jnp.stack([me, me - request_start // rows]), ends]).astype(jnp.int32)
    first_token, amounts = page_sources(lengths, page_table, me, devices)
    extra = extra_rows(variate, 2 * width)
    gains = gain_attn.reshape(1, -1), gain_ffn.reshape(1, -1)

    ready = (pieces[-1], w_out, cosine, sine, query_marks, info, first_token, amounts, extra, gains)
    ready = lax.optimization_barrier(ready)
    pieces[-1], w_out, cosine, sine, query_marks, info, first_token, amounts, extra, gains = ready
    w_out_all = lax.all_gather(w_out, "tp", axis=0, tiled=True)

    token_rows, queries, pairs = project(
        pieces, place, gains[0], w_query, w_key, w_value, cosine, sine, extra
    )
    row_pieces = seq_pieces(pairs)
    attended = attend(info, queries, query_marks, row_pieces, heads, reach, requests)
    attended_pieces = turn_gather(attended)
    cache = fill_cache(me.reshape(1), first_token, amounts, row_pieces, rows)
    mixed, joined = feed_forward(
        place, attended_pieces, token_rows, gains[1], w_out_all, w_gate, w_up, w_down
    )
    cache, _ = lax.optimization_barrier((cache, joined))
    return (mixed, cache.reshape(cache.shape[0], 2, width))


def solution(mesh):
    placed = (
        P("seq", "tp"),
        P("seq"),
        P("seq"),
        P(),
        P(),
        P(),
        P(None, "tp"),
        P(None, "tp"),
        P(None, "tp"),
        P(None, "tp"),
        P("tp", None),
        P(),
        P(None, "tp"),
        P(None, "tp"),
        P("tp", None),
    )
    return jax.shard_map(
        per_device,
        mesh=mesh,
        in_specs=placed,
        out_specs=(P("seq", "tp"), P("seq", None, "tp")),
        check_vma=False,
    )
```

```python
import functools

import jax
import jax.numpy as jnp
from jax import lax
from jax.experimental import pallas as pl
from jax.experimental.pallas import tpu as pltpu
from jax.sharding import PartitionSpec as P

HD = 64
PAGE = 64
VARS = 4
BIAS_PARTS = 3
LANES = 128
HIDDEN_SCORE = -1e30
EPS = 1e-06

VMEM = pl.BlockSpec(memory_space=pltpu.VMEM)
SMEM = pl.BlockSpec(memory_space=pltpu.SMEM)
ANY = pl.BlockSpec(memory_space=pl.ANY)
HBM = pl.BlockSpec(memory_space=pltpu.HBM)


def params(mib):
    return pltpu.CompilerParams(vmem_limit_bytes=mib << 20)


def cost(flops, nbytes, exps=0):
    return pl.CostEstimate(flops=flops, bytes_accessed=nbytes, transcendentals=exps)


def round_up(amount, unit):
    return (amount + unit - 1) // unit * unit


def dot_f32(left, right):
    return jnp.dot(left, right, preferred_element_type=jnp.float32)


def line_gather(shard):
    half = shard.shape[0] // 2
    two_away = [(0, 2), (1, 3), (2, 0), (3, 1)]
    far = [lax.ppermute(part, "tp", two_away) for part in (shard[:half], shard[half:])]
    left = lax.ppermute(shard, "tp", [(0, 1), (1, 2), (2, 3)])
    right = lax.ppermute(shard, "tp", [(3, 2), (2, 1), (1, 0)])
    ends = [lax.ppermute(part, "tp", [(2, 3), (1, 0)]) for part in far]
    return [shard, left, right] + far + ends


def turn_gather(shard):
    count = lax.axis_size("tp")
    turns = [2, 1, 3] if count == 4 else list(range(1, count))
    moved = {
        turn: lax.ppermute(shard, "tp", [(i, (i + turn) % count) for i in range(count)])
        for turn in turns
    }
    return [shard] + [moved[turn] for turn in range(1, count)]


def gather_pieces(shard):
    if lax.axis_size("tp") == 4:
        return line_gather(shard)
    return turn_gather(shard)


def assemble(pieces, place, count, target):
    width = pieces[0].shape[1]

    def put(block, value, first=0):
        columns = pl.ds(pl.multiple_of(block * width, width), width)
        target[pl.ds(first, value.shape[0]), columns] = value

    if len(pieces) == count:
        for turn, piece in enumerate(pieces):
            put(lax.rem(place + count - turn, count), piece[...])
        return
    own, left, right = pieces[:3]
    put(place, own[...])
    half = own.shape[0] // 2
    for first, far, ends in zip((0, half), pieces[3:5], pieces[5:]):
        part = pl.ds(first, half)
        put(lax.rem(place + 2, 4), far[...], first)
        put(lax.rem(place + 3, 4), jnp.where(place == 0, ends[...], left[part, :]), first)
        put(lax.rem(place + 1, 4), jnp.where(place == 3, ends[...], right[part, :]), first)


def rotate_lanes(vectors, cosine, signed_sine):
    lane = lax.broadcasted_iota(jnp.int32, vectors.shape, 1)
    half = HD // 2
    ahead = pltpu.roll(vectors, vectors.shape[1] - half, 1)
    behind = pltpu.roll(vectors, half, 1)
    partner = jnp.where(lane % HD < half, ahead, behind)
    return vectors * cosine + partner * signed_sine


def norm_rows(values, gain):
    scale = lax.rsqrt(jnp.mean(values * values, axis=-1, keepdims=True) + EPS)
    return (values * scale * gain).astype(jnp.bfloat16)


def project_kernel(places, count, place_ref, *refs):
    pieces = refs[:count]
    gain, w_q, w_k, w_v, cosine, sine, extra, tokens_out, queries, pairs = refs[count:-2]
    tokens, sem = refs[-2:]
    pairs[tokens.shape[0] :, :] = extra[...]
    assemble(pieces, place_ref[0], places, tokens)
    keep = pltpu.make_async_copy(tokens, tokens_out, sem)
    keep.start()
    rows = tokens.shape[0]
    width = w_q.shape[1]
    step = min(rows, 256)
    gain_row = gain[...].astype(jnp.float32)
    for first in range(0, rows, step):
        part = pl.ds(first, step)
        normed = norm_rows(tokens[part, :].astype(jnp.float32), gain_row)
        cos_part, sin_part = cosine[part, :], sine[part, :]
        query = rotate_lanes(dot_f32(normed, w_q[...]), cos_part, sin_part)
        queries[part, :] = query.astype(jnp.bfloat16) * jnp.bfloat16(HD**-0.5)
        key = rotate_lanes(dot_f32(normed, w_k[...]), cos_part, sin_part)
        pairs[part, :width] = key.astype(jnp.bfloat16)
        pairs[part, width:] = dot_f32(normed, w_v[...]).astype(jnp.bfloat16)
    keep.wait()


def project(pieces, place, gain, w_query, w_key, w_value, cosine, sine, extra):
    rows, part = pieces[0].shape
    width = w_query.shape[1]
    features = w_query.shape[0]
    return pl.pallas_call(
        functools.partial(project_kernel, lax.axis_size("tp"), len(pieces)),
        out_shape=[
            jax.ShapeDtypeStruct((rows, features), jnp.bfloat16),
            jax.ShapeDtypeStruct((rows, width), jnp.bfloat16),
            jax.ShapeDtypeStruct((rows + extra.shape[0], 2 * width), jnp.bfloat16),
        ],
        in_specs=[SMEM] + [VMEM] * (len(pieces) + 7),
        out_specs=[HBM, VMEM, VMEM],
        scratch_shapes=[pltpu.VMEM((rows, features), jnp.bfloat16), pltpu.SemaphoreType.DMA],
        compiler_params=params(6),
        cost_estimate=cost(6 * rows * features * width, 4 << 20),
        name="project",
    )(place, *pieces, gain, w_query, w_key, w_value, cosine, sine, extra)


def seq_xor(value, mask):
    return lax.ppermute(value, "seq", [(i, i ^ mask) for i in range(lax.axis_size("seq"))])


def seq_pieces(pairs):
    if lax.axis_size("seq") == 8:
        diagonal = seq_xor(pairs, 6)
        across = seq_xor(pairs, 2)
        down = seq_xor(pairs, 4)
        twin = seq_xor(pairs, 1)
        across_twin = seq_xor(across, 1)
        down_twin = seq_xor(down, 1)
        diagonal_twin = seq_xor(diagonal, 1)
        return [pairs, twin, across, across_twin, down, down_twin, diagonal, diagonal_twin]
    return [lax.all_gather(pairs, "seq", axis=0)]


def piece_copies(pieces, me, wanted):
    if len(pieces) > 1:
        for m, piece in enumerate(pieces):
            wanted(piece, me ^ m)
    else:
        for j in range(pieces[0].shape[0]):
            wanted(pieces[0].at[j], j)


def attend_kernel(count, heads, reach, requests, info, queries, query_marks, *refs):
    pieces = refs[:count]
    out, q_buf, k_buf, v_buf, extra_buf, scores, peak, total, sems = refs[count:]
    me, last = info[0], info[1]
    rows = queries.shape[0]
    width = queries.shape[1]

    def copies(source, slot):
        return [
            pltpu.make_async_copy(
                source.at[pl.ds(0, rows), pl.ds(0, width)],
                k_buf.at[slot, :, pl.ds(0, width)],
                sems.at[slot, 0],
            ),
            pltpu.make_async_copy(
                source.at[pl.ds(0, rows), pl.ds(width, width)],
                v_buf.at[slot, :, pl.ds(0, width)],
                sems.at[slot, 1],
            ),
            pltpu.make_async_copy(
                source.at[pl.ds(rows, extra_buf.shape[1]), :], extra_buf.at[slot], sems.at[slot, 2]
            ),
        ]

    def begin(source, block):
        distance = me - block

        @pl.when((distance >= 0) & (distance <= last))
        def _():
            for copy in copies(source, distance):
                copy.start()

    piece_copies(pieces, me, begin)
    example = pieces[0] if count > 1 else pieces[0].at[0]

    mark_count = round_up(BIAS_PARTS * VARS + requests, 16)

    def finish(slot):
        for copy in copies(example, slot):
            copy.wait()
        extra = extra_buf[slot].astype(jnp.float32)
        pair_width = extra.shape[1]
        variates = jnp.concatenate([extra[i : i + 1] for i in range(rows // pair_width)], axis=1)
        mark = lax.broadcasted_iota(jnp.int32, (mark_count, rows), 0)
        key = lax.broadcasted_iota(jnp.int32, (mark_count, rows), 1) + (me - slot) * rows
        segment = jnp.zeros_like(key)
        for r in range(requests):
            segment += (key >= info[2 + r]).astype(jnp.int32)
        same_variate = (mark % VARS).astype(jnp.float32) == variates
        same_segment = mark - BIAS_PARTS * VARS == segment
        marked = (same_variate & (mark < BIAS_PARTS * VARS)) | (
            same_segment & (mark >= BIAS_PARTS * VARS)
        )
        columns = jnp.transpose(jnp.where(marked, 1.0, 0.0))
        k_buf[slot, :, width : width + mark_count] = columns.astype(jnp.bfloat16)

    lane = lax.broadcasted_iota(jnp.int32, (rows, width), 1)
    for h in range(heads):
        part = pl.ds(h * rows, rows)
        q_buf[part, :width] = jnp.where(lane // HD == h, queries[...], jnp.bfloat16(0))
        q_buf[part, width:] = query_marks[h]
    for slot in range(reach + 1):
        v_buf[slot, :, width:] = jnp.ones((rows, LANES), jnp.bfloat16)
        k_buf[slot, :, width:] = jnp.zeros((rows, LANES), jnp.bfloat16)

    def narrow(tile):
        best = tile[:, :LANES]
        for first in range(LANES, rows, LANES):
            best = jnp.maximum(best, tile[:, first : first + LANES])
        return best

    def score(h, slot):
        return lax.dot_general(
            q_buf[pl.ds(h * rows, rows), :],
            k_buf[slot],
            (((1,), (1,)), ((), ())),
            preferred_element_type=jnp.float32,
        )

    finish(0)
    q_at = lax.broadcasted_iota(jnp.int32, (rows, rows), 0)
    k_at = lax.broadcasted_iota(jnp.int32, (rows, rows), 1)
    for h in range(heads):
        tile = jnp.where(k_at <= q_at, score(h, 0), HIDDEN_SCORE)
        scores[h, 0] = tile
        peak[h] = narrow(tile)

    def first_pass(slot, carry):
        finish(slot)
        for h in range(heads):
            tile = score(h, slot)
            scores[h, slot] = tile
            peak[h] = jnp.maximum(peak[h], narrow(tile))
        return carry

    lax.fori_loop(1, last + 1, first_pass, 0)
    for h in range(heads):
        best = jnp.max(peak[h], axis=1, keepdims=True)
        peak[h] = jnp.broadcast_to(best, (rows, LANES))
        total[h] = jnp.zeros_like(total[h])

    def second_pass(slot, carry):
        for h in range(heads):
            best = peak[h]
            wide = jnp.concatenate([best] * (rows // LANES), axis=1)
            weight = jnp.exp(scores[h, slot] - wide).astype(jnp.bfloat16)
            total[h] += dot_f32(weight, v_buf[slot])
        return carry

    lax.fori_loop(0, last + 1, second_pass, 0)
    result = total[0, :, :width] / total[0, :, width:]
    for h in range(1, heads):
        result = jnp.where(lane // HD == h, total[h, :, :width] / total[h, :, width:], result)
    out[...] = result.astype(jnp.bfloat16)


def attend(info, queries, query_marks, pieces, heads, reach, requests):
    rows, width = queries.shape
    slots = reach + 1
    return pl.pallas_call(
        functools.partial(attend_kernel, len(pieces), heads, reach, requests),
        out_shape=jax.ShapeDtypeStruct((rows, width), jnp.bfloat16),
        in_specs=[SMEM, VMEM, VMEM] + [ANY] * len(pieces),
        out_specs=VMEM,
        scratch_shapes=[
            pltpu.VMEM((heads * rows, width + LANES), jnp.bfloat16),
            pltpu.VMEM((slots, rows, width + LANES), jnp.bfloat16),
            pltpu.VMEM((slots, rows, width + LANES), jnp.bfloat16),
            pltpu.VMEM((slots, pieces[0].shape[-2] - rows, pieces[0].shape[-1]), jnp.bfloat16),
            pltpu.VMEM((heads, slots, rows, rows), jnp.float32),
            pltpu.VMEM((heads, rows, LANES), jnp.float32),
            pltpu.VMEM((heads, rows, width + LANES), jnp.float32),
            pltpu.SemaphoreType.DMA((slots, 3)),
        ],
        compiler_params=params(8 + 2 * slots),
        cost_estimate=cost(
            4 * heads * rows * rows * slots * 256, 4 << 20, heads * rows * rows * slots
        ),
        name="attend",
    )(info, queries, query_marks, *pieces)


def bias_marks(variate, segment, var_bias, requests):
    lane = jnp.arange(LANES, dtype=jnp.int32)
    high = lax.reduce_precision(var_bias, 8, 7)
    middle = lax.reduce_precision(var_bias - high, 8, 7)
    parts = jnp.stack([high, middle, var_bias - high - middle], axis=2)
    by_lane = jnp.repeat(parts, VARS, axis=2)
    by_lane = jnp.pad(by_lane, ((0, 0), (0, 0), (0, LANES - by_lane.shape[2])))
    by_lane = by_lane.astype(jnp.bfloat16)
    same = variate[None, :, None] == (lane % VARS)[None, None, :]
    marks = jnp.where(same, by_lane[0][:, None, :], by_lane[1][:, None, :])
    request = lane - BIAS_PARTS * VARS
    other = segment[None, :, None] != request[None, None, :]
    hidden = other & ((request >= 0) & (request < requests))[None, None, :]
    return jnp.where(hidden, jnp.bfloat16(HIDDEN_SCORE), marks)


def extra_rows(variate, width):
    extra = variate.astype(jnp.bfloat16).reshape(-1, width)
    return jnp.pad(extra, ((0, round_up(extra.shape[0], 16) - extra.shape[0]), (0, 0)))


def cache_kernel(count, window, me_ref, first_token, amounts, *refs):
    pieces = refs[:count]
    out, rows_buf, sems = refs[count:]
    rows = rows_buf.shape[1]
    blocks = rows_buf.shape[0]
    flat = rows_buf.shape[0] * rows
    me = me_ref[0]
    started = []

    def begin(source, block):
        copy = pltpu.make_async_copy(
            source.at[pl.ds(0, rows), :], rows_buf.at[block], sems.at[len(started)]
        )
        copy.start()
        started.append(copy)

    piece_copies(pieces, me, begin)
    for copy in started:
        copy.wait()
    row = lax.broadcasted_iota(jnp.int32, (PAGE, window), 0)
    column = lax.broadcasted_iota(jnp.int32, (PAGE, window), 1)

    def one_page(page, carry):
        first = first_token[page]
        block = first // rows
        total = None
        for ahead in range(2):
            at = jnp.minimum(block + ahead, blocks - 1)
            inside = first - block * rows
            if ahead == 0:
                start = jnp.minimum(inside // 16 * 16, rows - window)
                offset = inside - start
            else:
                start = 0
                offset = inside - rows
            wanted = (row + offset == column) & (row < amounts[page])
            if ahead == 1:
                wanted = wanted & (block + 1 < blocks)
            chooser = jnp.where(wanted, 1.0, 0.0).astype(jnp.bfloat16)
            found = dot_f32(chooser, rows_buf[at, pl.ds(pl.multiple_of(start, 16), window), :])
            total = found if total is None else total + found
        out[pl.ds(pl.multiple_of(page * PAGE, PAGE), PAGE), :] = total.astype(jnp.bfloat16)
        return carry

    lax.fori_loop(0, out.shape[0] // PAGE, one_page, 0)


def fill_cache(me, first_token, amounts, pieces, rows):
    width = pieces[0].shape[-1]
    blocks = lax.axis_size("seq")
    pages = first_token.shape[0]
    return pl.pallas_call(
        functools.partial(cache_kernel, len(pieces), 2 * PAGE),
        out_shape=jax.ShapeDtypeStruct((pages * PAGE, width), jnp.bfloat16),
        in_specs=[SMEM] * 3 + [ANY] * len(pieces),
        out_specs=VMEM,
        scratch_shapes=[
            pltpu.VMEM((blocks, rows, width), jnp.bfloat16),
            pltpu.SemaphoreType.DMA((blocks,)),
        ],
        compiler_params=params(8),
        cost_estimate=cost(4 * pages * PAGE * 2 * PAGE * width, 3 << 20),
        name="fill_cache",
    )(me, first_token, amounts, *pieces)


def running_sum(values):
    at = jnp.arange(values.shape[0], dtype=jnp.int32)
    return jnp.sum(jnp.where(at[None, :] <= at[:, None], values[None, :], 0), axis=1)


def page_sources(lengths, page_table, me, devices):
    ends = running_sum(lengths)
    starts = ends - lengths
    counts = (lengths + PAGE - 1) // PAGE
    bases = running_sum(counts) - counts
    pages = page_table.shape[0] // devices
    mine = me * pages + jnp.arange(pages, dtype=jnp.int32)
    order = jnp.arange(page_table.shape[0], dtype=jnp.int32)
    logical = jnp.sum(jnp.where(page_table[None, :] == mine[:, None], order[None, :], 0), axis=1)
    within = (logical[:, None] >= bases[None, :]) & (logical[:, None] < (bases + counts)[None, :])
    first = starts[None, :] + (logical[:, None] - bases[None, :]) * PAGE
    amount = jnp.minimum(ends[None, :] - first, PAGE)
    return (
        jnp.sum(jnp.where(within, first, 0), axis=1),
        jnp.sum(jnp.where(within, amount, 0), axis=1),
    )


def fetch_kernel(count, *refs):
    sems = refs[-1]
    loads = [
        pltpu.make_async_copy(source, target, sems.at[i])
        for i, (source, target) in enumerate(zip(refs[:count], refs[count:-1]))
    ]
    for load in loads:
        load.start()
    for load in loads:
        load.wait()


def fetch(arrays):
    return pl.pallas_call(
        functools.partial(fetch_kernel, len(arrays)),
        out_shape=[jax.ShapeDtypeStruct(array.shape, array.dtype) for array in arrays],
        in_specs=[HBM] * len(arrays),
        out_specs=[VMEM] * len(arrays),
        scratch_shapes=[pltpu.SemaphoreType.DMA((len(arrays),))],
        compiler_params=params(10),
        cost_estimate=cost(0, 4 * sum(array.size for array in arrays)),
        name="fetch",
    )(*arrays)


def hidden_kernel(places, count, on_line, place_ref, *refs):
    pieces = refs[:count]
    tokens, gain, w_out, w_gate, w_up, w_down = refs[count : count + 6]
    outs, attended = refs[count + 6 : -1], refs[-1]
    hidden, kept = outs[:2]
    place = place_ref[0]
    assemble(pieces, place, places, attended)
    rows, features = tokens.shape
    width = kept.shape[1]
    step = min(rows, 256)
    gain_row = gain[...].astype(jnp.float32)
    for first in range(0, rows, step):
        part = pl.ds(first, step)
        projected = dot_f32(attended[part, :], w_out[...])
        residual = (tokens[part, :].astype(jnp.float32) + projected).astype(jnp.bfloat16)
        mine = residual[:, :width]
        for i in range(1, places):
            mine = jnp.where(place == i, residual[:, i * width : (i + 1) * width], mine)
        kept[part, :] = mine
        normed = norm_rows(residual.astype(jnp.float32), gain_row)
        gate = dot_f32(normed, w_gate[...])
        up = dot_f32(normed, w_up[...])
        hidden[part, :] = (jax.nn.silu(gate) * up).astype(jnp.bfloat16)
    if not on_line:
        return

    def block(index):
        return w_down[:, pl.ds(pl.multiple_of(index * width, width), width)]

    toward_end = jnp.where(place == 3, 0, jnp.where(place == 0, 3, place))
    for out, first in zip(outs[2:], (0, rows // 2)):
        part = pl.ds(first, rows // 2)
        out[...] = dot_f32(hidden[part, :], block(toward_end)).astype(jnp.bfloat16)


def hidden_of(place, pieces, tokens, gain, w_out, w_gate, w_up, w_down):
    rows, features = tokens.shape
    places = lax.axis_size("tp")
    width = features // places
    units = w_gate.shape[1]
    on_line = places == 4
    shapes = [
        jax.ShapeDtypeStruct((rows, units), jnp.bfloat16),
        jax.ShapeDtypeStruct((rows, width), jnp.bfloat16),
    ]
    if on_line:
        shapes += [jax.ShapeDtypeStruct((rows // 2, width), jnp.bfloat16)] * 2
    return pl.pallas_call(
        functools.partial(hidden_kernel, places, len(pieces), on_line),
        out_shape=shapes,
        in_specs=[SMEM] + [VMEM] * (len(pieces) + 6),
        out_specs=[VMEM] * len(shapes),
        scratch_shapes=[pltpu.VMEM((rows, w_out.shape[0]), jnp.bfloat16)],
        compiler_params=params(12),
        cost_estimate=cost(6 * rows * features * units, 10 << 20),
        name="hidden",
    )(place, *pieces, tokens, gain, w_out, w_gate, w_up, w_down)


def down_kernel(place_ref, hidden, kept, w_down, far_top, far_low, to_right, to_left, own):
    place = place_ref[0]
    rows, width = own.shape

    def product(index):
        weights = w_down[:, pl.ds(pl.multiple_of(index * width, width), width)]
        return dot_f32(hidden[...], weights)

    to_left[...] = product(lax.rem(place + 3, 4)).astype(jnp.bfloat16)
    to_right[...] = product(lax.rem(place + 1, 4)).astype(jnp.bfloat16)
    far = product(lax.rem(place + 2, 4))
    far_top[...] = far[: rows // 2]
    far_low[...] = far[rows // 2 :]
    own[...] = product(place) + kept[...].astype(jnp.float32)


def down_blocks(place, hidden, kept, w_down):
    rows, width = kept.shape
    shapes = [((rows // 2, width), jnp.float32)] * 2
    shapes += [((rows, width), jnp.bfloat16)] * 2 + [((rows, width), jnp.float32)]
    return pl.pallas_call(
        down_kernel,
        out_shape=[jax.ShapeDtypeStruct(*shape) for shape in shapes],
        in_specs=[SMEM, VMEM, VMEM, VMEM],
        out_specs=[VMEM] * 5,
        compiler_params=params(6),
        cost_estimate=cost(2 * rows * w_down.shape[0] * width * 4, 5 << 20),
        name="down_blocks",
    )(place, hidden, kept, w_down)


def add_kernel(out_parts, *refs):
    whole, parts, out = refs[: -1 - out_parts], refs[-1 - out_parts : -1], refs[-1]
    step = out.shape[0] // max(out_parts, 1)
    for i, first in enumerate(range(0, out.shape[0], step)):
        rows = pl.ds(first, step)
        total = whole[0][rows, :].astype(jnp.float32)
        for ref in whole[1:]:
            total = total + ref[rows, :].astype(jnp.float32)
        if out_parts:
            total = total + parts[i][...].astype(jnp.float32)
        out[rows, :] = total.astype(jnp.bfloat16)


def add_up(whole, parts=()):
    terms = [*whole, *parts]
    size = whole[0].size
    return pl.pallas_call(
        functools.partial(add_kernel, len(parts)),
        out_shape=jax.ShapeDtypeStruct(whole[0].shape, jnp.bfloat16),
        in_specs=[VMEM] * len(terms),
        out_specs=VMEM,
        compiler_params=params(6),
        cost_estimate=cost(size * len(terms), 4 * size * len(terms)),
        name="add_up",
    )(*terms)


def feed_forward(place, pieces, tokens, gain, w_out, w_gate, w_up, w_down):
    outs = hidden_of(place, pieces, tokens, gain, w_out, w_gate, w_up, w_down)
    hidden, kept = outs[:2]
    if lax.axis_size("tp") != 4:
        share = lax.psum_scatter(
            dot_f32(hidden, w_down).astype(jnp.bfloat16), "tp", scatter_dimension=1, tiled=True
        )
        return add_up([kept, share]), hidden
    from_end = [lax.ppermute(part, "tp", [(3, 2), (0, 1)]) for part in outs[2:]]
    *far, to_right, to_left, own = down_blocks(place, hidden, kept, w_down)
    from_right = lax.ppermute(to_left, "tp", [(3, 2), (2, 1), (1, 0)])
    from_left = lax.ppermute(to_right, "tp", [(0, 1), (1, 2), (2, 3)])
    two_away = [(0, 2), (1, 3), (2, 0), (3, 1)]
    joined = [add_up([part, end]) for part, end in zip(far, from_end)]
    from_far = [lax.ppermute(part, "tp", two_away) for part in joined]
    return add_up([own, from_left, from_right], from_far), joined[-1]


def rope_tables(positions, width):
    half = HD // 2
    frequency = 10000.0 ** (-jnp.arange(half, dtype=jnp.float32) / half)
    angles = positions.astype(jnp.float32)[:, None] * frequency[None, :]
    cosine, sine = jnp.cos(angles), jnp.sin(angles)
    heads = width // HD
    return (
        jnp.concatenate([cosine, cosine] * heads, axis=1),
        jnp.concatenate([-sine, sine] * heads, axis=1),
    )


def segment_of(index, request_ends):
    return jnp.sum((index[:, None] >= request_ends[None, :]).astype(jnp.int32), axis=1)


def per_device(
    tokens,
    variate,
    positions,
    lengths,
    page_table,
    gain_attn,
    w_query,
    w_key,
    w_value,
    var_bias,
    w_out,
    gain_ffn,
    w_gate,
    w_up,
    w_down,
):
    devices = lax.axis_size("seq")
    me = lax.axis_index("seq").astype(jnp.int32)
    place = lax.axis_index("tp").astype(jnp.int32).reshape(1)
    rows = tokens.shape[0]
    width = w_query.shape[1]
    heads = width // HD
    requests = lengths.shape[0]
    reach = devices // 2

    pieces = gather_pieces(tokens)
    cosine, sine = rope_tables(positions, width)
    ends = running_sum(lengths)
    row_first = me * rows
    segment = segment_of(row_first + jnp.arange(rows, dtype=jnp.int32), ends)
    query_marks = bias_marks(variate, segment, var_bias, requests)
    request_start = jnp.sum(jnp.where(ends <= row_first, lengths, 0))
    info = jnp.concatenate([jnp.stack([me, me - request_start // rows]), ends]).astype(jnp.int32)
    first_token, amounts = page_sources(lengths, page_table, me, devices)
    extra = extra_rows(variate, 2 * width)
    gains = gain_attn.reshape(1, -1), gain_ffn.reshape(1, -1)

    ready = (pieces, w_out, cosine, sine, query_marks, info, first_token, amounts, extra, gains)
    ready = lax.optimization_barrier(ready)
    pieces, w_out, cosine, sine, query_marks, info, first_token, amounts, extra, gains = ready
    w_out_all = lax.all_gather(w_out, "tp", axis=0, tiled=True)

    token_rows, queries, pairs = project(
        pieces, place, gains[0], w_query, w_key, w_value, cosine, sine, extra
    )
    row_pieces = seq_pieces(pairs)
    attended = attend(info, queries, query_marks, row_pieces, heads, reach, requests)
    attended_pieces = turn_gather(attended)
    cache = fill_cache(me.reshape(1), first_token, amounts, row_pieces, rows)
    large = lax.optimization_barrier(((token_rows, w_out_all, w_gate, w_up, w_down), attended))[0]
    token_rows, w_out_all, w_gate, w_up, w_down = fetch(large)
    mixed, joined = feed_forward(
        place, attended_pieces, token_rows, gains[1], w_out_all, w_gate, w_up, w_down
    )
    cache, _ = lax.optimization_barrier((cache, joined))
    return (mixed, cache.reshape(cache.shape[0], 2, width))


def solution(mesh):
    placed = (
        P("seq", "tp"),
        P("seq"),
        P("seq"),
        P(),
        P(),
        P(),
        P(None, "tp"),
        P(None, "tp"),
        P(None, "tp"),
        P(None, "tp"),
        P("tp", None),
        P(),
        P(None, "tp"),
        P(None, "tp"),
        P("tp", None),
    )
    return jax.shard_map(
        per_device,
        mesh=mesh,
        in_specs=placed,
        out_specs=(P("seq", "tp"), P("seq", None, "tp")),
        check_vma=False,
    )
```

```python
import functools

import jax
import jax.numpy as jnp
import numpy as np
from jax import lax
from jax.experimental import pallas as pl
from jax.experimental.pallas import tpu as pltpu
from jax.sharding import PartitionSpec as P

HD = 64
PAGE = 64
VARS = 4
BIAS_PARTS = 3
LANES = 128
HIDDEN_SCORE = -1e30
EPS = 1e-06

VMEM = pl.BlockSpec(memory_space=pltpu.VMEM)
SMEM = pl.BlockSpec(memory_space=pltpu.SMEM)
ANY = pl.BlockSpec(memory_space=pl.ANY)
HBM = pl.BlockSpec(memory_space=pltpu.HBM)


def params(mib):
    return pltpu.CompilerParams(vmem_limit_bytes=mib << 20)


def cost(flops, nbytes, exps=0):
    return pl.CostEstimate(flops=flops, bytes_accessed=nbytes, transcendentals=exps)


def round_up(amount, unit):
    return (amount + unit - 1) // unit * unit


def dot_f32(left, right):
    return jnp.dot(left, right, preferred_element_type=jnp.float32)


def start_loads(sources, targets, sems):
    loads = [
        pltpu.make_async_copy(source, target, sems.at[i])
        for i, (source, target) in enumerate(zip(sources, targets))
    ]
    for load in loads:
        load.start()
    return loads


def finish_loads(loads):
    for load in loads:
        load.wait()


def tp_xor(value, mask):
    return lax.ppermute(value, "tp", [(i, i ^ mask) for i in range(lax.axis_size("tp"))])


def pair_gather(shard, parts, first=None):
    step = shard.shape[0] // parts
    split = [shard]
    if parts > 1:
        split = [shard[i * step : (i + 1) * step] for i in range(parts)]
        split, shard = lax.optimization_barrier((split, shard))
    far = [tp_xor(part, 2) for part in split]
    near = tp_xor(shard, 1)
    if first is not None:
        far[0], _ = lax.optimization_barrier((far[0], first))
    return [shard, near] + far + [tp_xor(part, 1) for part in far]


def turn_gather(shard):
    count = lax.axis_size("tp")
    pairs = [[(i, (i + turn) % count) for i in range(count)] for turn in range(1, count)]
    return [shard] + [lax.ppermute(shard, "tp", each) for each in pairs]


def gather_pieces(shard, parts, first=None):
    if lax.axis_size("tp") == 4:
        return pair_gather(shard, parts, first)
    return turn_gather(shard)


def assemble(pieces, place, count, target):
    width = pieces[0].shape[1]

    def put(block, value, first=0):
        columns = pl.ds(pl.multiple_of(block * width, width), width)
        target[pl.ds(first, value.shape[0]), columns] = value

    if count != 4:
        for turn, piece in enumerate(pieces):
            put(lax.rem(place + count - turn, count), piece[...])
        return
    put(place, pieces[0][...])
    put(place ^ 1, pieces[1][...])
    parts = (len(pieces) - 2) // 2
    for i in range(parts):
        first = i * (target.shape[0] // parts)
        put(place ^ 2, pieces[2 + i][...], first)
        put(place ^ 3, pieces[2 + parts + i][...], first)


def request_bounds(lengths):
    starts, ends, total = [], [], 0
    for r in range(lengths.shape[0]):
        starts.append(total)
        total = total + lengths[r]
        ends.append(total)
    return starts, ends


def segments_of(index, ends):
    segment = jnp.zeros_like(index)
    for end in ends:
        segment += (index >= end).astype(jnp.int32)
    return segment


def mark_count(requests):
    return round_up(BIAS_PARTS * VARS + requests, 16)


def tables_kernel(count, lengths, bias, frequency, positions, variate, *refs):
    cosine, sine, extra, marks = refs[count : count + 4]
    loads = start_loads(refs[:count], refs[count + 4 : -1], refs[-1])
    rows = positions.shape[1]
    width = cosine.shape[1]
    angles = frequency[...] * positions[...].astype(jnp.float32)
    cos_rows, sin_rows = jnp.cos(angles), jnp.sin(angles)
    copies = width // HD
    cosine[...] = jnp.transpose(jnp.concatenate([cos_rows, cos_rows] * copies, axis=0))
    sine[...] = jnp.transpose(jnp.concatenate([-sin_rows, sin_rows] * copies, axis=0))

    ids = variate[...].astype(jnp.float32)
    row = lax.broadcasted_iota(jnp.int32, extra.shape, 0)
    below = jnp.zeros(extra.shape, jnp.float32)
    for i in range(rows // extra.shape[1]):
        below = jnp.where(row == i, ids[:, i * extra.shape[1] : (i + 1) * extra.shape[1]], below)
    extra[...] = below.astype(jnp.bfloat16)

    requests = lengths.shape[0]
    shape = (mark_count(requests), rows)
    _, ends = request_bounds(lengths)
    me = lax.axis_index("seq")
    index = lax.broadcasted_iota(jnp.int32, shape, 1) + me * rows
    mark = lax.broadcasted_iota(jnp.int32, shape, 0)
    request = mark - BIAS_PARTS * VARS
    other = (segments_of(index, ends) != request) & (request >= 0) & (request < requests)
    same = (mark % VARS).astype(jnp.float32) == ids
    part = mark // VARS
    for h in range(marks.shape[0]):
        value = jnp.where(same, bias[0, h], bias[1, h])
        high = value.astype(jnp.bfloat16).astype(jnp.float32)
        middle = (value - high).astype(jnp.bfloat16).astype(jnp.float32)
        low = value - high - middle
        column = jnp.where(part == 0, high, jnp.where(part == 1, middle, low))
        column = jnp.where(part < BIAS_PARTS, column, 0.0)
        column = jnp.where(other, HIDDEN_SCORE, column)
        rest = jnp.zeros((LANES - shape[0], rows), jnp.float32)
        marks[h] = jnp.transpose(jnp.concatenate([column, rest], axis=0)).astype(jnp.bfloat16)
    finish_loads(loads)


def tables(lengths, bias, positions, variate, width, arrays):
    rows = positions.shape[0]
    half = HD // 2
    heads = width // HD
    frequency = 10000.0 ** (-np.arange(half, dtype=np.float32) / np.float32(half))
    extra = round_up(rows // (2 * width), 16)
    return pl.pallas_call(
        functools.partial(tables_kernel, len(arrays)),
        out_shape=[
            jax.ShapeDtypeStruct((rows, width), jnp.float32),
            jax.ShapeDtypeStruct((rows, width), jnp.float32),
            jax.ShapeDtypeStruct((extra, 2 * width), jnp.bfloat16),
            jax.ShapeDtypeStruct((heads, rows, LANES), jnp.bfloat16),
        ]
        + [jax.ShapeDtypeStruct(array.shape, array.dtype) for array in arrays],
        in_specs=[SMEM, SMEM, VMEM, VMEM, VMEM] + [ANY] * len(arrays),
        out_specs=[VMEM] * (4 + len(arrays)),
        scratch_shapes=[pltpu.SemaphoreType.DMA((len(arrays),))],
        compiler_params=params(6),
        cost_estimate=cost(rows * 1024, 1 << 20, rows * 64),
        name="tables",
    )(
        lengths,
        bias,
        jnp.asarray(frequency.astype(np.float32).reshape(half, 1)),
        positions.reshape(1, rows),
        variate.reshape(1, rows),
        *arrays,
    )


def rotate_lanes(vectors, cosine, signed_sine):
    lane = lax.broadcasted_iota(jnp.int32, vectors.shape, 1)
    half = HD // 2
    ahead = pltpu.roll(vectors, vectors.shape[1] - half, 1)
    behind = pltpu.roll(vectors, half, 1)
    partner = jnp.where(lane % HD < half, ahead, behind)
    return vectors * cosine + partner * signed_sine


def norm_rows(values, gain):
    scale = lax.rsqrt(jnp.mean(values * values, axis=-1, keepdims=True) + EPS)
    return (values * scale * gain).astype(jnp.bfloat16)


def project_kernel(places, count, *refs):
    pieces = refs[:count]
    gain, w_q, w_k, w_v, cosine, sine, extra, tokens_out, queries, pairs = refs[count:-2]
    tokens, sem = refs[-2:]
    pairs[tokens.shape[0] :, :] = extra[...]
    assemble(pieces, lax.axis_index("tp"), places, tokens)
    keep = pltpu.make_async_copy(tokens, tokens_out, sem)
    keep.start()
    rows = tokens.shape[0]
    width = w_q.shape[1]
    step = min(rows, 256)
    gain_row = gain[...].astype(jnp.float32).reshape(1, -1)
    for first in range(0, rows, step):
        part = pl.ds(first, step)
        normed = norm_rows(tokens[part, :].astype(jnp.float32), gain_row)
        cos_part, sin_part = cosine[part, :], sine[part, :]
        query = rotate_lanes(dot_f32(normed, w_q[...]), cos_part, sin_part)
        queries[part, :] = query.astype(jnp.bfloat16) * jnp.bfloat16(HD**-0.5)
        key = rotate_lanes(dot_f32(normed, w_k[...]), cos_part, sin_part)
        pairs[part, :width] = key.astype(jnp.bfloat16)
        pairs[part, width:] = dot_f32(normed, w_v[...]).astype(jnp.bfloat16)
    keep.wait()


def project(pieces, gain, w_query, w_key, w_value, cosine, sine, extra):
    rows, part = pieces[0].shape
    width = w_query.shape[1]
    features = w_query.shape[0]
    return pl.pallas_call(
        functools.partial(project_kernel, lax.axis_size("tp"), len(pieces)),
        out_shape=[
            jax.ShapeDtypeStruct((rows, features), jnp.bfloat16),
            jax.ShapeDtypeStruct((rows, width), jnp.bfloat16),
            jax.ShapeDtypeStruct((rows + extra.shape[0], 2 * width), jnp.bfloat16),
        ],
        in_specs=[VMEM] * (len(pieces) + 7),
        out_specs=[HBM, VMEM, VMEM],
        scratch_shapes=[pltpu.VMEM((rows, features), jnp.bfloat16), pltpu.SemaphoreType.DMA],
        compiler_params=params(6),
        cost_estimate=cost(6 * rows * features * width, 4 << 20),
        name="project",
    )(*pieces, gain, w_query, w_key, w_value, cosine, sine, extra)


def seq_xor(value, mask):
    return lax.ppermute(value, "seq", [(i, i ^ mask) for i in range(lax.axis_size("seq"))])


def seq_pieces(pairs):
    if lax.axis_size("seq") == 8:
        diagonal = seq_xor(pairs, 6)
        across = seq_xor(pairs, 2)
        down = seq_xor(pairs, 4)
        twin = seq_xor(pairs, 1)
        across_twin = seq_xor(across, 1)
        down_twin = seq_xor(down, 1)
        diagonal_twin = seq_xor(diagonal, 1)
        return [pairs, twin, across, across_twin, down, down_twin, diagonal, diagonal_twin]
    return [lax.all_gather(pairs, "seq", axis=0)]


def piece_copies(pieces, me, wanted):
    if len(pieces) > 1:
        for m, piece in enumerate(pieces):
            wanted(piece, me ^ m)
    else:
        for j in range(pieces[0].shape[0]):
            wanted(pieces[0].at[j], j)


def attend_kernel(count, heads, reach, lengths, queries, query_marks, *refs):
    pieces = refs[:count]
    out, q_buf, k_buf, v_buf, extra_buf, scores, peak, total, sems = refs[count:]
    me = lax.axis_index("seq")
    rows = queries.shape[0]
    _, ends = request_bounds(lengths)
    request_start = 0
    for end in ends:
        request_start = jnp.where(end <= me * rows, end, request_start)
    last = me - request_start // rows
    width = queries.shape[1]

    def copies(source, slot):
        return [
            pltpu.make_async_copy(
                source.at[pl.ds(0, rows), pl.ds(0, width)],
                k_buf.at[slot, :, pl.ds(0, width)],
                sems.at[slot, 0],
            ),
            pltpu.make_async_copy(
                source.at[pl.ds(0, rows), pl.ds(width, width)],
                v_buf.at[slot, :, pl.ds(0, width)],
                sems.at[slot, 1],
            ),
            pltpu.make_async_copy(
                source.at[pl.ds(rows, extra_buf.shape[1]), :], extra_buf.at[slot], sems.at[slot, 2]
            ),
        ]

    def begin(source, block):
        distance = me - block

        @pl.when((distance >= 0) & (distance <= last))
        def _():
            for copy in copies(source, distance):
                copy.start()

    piece_copies(pieces, me, begin)
    example = pieces[0] if count > 1 else pieces[0].at[0]

    marks = mark_count(lengths.shape[0])

    def finish(slot):
        for copy in copies(example, slot):
            copy.wait()
        extra = extra_buf[slot].astype(jnp.float32)
        pair_width = extra.shape[1]
        variates = jnp.concatenate([extra[i : i + 1] for i in range(rows // pair_width)], axis=1)
        mark = lax.broadcasted_iota(jnp.int32, (marks, rows), 0)
        key = lax.broadcasted_iota(jnp.int32, (marks, rows), 1) + (me - slot) * rows
        segment = segments_of(key, ends)
        same_variate = (mark % VARS).astype(jnp.float32) == variates
        same_segment = mark - BIAS_PARTS * VARS == segment
        marked = (same_variate & (mark < BIAS_PARTS * VARS)) | (
            same_segment & (mark >= BIAS_PARTS * VARS)
        )
        columns = jnp.transpose(jnp.where(marked, 1.0, 0.0))
        k_buf[slot, :, width : width + marks] = columns.astype(jnp.bfloat16)

    lane = lax.broadcasted_iota(jnp.int32, (rows, width), 1)
    for h in range(heads):
        part = pl.ds(h * rows, rows)
        q_buf[part, :width] = jnp.where(lane // HD == h, queries[...], jnp.bfloat16(0))
        q_buf[part, width:] = query_marks[h]
    for slot in range(reach + 1):
        v_buf[slot, :, width:] = jnp.ones((rows, LANES), jnp.bfloat16)
        k_buf[slot, :, width:] = jnp.zeros((rows, LANES), jnp.bfloat16)

    def narrow(tile):
        best = tile[:, :LANES]
        for first in range(LANES, rows, LANES):
            best = jnp.maximum(best, tile[:, first : first + LANES])
        return best

    def score(h, slot):
        return lax.dot_general(
            q_buf[pl.ds(h * rows, rows), :],
            k_buf[slot],
            (((1,), (1,)), ((), ())),
            preferred_element_type=jnp.float32,
        )

    finish(0)
    q_at = lax.broadcasted_iota(jnp.int32, (rows, rows), 0)
    k_at = lax.broadcasted_iota(jnp.int32, (rows, rows), 1)
    for h in range(heads):
        tile = jnp.where(k_at <= q_at, score(h, 0), HIDDEN_SCORE)
        scores[h, 0] = tile
        peak[h] = narrow(tile)

    def first_pass(slot, carry):
        finish(slot)
        for h in range(heads):
            tile = score(h, slot)
            scores[h, slot] = tile
            peak[h] = jnp.maximum(peak[h], narrow(tile))
        return carry

    lax.fori_loop(1, last + 1, first_pass, 0)
    for h in range(heads):
        best = jnp.max(peak[h], axis=1, keepdims=True)
        peak[h] = jnp.broadcast_to(best, (rows, LANES))
        total[h] = jnp.zeros_like(total[h])

    def second_pass(slot, carry):
        for h in range(heads):
            best = peak[h]
            wide = jnp.concatenate([best] * (rows // LANES), axis=1)
            weight = jnp.exp(scores[h, slot] - wide).astype(jnp.bfloat16)
            total[h] += dot_f32(weight, v_buf[slot])
        return carry

    lax.fori_loop(0, last + 1, second_pass, 0)
    result = total[0, :, :width] / total[0, :, width:]
    for h in range(1, heads):
        result = jnp.where(lane // HD == h, total[h, :, :width] / total[h, :, width:], result)
    out[...] = result.astype(jnp.bfloat16)


def attend(lengths, queries, query_marks, pieces, heads, reach):
    rows, width = queries.shape
    slots = reach + 1
    return pl.pallas_call(
        functools.partial(attend_kernel, len(pieces), heads, reach),
        out_shape=jax.ShapeDtypeStruct((rows, width), jnp.bfloat16),
        in_specs=[SMEM, VMEM, VMEM] + [ANY] * len(pieces),
        out_specs=VMEM,
        scratch_shapes=[
            pltpu.VMEM((heads * rows, width + LANES), jnp.bfloat16),
            pltpu.VMEM((slots, rows, width + LANES), jnp.bfloat16),
            pltpu.VMEM((slots, rows, width + LANES), jnp.bfloat16),
            pltpu.VMEM((slots, pieces[0].shape[-2] - rows, pieces[0].shape[-1]), jnp.bfloat16),
            pltpu.VMEM((heads, slots, rows, rows), jnp.float32),
            pltpu.VMEM((heads, rows, LANES), jnp.float32),
            pltpu.VMEM((heads, rows, width + LANES), jnp.float32),
            pltpu.SemaphoreType.DMA((slots, 3)),
        ],
        compiler_params=params(8 + 2 * slots),
        cost_estimate=cost(
            4 * heads * rows * rows * slots * 256, 4 << 20, heads * rows * rows * slots
        ),
        name="attend",
    )(lengths, queries, query_marks, *pieces)


def cache_kernel(count, window, lengths, page_table, *refs):
    pieces = refs[:count]
    out, rows_buf, logical, sems = refs[count:]
    rows = rows_buf.shape[1]
    blocks = rows_buf.shape[0]
    width = out.shape[2]
    pages = out.shape[0] // PAGE
    me = lax.axis_index("seq")
    started = []

    def begin(source, block):
        copy = pltpu.make_async_copy(
            source.at[pl.ds(0, rows), :], rows_buf.at[block], sems.at[len(started)]
        )
        copy.start()
        started.append(copy)

    piece_copies(pieces, me, begin)

    def place_page(page, carry):
        local = page_table[page] - me * pages

        @pl.when((local >= 0) & (local < pages))
        def _():
            logical[local] = page

        return carry

    lax.fori_loop(0, page_table.shape[0], place_page, 0)
    starts, _ = request_bounds(lengths)
    for copy in started:
        copy.wait()
    row = lax.broadcasted_iota(jnp.int32, (PAGE, window), 0)
    column = lax.broadcasted_iota(jnp.int32, (PAGE, window), 1)

    def one_page(page, carry):
        first, amount, base = 0, 0, 0
        for r, start in enumerate(starts):
            count_r = (lengths[r] + PAGE - 1) // PAGE
            ahead = (logical[page] - base) * PAGE
            within = (ahead >= 0) & (ahead < lengths[r])
            first = jnp.where(within, start + ahead, first)
            amount = jnp.where(within, jnp.minimum(lengths[r] - ahead, PAGE), amount)
            base = base + count_r
        block = first // rows
        total = None
        for ahead in range(2):
            at = jnp.minimum(block + ahead, blocks - 1)
            inside = first - block * rows
            if ahead == 0:
                start = jnp.minimum(inside // 16 * 16, rows - window)
                offset = inside - start
            else:
                start = 0
                offset = inside - rows
            wanted = (row + offset == column) & (row < amount)
            if ahead == 1:
                wanted = wanted & (block + 1 < blocks)
            chooser = jnp.where(wanted, 1.0, 0.0).astype(jnp.bfloat16)
            found = dot_f32(chooser, rows_buf[at, pl.ds(pl.multiple_of(start, 16), window), :])
            total = found if total is None else total + found
        part = pl.ds(pl.multiple_of(page * PAGE, PAGE), PAGE)
        out[part, 0, :] = total[:, :width].astype(jnp.bfloat16)
        out[part, 1, :] = total[:, width:].astype(jnp.bfloat16)
        return carry

    lax.fori_loop(0, pages, one_page, 0)


def fill_cache(lengths, page_table, pieces, rows):
    width = pieces[0].shape[-1]
    blocks = lax.axis_size("seq")
    pages = page_table.shape[0] // blocks
    return pl.pallas_call(
        functools.partial(cache_kernel, len(pieces), 2 * PAGE),
        out_shape=jax.ShapeDtypeStruct((pages * PAGE, 2, width // 2), jnp.bfloat16),
        in_specs=[SMEM] * 2 + [ANY] * len(pieces),
        out_specs=VMEM,
        scratch_shapes=[
            pltpu.VMEM((blocks, rows, width), jnp.bfloat16),
            pltpu.SMEM((pages,), jnp.int32),
            pltpu.SemaphoreType.DMA((blocks,)),
        ],
        compiler_params=params(8),
        cost_estimate=cost(4 * pages * PAGE * 2 * PAGE * width, 3 << 20),
        name="fill_cache",
    )(lengths, page_table, *pieces)


def fetch_kernel(count, *refs):
    finish_loads(start_loads(refs[:count], refs[count:-1], refs[-1]))


def fetch(arrays):
    return pl.pallas_call(
        functools.partial(fetch_kernel, len(arrays)),
        out_shape=[jax.ShapeDtypeStruct(array.shape, array.dtype) for array in arrays],
        in_specs=[HBM] * len(arrays),
        out_specs=[VMEM] * len(arrays),
        scratch_shapes=[pltpu.SemaphoreType.DMA((len(arrays),))],
        compiler_params=params(10),
        cost_estimate=cost(0, 4 * sum(array.size for array in arrays)),
        name="fetch",
    )(*arrays)


def hidden_kernel(places, count, on_line, *refs):
    pieces = refs[:count]
    tokens, gain, w_out, w_gate, w_up, w_down = refs[count : count + 6]
    outs, attended = refs[count + 6 : -1], refs[-1]
    hidden, kept = outs[:2]
    place = lax.axis_index("tp")
    assemble(pieces, place, places, attended)
    rows, features = tokens.shape
    width = kept.shape[1]
    step = min(rows, 256)
    gain_row = gain[...].astype(jnp.float32).reshape(1, -1)
    for first in range(0, rows, step):
        part = pl.ds(first, step)
        projected = dot_f32(attended[part, :], w_out[...])
        residual = (tokens[part, :].astype(jnp.float32) + projected).astype(jnp.bfloat16)
        mine = residual[:, :width]
        for i in range(1, places):
            mine = jnp.where(place == i, residual[:, i * width : (i + 1) * width], mine)
        kept[part, :] = mine
        normed = norm_rows(residual.astype(jnp.float32), gain_row)
        gate = dot_f32(normed, w_gate[...])
        up = dot_f32(normed, w_up[...])
        hidden[part, :] = (jax.nn.silu(gate) * up).astype(jnp.bfloat16)
    if not on_line:
        return

    weights = w_down[:, pl.ds(pl.multiple_of((place ^ 3) * width, width), width)]
    through = dot_f32(hidden[...], weights).astype(jnp.bfloat16)
    outs[2][...] = through[: rows // 2]
    outs[3][...] = through[rows // 2 :]


def hidden_of(pieces, tokens, gain, w_out, w_gate, w_up, w_down):
    rows, features = tokens.shape
    places = lax.axis_size("tp")
    width = features // places
    units = w_gate.shape[1]
    on_line = places == 4
    shapes = [
        jax.ShapeDtypeStruct((rows, units), jnp.bfloat16),
        jax.ShapeDtypeStruct((rows, width), jnp.bfloat16),
    ]
    if on_line:
        shapes += [jax.ShapeDtypeStruct((rows // 2, width), jnp.bfloat16)] * 2
    return pl.pallas_call(
        functools.partial(hidden_kernel, places, len(pieces), on_line),
        out_shape=shapes,
        in_specs=[VMEM] * (len(pieces) + 6),
        out_specs=[VMEM] * len(shapes),
        scratch_shapes=[pltpu.VMEM((rows, w_out.shape[0]), jnp.bfloat16)],
        compiler_params=params(12),
        cost_estimate=cost(6 * rows * features * units, 10 << 20),
        name="hidden",
    )(*pieces, tokens, gain, w_out, w_gate, w_up, w_down)


def down_kernel(hidden, kept, w_down, far_top, far_low, near, own):
    place = lax.axis_index("tp")
    rows, width = own.shape

    def product(index):
        weights = w_down[:, pl.ds(pl.multiple_of(index * width, width), width)]
        return dot_f32(hidden[...], weights)

    far = product(place ^ 2)
    far_top[...] = far[: rows // 2]
    far_low[...] = far[rows // 2 :]
    near[...] = product(place ^ 1).astype(jnp.bfloat16)
    own[...] = product(place) + kept[...].astype(jnp.float32)


def down_blocks(hidden, kept, w_down):
    rows, width = kept.shape
    shapes = [((rows // 2, width), jnp.float32)] * 2
    shapes += [((rows, width), jnp.bfloat16), ((rows, width), jnp.float32)]
    return pl.pallas_call(
        down_kernel,
        out_shape=[jax.ShapeDtypeStruct(*shape) for shape in shapes],
        in_specs=[VMEM] * 3,
        out_specs=[VMEM] * 4,
        compiler_params=params(6),
        cost_estimate=cost(2 * rows * w_down.shape[0] * width * 3, 5 << 20),
        name="down_blocks",
    )(hidden, kept, w_down)


def add_kernel(out_parts, *refs):
    whole, parts, out = refs[: -1 - out_parts], refs[-1 - out_parts : -1], refs[-1]
    step = out.shape[0] // max(out_parts, 1)
    for i, first in enumerate(range(0, out.shape[0], step)):
        rows = pl.ds(first, step)
        total = whole[0][rows, :].astype(jnp.float32)
        for ref in whole[1:]:
            total = total + ref[rows, :].astype(jnp.float32)
        if out_parts:
            total = total + parts[i][...].astype(jnp.float32)
        out[rows, :] = total.astype(jnp.bfloat16)


def add_up(whole, parts=()):
    terms = [*whole, *parts]
    size = whole[0].size
    return pl.pallas_call(
        functools.partial(add_kernel, len(parts)),
        out_shape=jax.ShapeDtypeStruct(whole[0].shape, jnp.bfloat16),
        in_specs=[VMEM] * len(terms),
        out_specs=VMEM,
        compiler_params=params(6),
        cost_estimate=cost(size * len(terms), 4 * size * len(terms)),
        name="add_up",
    )(*terms)


def feed_forward(pieces, tokens, gain, w_out, w_gate, w_up, w_down):
    hidden, kept, *through = hidden_of(pieces, tokens, gain, w_out, w_gate, w_up, w_down)
    if lax.axis_size("tp") != 4:
        share = lax.psum_scatter(
            dot_f32(hidden, w_down).astype(jnp.bfloat16), "tp", scatter_dimension=1, tiled=True
        )
        return add_up([kept, share]), hidden
    through = [tp_xor(part, 1) for part in through]
    far_top, far_low, near, own = down_blocks(hidden, kept, w_down)
    joined = [add_up([part, other]) for part, other in zip((far_top, far_low), through)]
    near = tp_xor(near, 1)
    far = [tp_xor(part, 2) for part in joined]
    return add_up([own, near], far), joined[-1]


def per_device(
    tokens,
    variate,
    positions,
    lengths,
    page_table,
    gain_attn,
    w_query,
    w_key,
    w_value,
    var_bias,
    w_out,
    gain_ffn,
    w_gate,
    w_up,
    w_down,
):
    rows = tokens.shape[0]
    width = w_query.shape[1]
    heads = width // HD
    reach = lax.axis_size("seq") // 2

    weights = (tokens, gain_attn, w_query, w_key, w_value)
    cosine, sine, extra, marks, *weights = tables(
        lengths, var_bias, positions, variate, width, weights
    )
    pieces = gather_pieces(tokens, 2, extra)
    pieces, w_out = lax.optimization_barrier((pieces, w_out))
    w_out_all = lax.all_gather(w_out, "tp", axis=0, tiled=True)
    pieces[0] = weights[0]
    token_rows, queries, pairs = project(pieces, *weights[1:], cosine, sine, extra)
    row_pieces = seq_pieces(pairs)
    attended = attend(lengths, queries, marks, row_pieces, heads, reach)
    attended_pieces = gather_pieces(attended, 1)
    large = (token_rows, gain_ffn, w_out_all, w_gate, w_up, w_down)
    large = lax.optimization_barrier((large, attended))[0]
    mixed, joined = feed_forward(attended_pieces, *fetch(large))
    row_pieces, _ = lax.optimization_barrier((row_pieces, joined))
    cache = fill_cache(lengths, page_table, row_pieces, rows)
    return (mixed, cache)


def solution(mesh):
    placed = (
        P("seq", "tp"),
        P("seq"),
        P("seq"),
        P(),
        P(),
        P(),
        P(None, "tp"),
        P(None, "tp"),
        P(None, "tp"),
        P(None, "tp"),
        P("tp", None),
        P(),
        P(None, "tp"),
        P(None, "tp"),
        P("tp", None),
    )
    return jax.shard_map(
        per_device,
        mesh=mesh,
        in_specs=placed,
        out_specs=(P("seq", "tp"), P("seq", None, "tp")),
        check_vma=False,
    )
```

```python
import functools

import jax
import jax.numpy as jnp
import numpy as np
from jax import lax
from jax.experimental import pallas as pl
from jax.experimental.pallas import tpu as pltpu
from jax.sharding import PartitionSpec as P

HD = 64
PAGE = 64
VARS = 4
BIAS_PARTS = 3
LANES = 128
HIDDEN_SCORE = -1e30
EPS = 1e-06

VMEM = pl.BlockSpec(memory_space=pltpu.VMEM)
SMEM = pl.BlockSpec(memory_space=pltpu.SMEM)
ANY = pl.BlockSpec(memory_space=pl.ANY)
HBM = pl.BlockSpec(memory_space=pltpu.HBM)


def params(mib):
    return pltpu.CompilerParams(vmem_limit_bytes=mib << 20)


def cost(flops, nbytes, exps=0):
    return pl.CostEstimate(flops=flops, bytes_accessed=nbytes, transcendentals=exps)


def round_up(amount, unit):
    return (amount + unit - 1) // unit * unit


def dot_f32(left, right):
    return jnp.dot(left, right, preferred_element_type=jnp.float32)


def start_loads(sources, targets, sems):
    loads = [
        pltpu.make_async_copy(source, target, sems.at[i])
        for i, (source, target) in enumerate(zip(sources, targets))
    ]
    for load in loads:
        load.start()
    return loads


def finish_loads(loads):
    for load in loads:
        load.wait()


def tp_xor(value, mask):
    return lax.ppermute(value, "tp", [(i, i ^ mask) for i in range(lax.axis_size("tp"))])


def pair_gather(shard, parts):
    step = shard.shape[0] // parts
    split = [shard]
    if parts > 1:
        split = [shard[i * step : (i + 1) * step] for i in range(parts)]
        split, shard = lax.optimization_barrier((split, shard))
    far = [tp_xor(part, 2) for part in split]
    near = tp_xor(shard, 1)
    return [shard, near] + far + [tp_xor(part, 1) for part in far]


def turn_gather(shard):
    count = lax.axis_size("tp")
    turns = sorted(range(1, count), key=lambda turn: -min(turn, count - turn))
    moved = {
        turn: lax.ppermute(shard, "tp", [(i, (i + turn) % count) for i in range(count)])
        for turn in turns
    }
    return [shard] + [moved[turn] for turn in range(1, count)]


def gather_pieces(shard, parts):
    if lax.axis_size("tp") == 4:
        return pair_gather(shard, parts)
    return turn_gather(shard)


def assemble(pieces, place, count, target, part=slice(None)):
    width = pieces[0].shape[1]

    def put(block, value, first=0):
        columns = pl.ds(pl.multiple_of(block * width, width), width)
        target[pl.ds(first, value.shape[0]), columns] = value

    if len(pieces) == count:
        for turn, piece in enumerate(pieces):
            put(lax.rem(place + count - turn, count), piece[part, :])
        return
    put(place, pieces[0][...])
    put(place ^ 1, pieces[1][...])
    parts = (len(pieces) - 2) // 2
    for i in range(parts):
        first = i * (target.shape[0] // parts)
        put(place ^ 2, pieces[2 + i][...], first)
        put(place ^ 3, pieces[2 + parts + i][...], first)


def request_bounds(lengths):
    starts, ends, total = [], [], 0
    for r in range(lengths.shape[0]):
        starts.append(total)
        total = total + lengths[r]
        ends.append(total)
    return starts, ends


def segments_of(index, ends):
    segment = jnp.zeros_like(index)
    for end in ends:
        segment += (index >= end).astype(jnp.int32)
    return segment


def mark_count(requests):
    return round_up(BIAS_PARTS * VARS + requests, 16)


def tables_kernel(
    lengths, bias, frequency, positions, variate, cosine, sine, extra, marks
):
    rows = positions.shape[1]
    width = cosine.shape[1]
    angles = frequency[...] * positions[...].astype(jnp.float32)
    cos_rows, sin_rows = jnp.cos(angles), jnp.sin(angles)
    copies = width // HD
    cosine[...] = jnp.transpose(jnp.concatenate([cos_rows, cos_rows] * copies, axis=0))
    sine[...] = jnp.transpose(jnp.concatenate([-sin_rows, sin_rows] * copies, axis=0))

    ids = variate[...].astype(jnp.float32)
    row = lax.broadcasted_iota(jnp.int32, extra.shape, 0)
    below = jnp.zeros(extra.shape, jnp.float32)
    for i in range(rows // extra.shape[1]):
        below = jnp.where(row == i, ids[:, i * extra.shape[1] : (i + 1) * extra.shape[1]], below)
    extra[...] = below.astype(jnp.bfloat16)

    requests = lengths.shape[0]
    shape = (mark_count(requests), rows)
    _, ends = request_bounds(lengths)
    me = lax.axis_index("seq")
    index = lax.broadcasted_iota(jnp.int32, shape, 1) + me * rows
    mark = lax.broadcasted_iota(jnp.int32, shape, 0)
    request = mark - BIAS_PARTS * VARS
    other = (segments_of(index, ends) != request) & (request >= 0) & (request < requests)
    same = (mark % VARS).astype(jnp.float32) == ids
    part = mark // VARS
    for h in range(marks.shape[0]):
        value = jnp.where(same, bias[0, h], bias[1, h])
        high = value.astype(jnp.bfloat16).astype(jnp.float32)
        middle = (value - high).astype(jnp.bfloat16).astype(jnp.float32)
        low = value - high - middle
        column = jnp.where(part == 0, high, jnp.where(part == 1, middle, low))
        column = jnp.where(part < BIAS_PARTS, column, 0.0)
        column = jnp.where(other, HIDDEN_SCORE, column)
        rest = jnp.zeros((LANES - shape[0], rows), jnp.float32)
        marks[h] = jnp.transpose(jnp.concatenate([column, rest], axis=0)).astype(jnp.bfloat16)


def tables(lengths, bias, positions, variate, width):
    rows = positions.shape[0]
    half = HD // 2
    heads = width // HD
    frequency = 10000.0 ** (-np.arange(half, dtype=np.float32) / np.float32(half))
    extra = round_up(rows // (2 * width), 16)
    return pl.pallas_call(
        tables_kernel,
        out_shape=[
            jax.ShapeDtypeStruct((rows, width), jnp.float32),
            jax.ShapeDtypeStruct((rows, width), jnp.float32),
            jax.ShapeDtypeStruct((extra, 2 * width), jnp.bfloat16),
            jax.ShapeDtypeStruct((heads, rows, LANES), jnp.bfloat16),
        ],
        in_specs=[SMEM, SMEM, VMEM, VMEM, VMEM],
        out_specs=[VMEM] * 4,
        compiler_params=params(60),
        cost_estimate=cost(rows * 1024, 1 << 20, rows * 64),
        name="tables",
    )(
        lengths,
        bias,
        jnp.asarray(frequency.astype(np.float32).reshape(half, 1)),
        positions.reshape(1, rows),
        variate.reshape(1, rows),
    )


def rotate_lanes(vectors, cosine, signed_sine):
    lane = lax.broadcasted_iota(jnp.int32, vectors.shape, 1)
    half = HD // 2
    ahead = pltpu.roll(vectors, vectors.shape[1] - half, 1)
    behind = pltpu.roll(vectors, half, 1)
    partner = jnp.where(lane % HD < half, ahead, behind)
    return vectors * cosine + partner * signed_sine


def norm_rows(values, gain):
    scale = lax.rsqrt(jnp.mean(values * values, axis=-1, keepdims=True) + EPS)
    return (values * scale * gain).astype(jnp.bfloat16)


def project_kernel(places, count, *refs):
    pieces = refs[:count]
    gain, w_q, w_k, w_v, cosine, sine, extra, tokens_out, queries, pairs = refs[count:-2]
    tokens, sem = refs[-2:]
    pairs[tokens.shape[0] :, :] = extra[...]
    assemble(pieces, lax.axis_index("tp"), places, tokens)
    keep = pltpu.make_async_copy(tokens, tokens_out, sem)
    keep.start()
    rows = tokens.shape[0]
    width = w_q.shape[1]
    step = min(rows, 256)
    gain_row = gain[...].astype(jnp.float32).reshape(1, -1)
    for first in range(0, rows, step):
        part = pl.ds(first, step)
        normed = norm_rows(tokens[part, :].astype(jnp.float32), gain_row)
        cos_part, sin_part = cosine[part, :], sine[part, :]
        query = rotate_lanes(dot_f32(normed, w_q[...]), cos_part, sin_part)
        queries[part, :] = query.astype(jnp.bfloat16) * jnp.bfloat16(HD**-0.5)
        key = rotate_lanes(dot_f32(normed, w_k[...]), cos_part, sin_part)
        pairs[part, :width] = key.astype(jnp.bfloat16)
        pairs[part, width:] = dot_f32(normed, w_v[...]).astype(jnp.bfloat16)
    keep.wait()


def project(pieces, gain, w_query, w_key, w_value, cosine, sine, extra):
    rows, part = pieces[0].shape
    width = w_query.shape[1]
    features = w_query.shape[0]
    return pl.pallas_call(
        functools.partial(project_kernel, lax.axis_size("tp"), len(pieces)),
        out_shape=[
            jax.ShapeDtypeStruct((rows, features), jnp.bfloat16),
            jax.ShapeDtypeStruct((rows, width), jnp.bfloat16),
            jax.ShapeDtypeStruct((rows + extra.shape[0], 2 * width), jnp.bfloat16),
        ],
        in_specs=[VMEM] * (len(pieces) + 7),
        out_specs=[HBM, VMEM, VMEM],
        scratch_shapes=[pltpu.VMEM((rows, features), jnp.bfloat16), pltpu.SemaphoreType.DMA],
        compiler_params=params(60),
        cost_estimate=cost(6 * rows * features * width, 4 << 20),
        name="project",
    )(*pieces, gain, w_query, w_key, w_value, cosine, sine, extra)


def seq_xor(value, mask):
    return lax.ppermute(value, "seq", [(i, i ^ mask) for i in range(lax.axis_size("seq"))])


def seq_pieces(pairs):
    if lax.axis_size("seq") == 8:
        diagonal = seq_xor(pairs, 6)
        across = seq_xor(pairs, 2)
        down = seq_xor(pairs, 4)
        twin = seq_xor(pairs, 1)
        across_twin = seq_xor(across, 1)
        down_twin = seq_xor(down, 1)
        diagonal_twin = seq_xor(diagonal, 1)
        return [pairs, twin, across, across_twin, down, down_twin, diagonal, diagonal_twin]
    return [lax.all_gather(pairs, "seq", axis=0)]


def piece_copies(pieces, me, wanted):
    if len(pieces) > 1:
        for m, piece in enumerate(pieces):
            wanted(piece, me ^ m)
    else:
        for j in range(pieces[0].shape[0]):
            wanted(pieces[0].at[j], j)


def attend_kernel(count, heads, reach, lengths, queries, query_marks, *refs):
    pieces = refs[:count]
    out, q_buf, k_buf, v_buf, extra_buf, scores, peak, total, sems = refs[count:]
    me = lax.axis_index("seq")
    rows = queries.shape[0]
    _, ends = request_bounds(lengths)
    request_start = 0
    for end in ends:
        request_start = jnp.where(end <= me * rows, end, request_start)
    last = me - request_start // rows
    width = queries.shape[1]

    def copies(source, slot):
        return [
            pltpu.make_async_copy(
                source.at[pl.ds(0, rows), pl.ds(0, width)],
                k_buf.at[slot, :, pl.ds(0, width)],
                sems.at[slot, 0],
            ),
            pltpu.make_async_copy(
                source.at[pl.ds(0, rows), pl.ds(width, width)],
                v_buf.at[slot, :, pl.ds(0, width)],
                sems.at[slot, 1],
            ),
            pltpu.make_async_copy(
                source.at[pl.ds(rows, extra_buf.shape[1]), :], extra_buf.at[slot], sems.at[slot, 2]
            ),
        ]

    def begin(source, block):
        distance = me - block

        @pl.when((distance >= 0) & (distance <= last))
        def _():
            for copy in copies(source, distance):
                copy.start()

    piece_copies(pieces, me, begin)
    example = pieces[0] if count > 1 else pieces[0].at[0]

    marks = mark_count(lengths.shape[0])

    def finish(slot):
        for copy in copies(example, slot):
            copy.wait()
        extra = extra_buf[slot].astype(jnp.float32)
        pair_width = extra.shape[1]
        variates = jnp.concatenate([extra[i : i + 1] for i in range(rows // pair_width)], axis=1)
        mark = lax.broadcasted_iota(jnp.int32, (marks, rows), 0)
        key = lax.broadcasted_iota(jnp.int32, (marks, rows), 1) + (me - slot) * rows
        segment = segments_of(key, ends)
        same_variate = (mark % VARS).astype(jnp.float32) == variates
        same_segment = mark - BIAS_PARTS * VARS == segment
        marked = (same_variate & (mark < BIAS_PARTS * VARS)) | (
            same_segment & (mark >= BIAS_PARTS * VARS)
        )
        columns = jnp.transpose(jnp.where(marked, 1.0, 0.0))
        k_buf[slot, :, width : width + marks] = columns.astype(jnp.bfloat16)

    lane = lax.broadcasted_iota(jnp.int32, (rows, width), 1)
    for h in range(heads):
        part = pl.ds(h * rows, rows)
        q_buf[part, :width] = jnp.where(lane // HD == h, queries[...], jnp.bfloat16(0))
        q_buf[part, width:] = query_marks[h]
    for slot in range(reach + 1):
        v_buf[slot, :, width:] = jnp.ones((rows, LANES), jnp.bfloat16)
        k_buf[slot, :, width:] = jnp.zeros((rows, LANES), jnp.bfloat16)

    def narrow(tile):
        best = tile[:, :LANES]
        for first in range(LANES, rows, LANES):
            best = jnp.maximum(best, tile[:, first : first + LANES])
        return best

    def score(h, slot):
        return lax.dot_general(
            q_buf[pl.ds(h * rows, rows), :],
            k_buf[slot],
            (((1,), (1,)), ((), ())),
            preferred_element_type=jnp.float32,
        )

    finish(0)
    q_at = lax.broadcasted_iota(jnp.int32, (rows, rows), 0)
    k_at = lax.broadcasted_iota(jnp.int32, (rows, rows), 1)
    for h in range(heads):
        tile = jnp.where(k_at <= q_at, score(h, 0), HIDDEN_SCORE)
        scores[h, 0] = tile
        peak[h] = narrow(tile)

    def first_pass(slot, carry):
        finish(slot)
        for h in range(heads):
            tile = score(h, slot)
            scores[h, slot] = tile
            peak[h] = jnp.maximum(peak[h], narrow(tile))
        return carry

    lax.fori_loop(1, last + 1, first_pass, 0)
    for h in range(heads):
        best = jnp.max(peak[h], axis=1, keepdims=True)
        peak[h] = jnp.broadcast_to(best, (rows, LANES))
        total[h] = jnp.zeros_like(total[h])

    def second_pass(slot, carry):
        for h in range(heads):
            best = peak[h]
            wide = jnp.concatenate([best] * (rows // LANES), axis=1)
            weight = jnp.exp(scores[h, slot] - wide).astype(jnp.bfloat16)
            total[h] += dot_f32(weight, v_buf[slot])
        return carry

    lax.fori_loop(0, last + 1, second_pass, 0)
    result = total[0, :, :width] / total[0, :, width:]
    for h in range(1, heads):
        result = jnp.where(lane // HD == h, total[h, :, :width] / total[h, :, width:], result)
    out[...] = result.astype(jnp.bfloat16)


def attend(lengths, queries, query_marks, pieces, heads, reach):
    rows, width = queries.shape
    slots = reach + 1
    return pl.pallas_call(
        functools.partial(attend_kernel, len(pieces), heads, reach),
        out_shape=jax.ShapeDtypeStruct((rows, width), jnp.bfloat16),
        in_specs=[SMEM, VMEM, VMEM] + [ANY] * len(pieces),
        out_specs=VMEM,
        scratch_shapes=[
            pltpu.VMEM((heads * rows, width + LANES), jnp.bfloat16),
            pltpu.VMEM((slots, rows, width + LANES), jnp.bfloat16),
            pltpu.VMEM((slots, rows, width + LANES), jnp.bfloat16),
            pltpu.VMEM((slots, pieces[0].shape[-2] - rows, pieces[0].shape[-1]), jnp.bfloat16),
            pltpu.VMEM((heads, slots, rows, rows), jnp.float32),
            pltpu.VMEM((heads, rows, LANES), jnp.float32),
            pltpu.VMEM((heads, rows, width + LANES), jnp.float32),
            pltpu.SemaphoreType.DMA((slots, 3)),
        ],
        compiler_params=params(8 + 2 * slots),
        cost_estimate=cost(
            4 * heads * rows * rows * slots * 256, 4 << 20, heads * rows * rows * slots
        ),
        name="attend",
    )(lengths, queries, query_marks, *pieces)


def cache_kernel(count, window, lengths, page_table, *refs):
    pieces = refs[:count]
    out, rows_buf, logical, sems = refs[count:]
    rows = rows_buf.shape[1]
    blocks = rows_buf.shape[0]
    width = out.shape[2]
    pages = out.shape[0] // PAGE
    me = lax.axis_index("seq")
    started = []

    def begin(source, block):
        copy = pltpu.make_async_copy(
            source.at[pl.ds(0, rows), :], rows_buf.at[block], sems.at[len(started)]
        )
        copy.start()
        started.append(copy)

    piece_copies(pieces, me, begin)

    def place_page(page, carry):
        local = page_table[page] - me * pages

        @pl.when((local >= 0) & (local < pages))
        def _():
            logical[local] = page

        return carry

    lax.fori_loop(0, page_table.shape[0], place_page, 0)
    starts, _ = request_bounds(lengths)
    for copy in started:
        copy.wait()
    row = lax.broadcasted_iota(jnp.int32, (PAGE, window), 0)
    column = lax.broadcasted_iota(jnp.int32, (PAGE, window), 1)

    def one_page(page, carry):
        first, amount, base = 0, 0, 0
        for r, start in enumerate(starts):
            count_r = (lengths[r] + PAGE - 1) // PAGE
            ahead = (logical[page] - base) * PAGE
            within = (ahead >= 0) & (ahead < lengths[r])
            first = jnp.where(within, start + ahead, first)
            amount = jnp.where(within, jnp.minimum(lengths[r] - ahead, PAGE), amount)
            base = base + count_r
        block = first // rows
        total = None
        for ahead in range(2):
            at = jnp.minimum(block + ahead, blocks - 1)
            inside = first - block * rows
            if ahead == 0:
                start = jnp.minimum(inside // 16 * 16, rows - window)
                offset = inside - start
            else:
                start = 0
                offset = inside - rows
            wanted = (row + offset == column) & (row < amount)
            if ahead == 1:
                wanted = wanted & (block + 1 < blocks)
            chooser = jnp.where(wanted, 1.0, 0.0).astype(jnp.bfloat16)
            found = dot_f32(chooser, rows_buf[at, pl.ds(pl.multiple_of(start, 16), window), :])
            total = found if total is None else total + found
        part = pl.ds(pl.multiple_of(page * PAGE, PAGE), PAGE)
        out[part, 0, :] = total[:, :width].astype(jnp.bfloat16)
        out[part, 1, :] = total[:, width:].astype(jnp.bfloat16)
        return carry

    lax.fori_loop(0, pages, one_page, 0)


def fill_cache(lengths, page_table, pieces, rows):
    width = pieces[0].shape[-1]
    blocks = lax.axis_size("seq")
    pages = page_table.shape[0] // blocks
    return pl.pallas_call(
        functools.partial(cache_kernel, len(pieces), 2 * PAGE),
        out_shape=jax.ShapeDtypeStruct((pages * PAGE, 2, width // 2), jnp.bfloat16),
        in_specs=[SMEM] * 2 + [ANY] * len(pieces),
        out_specs=VMEM,
        scratch_shapes=[
            pltpu.VMEM((blocks, rows, width), jnp.bfloat16),
            pltpu.SMEM((pages,), jnp.int32),
            pltpu.SemaphoreType.DMA((blocks,)),
        ],
        compiler_params=params(8),
        cost_estimate=cost(4 * pages * PAGE * 2 * PAGE * width, 3 << 20),
        name="fill_cache",
    )(lengths, page_table, *pieces)


def fetch_kernel(count, *refs):
    finish_loads(start_loads(refs[:count], refs[count:-1], refs[-1]))


def fetch(arrays):
    return pl.pallas_call(
        functools.partial(fetch_kernel, len(arrays)),
        out_shape=[jax.ShapeDtypeStruct(array.shape, array.dtype) for array in arrays],
        in_specs=[HBM] * len(arrays),
        out_specs=[VMEM] * len(arrays),
        scratch_shapes=[pltpu.SemaphoreType.DMA((len(arrays),))],
        compiler_params=params(10),
        cost_estimate=cost(0, 4 * sum(array.size for array in arrays)),
        name="fetch",
    )(*arrays)


def hidden_kernel(places, count, first, *refs):
    pieces = refs[:count]
    tokens, gain, w_out, w_gate, w_up, w_down = refs[count : count + 6]
    outs, attended = refs[count + 6 : -1], refs[-1]
    hidden, kept = outs[:2]
    place = lax.axis_index("tp")
    rows, width = kept.shape
    part = pl.ds(first, rows)
    assemble(pieces, place, places, attended, part)
    projected = dot_f32(attended[...], w_out[...])
    residual = (tokens[part, :].astype(jnp.float32) + projected).astype(jnp.bfloat16)
    mine = residual[:, :width]
    for i in range(1, places):
        mine = jnp.where(place == i, residual[:, i * width : (i + 1) * width], mine)
    kept[...] = mine
    gain_row = gain[...].astype(jnp.float32).reshape(1, -1)
    normed = norm_rows(residual.astype(jnp.float32), gain_row)
    gate = dot_f32(normed, w_gate[...])
    up = dot_f32(normed, w_up[...])
    hidden[...] = (jax.nn.silu(gate) * up).astype(jnp.bfloat16)
    if len(outs) > 2:
        weights = w_down[:, pl.ds(pl.multiple_of((place ^ 3) * width, width), width)]
        outs[2][...] = dot_f32(hidden[...], weights).astype(jnp.bfloat16)


def hidden_of(pieces, tokens, gain, w_out, w_gate, w_up, w_down, part, parts):
    rows, features = tokens.shape[0] // parts, tokens.shape[1]
    places = lax.axis_size("tp")
    width = features // places
    units = w_gate.shape[1]
    widths = [units, width] + [width] * (places == 4)
    return pl.pallas_call(
        functools.partial(hidden_kernel, places, len(pieces), part * rows),
        out_shape=[jax.ShapeDtypeStruct((rows, each), jnp.bfloat16) for each in widths],
        in_specs=[VMEM] * (len(pieces) + 6),
        out_specs=[VMEM] * len(widths),
        scratch_shapes=[pltpu.VMEM((rows, w_out.shape[0]), jnp.bfloat16)],
        compiler_params=params(12),
        cost_estimate=cost(6 * rows * features * units, 10 << 20),
        name="hidden",
    )(*pieces, tokens, gain, w_out, w_gate, w_up, w_down)


def down_kernel(parts, *refs):
    hidden, kept, w_down = refs[:parts], refs[parts : 2 * parts], refs[2 * parts]
    far, near, own = refs[2 * parts + 1 : 3 * parts + 1], refs[-2], refs[-1]
    place = lax.axis_index("tp")
    width = own.shape[1]
    rows = own.shape[0] // parts

    def weights(index):
        return w_down[:, pl.ds(pl.multiple_of(index * width, width), width)]

    for i in range(parts):
        far[i][...] = dot_f32(hidden[i][...], weights(place ^ 2))
    for i in range(parts):
        part = pl.ds(i * rows, rows)
        near[part, :] = dot_f32(hidden[i][...], weights(place ^ 1)).astype(jnp.bfloat16)
    for i in range(parts):
        part = pl.ds(i * rows, rows)
        own[part, :] = dot_f32(hidden[i][...], weights(place)) + kept[i][...].astype(jnp.float32)


def down_blocks(hidden, kept, w_down):
    parts = len(hidden)
    rows, width = kept[0].shape
    shapes = [((rows, width), jnp.float32)] * parts
    shapes += [((rows * parts, width), jnp.bfloat16), ((rows * parts, width), jnp.float32)]
    *far, near, own = pl.pallas_call(
        functools.partial(down_kernel, parts),
        out_shape=[jax.ShapeDtypeStruct(*shape) for shape in shapes],
        in_specs=[VMEM] * (2 * parts + 1),
        out_specs=[VMEM] * len(shapes),
        compiler_params=params(6),
        cost_estimate=cost(2 * rows * parts * w_down.shape[0] * width * 3, 5 << 20),
        name="down_blocks",
    )(*hidden, *kept, w_down)
    return far, near, own


def add_kernel(out_parts, *refs):
    whole, parts, out = refs[: -1 - out_parts], refs[-1 - out_parts : -1], refs[-1]
    step = out.shape[0] // max(out_parts, 1)
    for i, first in enumerate(range(0, out.shape[0], step)):
        rows = pl.ds(first, step)
        total = whole[0][rows, :].astype(jnp.float32)
        for ref in whole[1:]:
            total = total + ref[rows, :].astype(jnp.float32)
        if out_parts:
            total = total + parts[i][...].astype(jnp.float32)
        out[rows, :] = total.astype(jnp.bfloat16)


def add_up(whole, parts=()):
    terms = [*whole, *parts]
    size = whole[0].size
    return pl.pallas_call(
        functools.partial(add_kernel, len(parts)),
        out_shape=jax.ShapeDtypeStruct(whole[0].shape, jnp.bfloat16),
        in_specs=[VMEM] * len(terms),
        out_specs=VMEM,
        compiler_params=params(6),
        cost_estimate=cost(size * len(terms), 4 * size * len(terms)),
        name="add_up",
    )(*terms)


def feed_forward(pieces, *arrays):
    w_down = arrays[-1]
    if lax.axis_size("tp") != 4:
        hidden, kept = hidden_of(pieces, *arrays, 0, 1)
        share = lax.psum_scatter(
            dot_f32(hidden, w_down).astype(jnp.bfloat16), "tp", scatter_dimension=1, tiled=True
        )
        return add_up([kept, share]), hidden
    parts = 2
    outs = [hidden_of(pieces, *arrays, part, parts) for part in range(parts)]
    hidden, kept, through = zip(*outs)
    through = [tp_xor(part, 1) for part in through]
    far, near, own = down_blocks(hidden, kept, w_down)
    joined = [add_up([part, other]) for part, other in zip(far, through)]
    near = tp_xor(near, 1)
    far = [tp_xor(part, 2) for part in joined]
    return add_up([own, near], far), joined[-1]


def per_device(
    tokens,
    variate,
    positions,
    lengths,
    page_table,
    gain_attn,
    w_query,
    w_key,
    w_value,
    var_bias,
    w_out,
    gain_ffn,
    w_gate,
    w_up,
    w_down,
):
    rows = tokens.shape[0]
    width = w_query.shape[1]
    heads = width // HD
    reach = lax.axis_size("seq") // 2

    pieces = gather_pieces(tokens, 2)
    cosine, sine, extra, marks = tables(lengths, var_bias, positions, variate, width)
    pieces, w_out = lax.optimization_barrier((pieces, w_out))
    w_out_all = lax.all_gather(w_out, "tp", axis=0, tiled=True)
    token_rows, queries, pairs = project(
        pieces, gain_attn, w_query, w_key, w_value, cosine, sine, extra
    )
    row_pieces = seq_pieces(pairs)
    attended = attend(lengths, queries, marks, row_pieces, heads, reach)
    attended_pieces = turn_gather(attended)
    large = (token_rows, gain_ffn, w_out_all, w_gate, w_up, w_down)
    large = lax.optimization_barrier((large, attended))[0]
    mixed, joined = feed_forward(attended_pieces, *fetch(large))
    row_pieces, _ = lax.optimization_barrier((row_pieces, joined))
    cache = fill_cache(lengths, page_table, row_pieces, rows)
    return (mixed, cache)


def solution(mesh):
    placed = (
        P("seq", "tp"),
        P("seq"),
        P("seq"),
        P(),
        P(),
        P(),
        P(None, "tp"),
        P(None, "tp"),
        P(None, "tp"),
        P(None, "tp"),
        P("tp", None),
        P(),
        P(None, "tp"),
        P(None, "tp"),
        P("tp", None),
    )
    return jax.shard_map(
        per_device,
        mesh=mesh,
        in_specs=placed,
        out_specs=(P("seq", "tp"), P("seq", None, "tp")),
        check_vma=False,
    )
```

```python
import functools

import jax
import jax.numpy as jnp
import numpy as np
from jax import lax
from jax.experimental import pallas as pl
from jax.experimental.pallas import tpu as pltpu
from jax.sharding import PartitionSpec as P

HD = 64
PAGE = 64
VARS = 4
BIAS_PARTS = 3
LANES = 128
HIDDEN_SCORE = -1e30
EPS = 1e-06

VMEM = pl.BlockSpec(memory_space=pltpu.VMEM)
SMEM = pl.BlockSpec(memory_space=pltpu.SMEM)
ANY = pl.BlockSpec(memory_space=pl.ANY)
HBM = pl.BlockSpec(memory_space=pltpu.HBM)


def params(mib):
    return pltpu.CompilerParams(vmem_limit_bytes=mib << 20)


def cost(flops, nbytes, exps=0):
    return pl.CostEstimate(flops=flops, bytes_accessed=nbytes, transcendentals=exps)


def round_up(amount, unit):
    return (amount + unit - 1) // unit * unit


def dot_f32(left, right):
    return jnp.dot(left, right, preferred_element_type=jnp.float32)


def start_loads(sources, targets, sems):
    loads = [
        pltpu.make_async_copy(source, target, sems.at[i])
        for i, (source, target) in enumerate(zip(sources, targets))
    ]
    for load in loads:
        load.start()
    return loads


def finish_loads(loads):
    for load in loads:
        load.wait()


def tp_xor(value, mask):
    return lax.ppermute(value, "tp", [(i, i ^ mask) for i in range(lax.axis_size("tp"))])


def pair_gather(shard, parts, first=None):
    step = shard.shape[0] // parts
    split = [shard]
    if parts > 1:
        split = [shard[i * step : (i + 1) * step] for i in range(parts)]
        split, shard = lax.optimization_barrier((split, shard))
    far = [tp_xor(part, 2) for part in split]
    near = tp_xor(shard, 1)
    if first is not None:
        far[0], _ = lax.optimization_barrier((far[0], first))
    return [shard, near] + far + [tp_xor(part, 1) for part in far]


def turn_gather(shard):
    count = lax.axis_size("tp")
    pairs = [[(i, (i + turn) % count) for i in range(count)] for turn in range(1, count)]
    return [shard] + [lax.ppermute(shard, "tp", each) for each in pairs]


def gather_pieces(shard, parts, first=None):
    if lax.axis_size("tp") == 4:
        return pair_gather(shard, parts, first)
    return turn_gather(shard)


def assemble(pieces, place, count, target):
    width = pieces[0].shape[1]

    def put(block, value, first=0):
        columns = pl.ds(pl.multiple_of(block * width, width), width)
        target[pl.ds(first, value.shape[0]), columns] = value

    if count != 4:
        for turn, piece in enumerate(pieces):
            put(lax.rem(place + count - turn, count), piece[...])
        return
    put(place, pieces[0][...])
    put(place ^ 1, pieces[1][...])
    parts = (len(pieces) - 2) // 2
    for i in range(parts):
        first = i * (target.shape[0] // parts)
        put(place ^ 2, pieces[2 + i][...], first)
        put(place ^ 3, pieces[2 + parts + i][...], first)


def request_bounds(lengths):
    starts, ends, total = [], [], 0
    for r in range(lengths.shape[0]):
        starts.append(total)
        total = total + lengths[r]
        ends.append(total)
    return starts, ends


def segments_of(index, ends):
    segment = jnp.zeros_like(index)
    for end in ends:
        segment += (index >= end).astype(jnp.int32)
    return segment


def mark_count(requests):
    return round_up(BIAS_PARTS * VARS + requests, 16)


def tables_kernel(
    lengths, bias, frequency, positions, variate, cosine, sine, extra, marks
):
    rows = positions.shape[1]
    width = cosine.shape[1]
    angles = frequency[...] * positions[...].astype(jnp.float32)
    cos_rows, sin_rows = jnp.cos(angles), jnp.sin(angles)
    copies = width // HD
    cosine[...] = jnp.transpose(jnp.concatenate([cos_rows, cos_rows] * copies, axis=0))
    sine[...] = jnp.transpose(jnp.concatenate([-sin_rows, sin_rows] * copies, axis=0))

    ids = variate[...].astype(jnp.float32)
    row = lax.broadcasted_iota(jnp.int32, extra.shape, 0)
    below = jnp.zeros(extra.shape, jnp.float32)
    for i in range(rows // extra.shape[1]):
        below = jnp.where(row == i, ids[:, i * extra.shape[1] : (i + 1) * extra.shape[1]], below)
    extra[...] = below.astype(jnp.bfloat16)

    requests = lengths.shape[0]
    shape = (mark_count(requests), rows)
    _, ends = request_bounds(lengths)
    me = lax.axis_index("seq")
    index = lax.broadcasted_iota(jnp.int32, shape, 1) + me * rows
    mark = lax.broadcasted_iota(jnp.int32, shape, 0)
    request = mark - BIAS_PARTS * VARS
    other = (segments_of(index, ends) != request) & (request >= 0) & (request < requests)
    same = (mark % VARS).astype(jnp.float32) == ids
    part = mark // VARS
    for h in range(marks.shape[0]):
        value = jnp.where(same, bias[0, h], bias[1, h])
        high = value.astype(jnp.bfloat16).astype(jnp.float32)
        middle = (value - high).astype(jnp.bfloat16).astype(jnp.float32)
        low = value - high - middle
        column = jnp.where(part == 0, high, jnp.where(part == 1, middle, low))
        column = jnp.where(part < BIAS_PARTS, column, 0.0)
        column = jnp.where(other, HIDDEN_SCORE, column)
        rest = jnp.zeros((LANES - shape[0], rows), jnp.float32)
        marks[h] = jnp.transpose(jnp.concatenate([column, rest], axis=0)).astype(jnp.bfloat16)


def tables(lengths, bias, positions, variate, width):
    rows = positions.shape[0]
    half = HD // 2
    heads = width // HD
    frequency = 10000.0 ** (-np.arange(half, dtype=np.float32) / np.float32(half))
    extra = round_up(rows // (2 * width), 16)
    return pl.pallas_call(
        tables_kernel,
        out_shape=[
            jax.ShapeDtypeStruct((rows, width), jnp.float32),
            jax.ShapeDtypeStruct((rows, width), jnp.float32),
            jax.ShapeDtypeStruct((extra, 2 * width), jnp.bfloat16),
            jax.ShapeDtypeStruct((heads, rows, LANES), jnp.bfloat16),
        ],
        in_specs=[SMEM, SMEM, VMEM, VMEM, VMEM],
        out_specs=[VMEM] * 4,
        compiler_params=params(4),
        cost_estimate=cost(rows * 1024, 1 << 20, rows * 64),
        name="tables",
    )(
        lengths,
        bias,
        jnp.asarray(frequency.astype(np.float32).reshape(half, 1)),
        positions.reshape(1, rows),
        variate.reshape(1, rows),
    )


def rotate_lanes(vectors, cosine, signed_sine):
    lane = lax.broadcasted_iota(jnp.int32, vectors.shape, 1)
    half = HD // 2
    ahead = pltpu.roll(vectors, vectors.shape[1] - half, 1)
    behind = pltpu.roll(vectors, half, 1)
    partner = jnp.where(lane % HD < half, ahead, behind)
    return vectors * cosine + partner * signed_sine


def norm_rows(values, gain):
    scale = lax.rsqrt(jnp.mean(values * values, axis=-1, keepdims=True) + EPS)
    return (values * scale * gain).astype(jnp.bfloat16)


def project_kernel(places, count, *refs):
    pieces = refs[:count]
    gain, w_q, w_k, w_v, cosine, sine, extra, tokens_out, queries, pairs = refs[count:-2]
    tokens, sem = refs[-2:]
    pairs[tokens.shape[0] :, :] = extra[...]
    assemble(pieces, lax.axis_index("tp"), places, tokens)
    keep = pltpu.make_async_copy(tokens, tokens_out, sem)
    keep.start()
    rows = tokens.shape[0]
    width = w_q.shape[1]
    step = min(rows, 256)
    gain_row = gain[...].astype(jnp.float32).reshape(1, -1)
    for first in range(0, rows, step):
        part = pl.ds(first, step)
        normed = norm_rows(tokens[part, :].astype(jnp.float32), gain_row)
        cos_part, sin_part = cosine[part, :], sine[part, :]
        query = rotate_lanes(dot_f32(normed, w_q[...]), cos_part, sin_part)
        queries[part, :] = query.astype(jnp.bfloat16) * jnp.bfloat16(HD**-0.5)
        key = rotate_lanes(dot_f32(normed, w_k[...]), cos_part, sin_part)
        pairs[part, :width] = key.astype(jnp.bfloat16)
        pairs[part, width:] = dot_f32(normed, w_v[...]).astype(jnp.bfloat16)
    keep.wait()


def project(pieces, gain, w_query, w_key, w_value, cosine, sine, extra):
    rows, part = pieces[0].shape
    width = w_query.shape[1]
    features = w_query.shape[0]
    return pl.pallas_call(
        functools.partial(project_kernel, lax.axis_size("tp"), len(pieces)),
        out_shape=[
            jax.ShapeDtypeStruct((rows, features), jnp.bfloat16),
            jax.ShapeDtypeStruct((rows, width), jnp.bfloat16),
            jax.ShapeDtypeStruct((rows + extra.shape[0], 2 * width), jnp.bfloat16),
        ],
        in_specs=[VMEM] * (len(pieces) + 7),
        out_specs=[HBM, VMEM, VMEM],
        scratch_shapes=[pltpu.VMEM((rows, features), jnp.bfloat16), pltpu.SemaphoreType.DMA],
        compiler_params=params(5),
        cost_estimate=cost(6 * rows * features * width, 4 << 20),
        name="project",
    )(*pieces, gain, w_query, w_key, w_value, cosine, sine, extra)


def seq_xor(value, mask):
    return lax.ppermute(value, "seq", [(i, i ^ mask) for i in range(lax.axis_size("seq"))])


def seq_pieces(pairs):
    if lax.axis_size("seq") == 8:
        diagonal = seq_xor(pairs, 6)
        across = seq_xor(pairs, 2)
        down = seq_xor(pairs, 4)
        twin = seq_xor(pairs, 1)
        across_twin = seq_xor(across, 1)
        down_twin = seq_xor(down, 1)
        diagonal_twin = seq_xor(diagonal, 1)
        return [pairs, twin, across, across_twin, down, down_twin, diagonal, diagonal_twin]
    return [lax.all_gather(pairs, "seq", axis=0)]


def piece_copies(pieces, me, wanted):
    if len(pieces) > 1:
        for m, piece in enumerate(pieces):
            wanted(piece, me ^ m)
    else:
        for j in range(pieces[0].shape[0]):
            wanted(pieces[0].at[j], j)


def attend_kernel(count, heads, reach, lengths, queries, query_marks, *refs):
    pieces = refs[:count]
    out, q_buf, k_buf, v_buf, extra_buf, scores, peak, total, sems = refs[count:]
    me = lax.axis_index("seq")
    rows = queries.shape[0]
    _, ends = request_bounds(lengths)
    request_start = 0
    for end in ends:
        request_start = jnp.where(end <= me * rows, end, request_start)
    last = me - request_start // rows
    width = queries.shape[1]

    def copies(source, slot):
        return [
            pltpu.make_async_copy(
                source.at[pl.ds(0, rows), pl.ds(0, width)],
                k_buf.at[slot, :, pl.ds(0, width)],
                sems.at[slot, 0],
            ),
            pltpu.make_async_copy(
                source.at[pl.ds(0, rows), pl.ds(width, width)],
                v_buf.at[slot, :, pl.ds(0, width)],
                sems.at[slot, 1],
            ),
            pltpu.make_async_copy(
                source.at[pl.ds(rows, extra_buf.shape[1]), :], extra_buf.at[slot], sems.at[slot, 2]
            ),
        ]

    def begin(source, block):
        distance = me - block

        @pl.when((distance >= 0) & (distance <= last))
        def _():
            for copy in copies(source, distance):
                copy.start()

    piece_copies(pieces, me, begin)
    example = pieces[0] if count > 1 else pieces[0].at[0]

    marks = mark_count(lengths.shape[0])

    def finish(slot):
        for copy in copies(example, slot):
            copy.wait()
        extra = extra_buf[slot].astype(jnp.float32)
        pair_width = extra.shape[1]
        variates = jnp.concatenate([extra[i : i + 1] for i in range(rows // pair_width)], axis=1)
        mark = lax.broadcasted_iota(jnp.int32, (marks, rows), 0)
        key = lax.broadcasted_iota(jnp.int32, (marks, rows), 1) + (me - slot) * rows
        segment = segments_of(key, ends)
        same_variate = (mark % VARS).astype(jnp.float32) == variates
        same_segment = mark - BIAS_PARTS * VARS == segment
        marked = (same_variate & (mark < BIAS_PARTS * VARS)) | (
            same_segment & (mark >= BIAS_PARTS * VARS)
        )
        columns = jnp.transpose(jnp.where(marked, 1.0, 0.0))
        k_buf[slot, :, width : width + marks] = columns.astype(jnp.bfloat16)

    lane = lax.broadcasted_iota(jnp.int32, (rows, width), 1)
    for h in range(heads):
        part = pl.ds(h * rows, rows)
        q_buf[part, :width] = jnp.where(lane // HD == h, queries[...], jnp.bfloat16(0))
        q_buf[part, width:] = query_marks[h]
    for slot in range(reach + 1):
        v_buf[slot, :, width:] = jnp.ones((rows, LANES), jnp.bfloat16)
        k_buf[slot, :, width:] = jnp.zeros((rows, LANES), jnp.bfloat16)

    def narrow(tile):
        best = tile[:, :LANES]
        for first in range(LANES, rows, LANES):
            best = jnp.maximum(best, tile[:, first : first + LANES])
        return best

    def score(h, slot):
        return lax.dot_general(
            q_buf[pl.ds(h * rows, rows), :],
            k_buf[slot],
            (((1,), (1,)), ((), ())),
            preferred_element_type=jnp.float32,
        )

    finish(0)
    q_at = lax.broadcasted_iota(jnp.int32, (rows, rows), 0)
    k_at = lax.broadcasted_iota(jnp.int32, (rows, rows), 1)
    for h in range(heads):
        tile = jnp.where(k_at <= q_at, score(h, 0), HIDDEN_SCORE)
        scores[h, 0] = tile
        peak[h] = narrow(tile)

    def first_pass(slot, carry):
        finish(slot)
        for h in range(heads):
            tile = score(h, slot)
            scores[h, slot] = tile
            peak[h] = jnp.maximum(peak[h], narrow(tile))
        return carry

    lax.fori_loop(1, last + 1, first_pass, 0)
    for h in range(heads):
        best = jnp.max(peak[h], axis=1, keepdims=True)
        peak[h] = jnp.broadcast_to(best, (rows, LANES))
        total[h] = jnp.zeros_like(total[h])

    def second_pass(slot, carry):
        for h in range(heads):
            best = peak[h]
            wide = jnp.concatenate([best] * (rows // LANES), axis=1)
            weight = jnp.exp(scores[h, slot] - wide).astype(jnp.bfloat16)
            total[h] += dot_f32(weight, v_buf[slot])
        return carry

    lax.fori_loop(0, last + 1, second_pass, 0)
    result = total[0, :, :width] / total[0, :, width:]
    for h in range(1, heads):
        result = jnp.where(lane // HD == h, total[h, :, :width] / total[h, :, width:], result)
    out[...] = result.astype(jnp.bfloat16)


def attend(lengths, queries, query_marks, pieces, heads, reach):
    rows, width = queries.shape
    slots = reach + 1
    return pl.pallas_call(
        functools.partial(attend_kernel, len(pieces), heads, reach),
        out_shape=jax.ShapeDtypeStruct((rows, width), jnp.bfloat16),
        in_specs=[SMEM, VMEM, VMEM] + [ANY] * len(pieces),
        out_specs=VMEM,
        scratch_shapes=[
            pltpu.VMEM((heads * rows, width + LANES), jnp.bfloat16),
            pltpu.VMEM((slots, rows, width + LANES), jnp.bfloat16),
            pltpu.VMEM((slots, rows, width + LANES), jnp.bfloat16),
            pltpu.VMEM((slots, pieces[0].shape[-2] - rows, pieces[0].shape[-1]), jnp.bfloat16),
            pltpu.VMEM((heads, slots, rows, rows), jnp.float32),
            pltpu.VMEM((heads, rows, LANES), jnp.float32),
            pltpu.VMEM((heads, rows, width + LANES), jnp.float32),
            pltpu.SemaphoreType.DMA((slots, 3)),
        ],
        compiler_params=params(8 + 2 * slots),
        cost_estimate=cost(
            4 * heads * rows * rows * slots * 256, 4 << 20, heads * rows * rows * slots
        ),
        name="attend",
    )(lengths, queries, query_marks, *pieces)


def cache_kernel(count, window, lengths, page_table, *refs):
    pieces = refs[:count]
    out, rows_buf, logical, sems = refs[count:]
    rows = rows_buf.shape[1]
    blocks = rows_buf.shape[0]
    width = out.shape[2]
    pages = out.shape[0] // PAGE
    me = lax.axis_index("seq")
    started = []

    def begin(source, block):
        copy = pltpu.make_async_copy(
            source.at[pl.ds(0, rows), :], rows_buf.at[block], sems.at[len(started)]
        )
        copy.start()
        started.append(copy)

    piece_copies(pieces, me, begin)

    def place_page(page, carry):
        local = page_table[page] - me * pages

        @pl.when((local >= 0) & (local < pages))
        def _():
            logical[local] = page

        return carry

    lax.fori_loop(0, page_table.shape[0], place_page, 0)
    starts, _ = request_bounds(lengths)
    for copy in started:
        copy.wait()
    row = lax.broadcasted_iota(jnp.int32, (PAGE, window), 0)
    column = lax.broadcasted_iota(jnp.int32, (PAGE, window), 1)

    def one_page(page, carry):
        first, amount, base = 0, 0, 0
        for r, start in enumerate(starts):
            count_r = (lengths[r] + PAGE - 1) // PAGE
            ahead = (logical[page] - base) * PAGE
            within = (ahead >= 0) & (ahead < lengths[r])
            first = jnp.where(within, start + ahead, first)
            amount = jnp.where(within, jnp.minimum(lengths[r] - ahead, PAGE), amount)
            base = base + count_r
        block = first // rows
        total = None
        for ahead in range(2):
            at = jnp.minimum(block + ahead, blocks - 1)
            inside = first - block * rows
            if ahead == 0:
                start = jnp.minimum(inside // 16 * 16, rows - window)
                offset = inside - start
            else:
                start = 0
                offset = inside - rows
            wanted = (row + offset == column) & (row < amount)
            if ahead == 1:
                wanted = wanted & (block + 1 < blocks)
            chooser = jnp.where(wanted, 1.0, 0.0).astype(jnp.bfloat16)
            found = dot_f32(chooser, rows_buf[at, pl.ds(pl.multiple_of(start, 16), window), :])
            total = found if total is None else total + found
        part = pl.ds(pl.multiple_of(page * PAGE, PAGE), PAGE)
        out[part, 0, :] = total[:, :width].astype(jnp.bfloat16)
        out[part, 1, :] = total[:, width:].astype(jnp.bfloat16)
        return carry

    lax.fori_loop(0, pages, one_page, 0)


def fill_cache(lengths, page_table, pieces, rows):
    width = pieces[0].shape[-1]
    blocks = lax.axis_size("seq")
    pages = page_table.shape[0] // blocks
    return pl.pallas_call(
        functools.partial(cache_kernel, len(pieces), 2 * PAGE),
        out_shape=jax.ShapeDtypeStruct((pages * PAGE, 2, width // 2), jnp.bfloat16),
        in_specs=[SMEM] * 2 + [ANY] * len(pieces),
        out_specs=VMEM,
        scratch_shapes=[
            pltpu.VMEM((blocks, rows, width), jnp.bfloat16),
            pltpu.SMEM((pages,), jnp.int32),
            pltpu.SemaphoreType.DMA((blocks,)),
        ],
        compiler_params=params(8),
        cost_estimate=cost(4 * pages * PAGE * 2 * PAGE * width, 3 << 20),
        name="fill_cache",
    )(lengths, page_table, *pieces)


def fetch_kernel(count, *refs):
    finish_loads(start_loads(refs[:count], refs[count:-1], refs[-1]))


def fetch(arrays):
    return pl.pallas_call(
        functools.partial(fetch_kernel, len(arrays)),
        out_shape=[jax.ShapeDtypeStruct(array.shape, array.dtype) for array in arrays],
        in_specs=[HBM] * len(arrays),
        out_specs=[VMEM] * len(arrays),
        scratch_shapes=[pltpu.SemaphoreType.DMA((len(arrays),))],
        compiler_params=params(10),
        cost_estimate=cost(0, 4 * sum(array.size for array in arrays)),
        name="fetch",
    )(*arrays)


def hidden_kernel(places, *refs):
    pieces, w_out_pieces = refs[:places], refs[places : 2 * places]
    tokens, gain, w_gate, w_up, w_down = refs[2 * places : 2 * places + 5]
    outs, attended, w_out = refs[2 * places + 5 : -2], refs[-2], refs[-1]
    hidden, kept = outs[:2]
    place = lax.axis_index("tp")
    each = pieces[0].shape[1]
    for i in range(places):
        attended[:, i * each : (i + 1) * each] = pieces[i][...]
        w_out[i * each : (i + 1) * each, :] = w_out_pieces[i][...]
    rows, features = tokens.shape
    width = kept.shape[1]
    step = min(rows, 256)
    gain_row = gain[...].astype(jnp.float32).reshape(1, -1)
    for first in range(0, rows, step):
        part = pl.ds(first, step)
        projected = dot_f32(attended[part, :], w_out[...])
        residual = (tokens[part, :].astype(jnp.float32) + projected).astype(jnp.bfloat16)
        mine = residual[:, :width]
        for i in range(1, places):
            mine = jnp.where(place == i, residual[:, i * width : (i + 1) * width], mine)
        kept[part, :] = mine
        normed = norm_rows(residual.astype(jnp.float32), gain_row)
        gate = dot_f32(normed, w_gate[...])
        up = dot_f32(normed, w_up[...])
        hidden[part, :] = (jax.nn.silu(gate) * up).astype(jnp.bfloat16)
    if len(outs) == 2:
        return
    weights = w_down[:, pl.ds(pl.multiple_of((place ^ 3) * width, width), width)]
    through = dot_f32(hidden[...], weights).astype(jnp.bfloat16)
    outs[2][...] = through[: rows // 2]
    outs[3][...] = through[rows // 2 :]


def hidden_of(pieces, w_out_pieces, tokens, gain, w_gate, w_up, w_down):
    rows, features = tokens.shape
    places = lax.axis_size("tp")
    width = features // places
    units = w_gate.shape[1]
    inner = places * pieces[0].shape[1]
    shapes = [(rows, units), (rows, width)] + [(rows // 2, width)] * (2 * (places == 4))
    return pl.pallas_call(
        functools.partial(hidden_kernel, places),
        out_shape=[jax.ShapeDtypeStruct(shape, jnp.bfloat16) for shape in shapes],
        in_specs=[VMEM] * (2 * places + 5),
        out_specs=[VMEM] * len(shapes),
        scratch_shapes=[
            pltpu.VMEM((rows, inner), jnp.bfloat16),
            pltpu.VMEM((inner, features), jnp.bfloat16),
        ],
        compiler_params=params(12),
        cost_estimate=cost(6 * rows * features * units, 10 << 20),
        name="hidden",
    )(*pieces, *w_out_pieces, tokens, gain, w_gate, w_up, w_down)


def down_kernel(hidden, kept, w_down, far_top, far_low, near, own):
    place = lax.axis_index("tp")
    rows, width = own.shape

    def product(index):
        weights = w_down[:, pl.ds(pl.multiple_of(index * width, width), width)]
        return dot_f32(hidden[...], weights)

    far = product(place ^ 2)
    far_top[...] = far[: rows // 2]
    far_low[...] = far[rows // 2 :]
    near[...] = product(place ^ 1).astype(jnp.bfloat16)
    own[...] = product(place) + kept[...].astype(jnp.float32)


def down_blocks(hidden, kept, w_down):
    rows, width = kept.shape
    shapes = [((rows // 2, width), jnp.float32)] * 2
    shapes += [((rows, width), jnp.bfloat16), ((rows, width), jnp.float32)]
    return pl.pallas_call(
        down_kernel,
        out_shape=[jax.ShapeDtypeStruct(*shape) for shape in shapes],
        in_specs=[VMEM] * 3,
        out_specs=[VMEM] * 4,
        compiler_params=params(6),
        cost_estimate=cost(2 * rows * w_down.shape[0] * width * 3, 5 << 20),
        name="down_blocks",
    )(hidden, kept, w_down)


def add_kernel(out_parts, *refs):
    whole, parts, out = refs[: -1 - out_parts], refs[-1 - out_parts : -1], refs[-1]
    step = out.shape[0] // max(out_parts, 1)
    for i, first in enumerate(range(0, out.shape[0], step)):
        rows = pl.ds(first, step)
        total = whole[0][rows, :].astype(jnp.float32)
        for ref in whole[1:]:
            total = total + ref[rows, :].astype(jnp.float32)
        if out_parts:
            total = total + parts[i][...].astype(jnp.float32)
        out[rows, :] = total.astype(jnp.bfloat16)


def add_up(whole, parts=()):
    terms = [*whole, *parts]
    size = whole[0].size
    return pl.pallas_call(
        functools.partial(add_kernel, len(parts)),
        out_shape=jax.ShapeDtypeStruct(whole[0].shape, jnp.bfloat16),
        in_specs=[VMEM] * len(terms),
        out_specs=VMEM,
        compiler_params=params(6),
        cost_estimate=cost(size * len(terms), 4 * size * len(terms)),
        name="add_up",
    )(*terms)


def feed_forward(pieces, w_out_pieces, *arrays):
    hidden, kept, *through = hidden_of(pieces, w_out_pieces, *arrays)
    w_down = arrays[-1]
    if lax.axis_size("tp") != 4:
        share = lax.psum_scatter(
            dot_f32(hidden, w_down).astype(jnp.bfloat16), "tp", scatter_dimension=1, tiled=True
        )
        return add_up([kept, share]), hidden
    through = [tp_xor(part, 1) for part in through]
    far_top, far_low, near, own = down_blocks(hidden, kept, w_down)
    joined = [add_up([part, other]) for part, other in zip((far_top, far_low), through)]
    near = tp_xor(near, 1)
    far = [tp_xor(part, 2) for part in joined]
    return add_up([own, near], far), joined[-1]


def per_device(
    tokens,
    variate,
    positions,
    lengths,
    page_table,
    gain_attn,
    w_query,
    w_key,
    w_value,
    var_bias,
    w_out,
    gain_ffn,
    w_gate,
    w_up,
    w_down,
):
    rows = tokens.shape[0]
    width = w_query.shape[1]
    heads = width // HD
    reach = lax.axis_size("seq") // 2

    cosine, sine, extra, marks = tables(lengths, var_bias, positions, variate, width)
    pieces = gather_pieces(tokens, 2, extra)
    token_rows, queries, pairs = project(
        pieces, gain_attn, w_query, w_key, w_value, cosine, sine, extra
    )
    w_out, _ = lax.optimization_barrier((w_out, pairs))
    row_pieces = seq_pieces(pairs)
    w_out_pieces = gather_pieces(w_out, 1)
    attended = attend(lengths, queries, marks, row_pieces, heads, reach)
    large = (token_rows, gain_ffn, w_gate, w_up, w_down)
    large = lax.optimization_barrier((large, attended))[0]
    large = fetch(large)
    attended_pieces = gather_pieces(attended, 1, large[1])
    mixed, joined = feed_forward(attended_pieces, w_out_pieces, *large)
    row_pieces, _ = lax.optimization_barrier((row_pieces, joined))
    cache = fill_cache(lengths, page_table, row_pieces, rows)
    return (mixed, cache)


def solution(mesh):
    placed = (
        P("seq", "tp"),
        P("seq"),
        P("seq"),
        P(),
        P(),
        P(),
        P(None, "tp"),
        P(None, "tp"),
        P(None, "tp"),
        P(None, "tp"),
        P("tp", None),
        P(),
        P(None, "tp"),
        P(None, "tp"),
        P("tp", None),
    )
    return jax.shard_map(
        per_device,
        mesh=mesh,
        in_specs=placed,
        out_specs=(P("seq", "tp"), P("seq", None, "tp")),
        check_vma=False,
    )
```

```python
import functools

import jax
import jax.numpy as jnp
import numpy as np
from jax import lax
from jax.experimental import pallas as pl
from jax.experimental.pallas import tpu as pltpu
from jax.sharding import PartitionSpec as P

HD = 64
PAGE = 64
VARS = 4
BIAS_PARTS = 3
LANES = 128
HIDDEN_SCORE = -1e30
EPS = 1e-06

VMEM = pl.BlockSpec(memory_space=pltpu.VMEM)
SMEM = pl.BlockSpec(memory_space=pltpu.SMEM)
ANY = pl.BlockSpec(memory_space=pl.ANY)
HBM = pl.BlockSpec(memory_space=pltpu.HBM)


def params(mib):
    return pltpu.CompilerParams(vmem_limit_bytes=mib << 20)


def cost(flops, nbytes, exps=0):
    return pl.CostEstimate(flops=flops, bytes_accessed=nbytes, transcendentals=exps)


def round_up(amount, unit):
    return (amount + unit - 1) // unit * unit


def dot_f32(left, right):
    return jnp.dot(left, right, preferred_element_type=jnp.float32)


def start_loads(sources, targets, sems):
    loads = [
        pltpu.make_async_copy(source, target, sems.at[i])
        for i, (source, target) in enumerate(zip(sources, targets))
    ]
    for load in loads:
        load.start()
    return loads


def finish_loads(loads):
    for load in loads:
        load.wait()


def tp_xor(value, mask):
    return lax.ppermute(value, "tp", [(i, i ^ mask) for i in range(lax.axis_size("tp"))])


def pair_gather(shard, parts, first=None):
    step = shard.shape[0] // parts
    split = [shard]
    if parts > 1:
        split = [shard[i * step : (i + 1) * step] for i in range(parts)]
        split, shard = lax.optimization_barrier((split, shard))
    far = [tp_xor(part, 2) for part in split]
    near = tp_xor(shard, 1)
    if first is not None:
        far[0], _ = lax.optimization_barrier((far[0], first))
    return [shard, near] + far + [tp_xor(part, 1) for part in far]


def turn_gather(shard):
    count = lax.axis_size("tp")
    pairs = [[(i, (i + turn) % count) for i in range(count)] for turn in range(1, count)]
    return [shard] + [lax.ppermute(shard, "tp", each) for each in pairs]


def gather_pieces(shard, parts, first=None):
    if lax.axis_size("tp") == 4:
        return pair_gather(shard, parts, first)
    return turn_gather(shard)


def assemble(pieces, place, count, target):
    width = pieces[0].shape[1]

    def put(block, value, first=0):
        columns = pl.ds(pl.multiple_of(block * width, width), width)
        target[pl.ds(first, value.shape[0]), columns] = value

    if count != 4:
        for turn, piece in enumerate(pieces):
            put(lax.rem(place + count - turn, count), piece[...])
        return
    put(place, pieces[0][...])
    put(place ^ 1, pieces[1][...])
    parts = (len(pieces) - 2) // 2
    for i in range(parts):
        first = i * (target.shape[0] // parts)
        put(place ^ 2, pieces[2 + i][...], first)
        put(place ^ 3, pieces[2 + parts + i][...], first)


def request_bounds(lengths):
    starts, ends, total = [], [], 0
    for r in range(lengths.shape[0]):
        starts.append(total)
        total = total + lengths[r]
        ends.append(total)
    return starts, ends


def segments_of(index, ends):
    segment = jnp.zeros_like(index)
    for end in ends:
        segment += (index >= end).astype(jnp.int32)
    return segment


def mark_count(requests):
    return round_up(BIAS_PARTS * VARS + requests, 16)


def tables_kernel(count, lengths, bias, frequency, positions, variate, *refs):
    cosine, sine, extra, marks = refs[count : count + 4]
    sources, targets, sems = list(refs[:count]), refs[count + 4 : -1], refs[-1]
    if targets[-1].shape != sources[-1].shape:
        half = targets[-1].shape[1]
        columns = pl.ds(pl.multiple_of(lax.rem(lax.axis_index("seq"), 2) * half, half), half)
        sources[-1] = sources[-1].at[:, columns]
    loads = start_loads(sources, targets, sems)
    rows = positions.shape[1]
    width = cosine.shape[1]
    angles = frequency[...] * positions[...].astype(jnp.float32)
    cos_rows, sin_rows = jnp.cos(angles), jnp.sin(angles)
    copies = width // HD
    cosine[...] = jnp.transpose(jnp.concatenate([cos_rows, cos_rows] * copies, axis=0))
    sine[...] = jnp.transpose(jnp.concatenate([-sin_rows, sin_rows] * copies, axis=0))

    ids = variate[...].astype(jnp.float32)
    row = lax.broadcasted_iota(jnp.int32, extra.shape, 0)
    below = jnp.zeros(extra.shape, jnp.float32)
    for i in range(rows // extra.shape[1]):
        below = jnp.where(row == i, ids[:, i * extra.shape[1] : (i + 1) * extra.shape[1]], below)
    extra[...] = below.astype(jnp.bfloat16)

    requests = lengths.shape[0]
    shape = (mark_count(requests), rows)
    _, ends = request_bounds(lengths)
    me = lax.axis_index("seq")
    index = lax.broadcasted_iota(jnp.int32, shape, 1) + me * rows
    mark = lax.broadcasted_iota(jnp.int32, shape, 0)
    request = mark - BIAS_PARTS * VARS
    other = (segments_of(index, ends) != request) & (request >= 0) & (request < requests)
    same = (mark % VARS).astype(jnp.float32) == ids
    part = mark // VARS
    for h in range(marks.shape[0]):
        value = jnp.where(same, bias[0, h], bias[1, h])
        high = value.astype(jnp.bfloat16).astype(jnp.float32)
        middle = (value - high).astype(jnp.bfloat16).astype(jnp.float32)
        low = value - high - middle
        column = jnp.where(part == 0, high, jnp.where(part == 1, middle, low))
        column = jnp.where(part < BIAS_PARTS, column, 0.0)
        column = jnp.where(other, HIDDEN_SCORE, column)
        rest = jnp.zeros((LANES - shape[0], rows), jnp.float32)
        marks[h] = jnp.transpose(jnp.concatenate([column, rest], axis=0)).astype(jnp.bfloat16)
    finish_loads(loads)


def tables(lengths, bias, positions, variate, width, arrays, halve):
    rows = positions.shape[0]
    half = HD // 2
    heads = width // HD
    frequency = 10000.0 ** (-np.arange(half, dtype=np.float32) / np.float32(half))
    extra = round_up(rows // (2 * width), 16)
    kept = [array.shape for array in arrays]
    if halve:
        kept[-1] = (kept[-1][0], kept[-1][1] // 2)
    return pl.pallas_call(
        functools.partial(tables_kernel, len(arrays)),
        out_shape=[
            jax.ShapeDtypeStruct((rows, width), jnp.float32),
            jax.ShapeDtypeStruct((rows, width), jnp.float32),
            jax.ShapeDtypeStruct((extra, 2 * width), jnp.bfloat16),
            jax.ShapeDtypeStruct((heads, rows, LANES), jnp.bfloat16),
        ]
        + [jax.ShapeDtypeStruct(shape, array.dtype) for shape, array in zip(kept, arrays)],
        in_specs=[SMEM, SMEM, VMEM, VMEM, VMEM] + [ANY] * len(arrays),
        out_specs=[VMEM] * (4 + len(arrays)),
        scratch_shapes=[pltpu.SemaphoreType.DMA((len(arrays),))],
        compiler_params=params(6),
        cost_estimate=cost(rows * 1024, 1 << 20, rows * 64),
        name="tables",
    )(
        lengths,
        bias,
        jnp.asarray(frequency.astype(np.float32).reshape(half, 1)),
        positions.reshape(1, rows),
        variate.reshape(1, rows),
        *arrays,
    )


def rotate_lanes(vectors, cosine, signed_sine):
    lane = lax.broadcasted_iota(jnp.int32, vectors.shape, 1)
    half = HD // 2
    ahead = pltpu.roll(vectors, vectors.shape[1] - half, 1)
    behind = pltpu.roll(vectors, half, 1)
    partner = jnp.where(lane % HD < half, ahead, behind)
    return vectors * cosine + partner * signed_sine


def norm_rows(values, gain):
    scale = lax.rsqrt(jnp.mean(values * values, axis=-1, keepdims=True) + EPS)
    return (values * scale * gain).astype(jnp.bfloat16)


def project_kernel(places, count, *refs):
    pieces = refs[:count]
    gain, w_q, w_k, w_v, cosine, sine, extra, tokens_out, queries, pairs = refs[count:-2]
    tokens, sem = refs[-2:]
    pairs[tokens.shape[0] :, :] = extra[...]
    assemble(pieces, lax.axis_index("tp"), places, tokens)
    keep = pltpu.make_async_copy(tokens, tokens_out, sem)
    keep.start()
    rows = tokens.shape[0]
    width = w_q.shape[1]
    step = min(rows, 256)
    gain_row = gain[...].astype(jnp.float32).reshape(1, -1)
    for first in range(0, rows, step):
        part = pl.ds(first, step)
        normed = norm_rows(tokens[part, :].astype(jnp.float32), gain_row)
        cos_part, sin_part = cosine[part, :], sine[part, :]
        query = rotate_lanes(dot_f32(normed, w_q[...]), cos_part, sin_part)
        queries[part, :] = query.astype(jnp.bfloat16) * jnp.bfloat16(HD**-0.5)
        key = rotate_lanes(dot_f32(normed, w_k[...]), cos_part, sin_part)
        pairs[part, :width] = key.astype(jnp.bfloat16)
        pairs[part, width:] = dot_f32(normed, w_v[...]).astype(jnp.bfloat16)
    keep.wait()


def project(pieces, gain, w_query, w_key, w_value, cosine, sine, extra):
    rows, part = pieces[0].shape
    width = w_query.shape[1]
    features = w_query.shape[0]
    return pl.pallas_call(
        functools.partial(project_kernel, lax.axis_size("tp"), len(pieces)),
        out_shape=[
            jax.ShapeDtypeStruct((rows, features), jnp.bfloat16),
            jax.ShapeDtypeStruct((rows, width), jnp.bfloat16),
            jax.ShapeDtypeStruct((rows + extra.shape[0], 2 * width), jnp.bfloat16),
        ],
        in_specs=[VMEM] * (len(pieces) + 7),
        out_specs=[HBM, VMEM, VMEM],
        scratch_shapes=[pltpu.VMEM((rows, features), jnp.bfloat16), pltpu.SemaphoreType.DMA],
        compiler_params=params(5),
        cost_estimate=cost(6 * rows * features * width, 4 << 20),
        name="project",
    )(*pieces, gain, w_query, w_key, w_value, cosine, sine, extra)


def seq_xor(value, mask):
    return lax.ppermute(value, "seq", [(i, i ^ mask) for i in range(lax.axis_size("seq"))])


def seq_pieces(pairs):
    if lax.axis_size("seq") == 8:
        diagonal = seq_xor(pairs, 6)
        across = seq_xor(pairs, 2)
        down = seq_xor(pairs, 4)
        twin = seq_xor(pairs, 1)
        across_twin = seq_xor(across, 1)
        down_twin = seq_xor(down, 1)
        diagonal_twin = seq_xor(diagonal, 1)
        return [pairs, twin, across, across_twin, down, down_twin, diagonal, diagonal_twin]
    return [lax.all_gather(pairs, "seq", axis=0)]


def piece_copies(pieces, me, wanted):
    if len(pieces) > 1:
        for m, piece in enumerate(pieces):
            wanted(piece, me ^ m)
    else:
        for j in range(pieces[0].shape[0]):
            wanted(pieces[0].at[j], j)


def attend_kernel(count, heads, reach, lengths, queries, query_marks, *refs):
    pieces = refs[:count]
    out, q_buf, k_buf, v_buf, extra_buf, scores, peak, total, sems = refs[count:]
    me = lax.axis_index("seq")
    rows = queries.shape[0]
    _, ends = request_bounds(lengths)
    request_start = 0
    for end in ends:
        request_start = jnp.where(end <= me * rows, end, request_start)
    last = me - request_start // rows
    width = queries.shape[1]

    def copies(source, slot):
        return [
            pltpu.make_async_copy(
                source.at[pl.ds(0, rows), pl.ds(0, width)],
                k_buf.at[slot, :, pl.ds(0, width)],
                sems.at[slot, 0],
            ),
            pltpu.make_async_copy(
                source.at[pl.ds(0, rows), pl.ds(width, width)],
                v_buf.at[slot, :, pl.ds(0, width)],
                sems.at[slot, 1],
            ),
            pltpu.make_async_copy(
                source.at[pl.ds(rows, extra_buf.shape[1]), :], extra_buf.at[slot], sems.at[slot, 2]
            ),
        ]

    def begin(source, block):
        distance = me - block

        @pl.when((distance >= 0) & (distance <= last))
        def _():
            for copy in copies(source, distance):
                copy.start()

    piece_copies(pieces, me, begin)
    example = pieces[0] if count > 1 else pieces[0].at[0]

    marks = mark_count(lengths.shape[0])

    def finish(slot):
        for copy in copies(example, slot):
            copy.wait()
        extra = extra_buf[slot].astype(jnp.float32)
        pair_width = extra.shape[1]
        variates = jnp.concatenate([extra[i : i + 1] for i in range(rows // pair_width)], axis=1)
        mark = lax.broadcasted_iota(jnp.int32, (marks, rows), 0)
        key = lax.broadcasted_iota(jnp.int32, (marks, rows), 1) + (me - slot) * rows
        segment = segments_of(key, ends)
        same_variate = (mark % VARS).astype(jnp.float32) == variates
        same_segment = mark - BIAS_PARTS * VARS == segment
        marked = (same_variate & (mark < BIAS_PARTS * VARS)) | (
            same_segment & (mark >= BIAS_PARTS * VARS)
        )
        columns = jnp.transpose(jnp.where(marked, 1.0, 0.0))
        k_buf[slot, :, width : width + marks] = columns.astype(jnp.bfloat16)

    lane = lax.broadcasted_iota(jnp.int32, (rows, width), 1)
    for h in range(heads):
        part = pl.ds(h * rows, rows)
        q_buf[part, :width] = jnp.where(lane // HD == h, queries[...], jnp.bfloat16(0))
        q_buf[part, width:] = query_marks[h]
    for slot in range(reach + 1):
        v_buf[slot, :, width:] = jnp.ones((rows, LANES), jnp.bfloat16)
        k_buf[slot, :, width:] = jnp.zeros((rows, LANES), jnp.bfloat16)

    def narrow(tile):
        best = tile[:, :LANES]
        for first in range(LANES, rows, LANES):
            best = jnp.maximum(best, tile[:, first : first + LANES])
        return best

    def score(h, slot):
        return lax.dot_general(
            q_buf[pl.ds(h * rows, rows), :],
            k_buf[slot],
            (((1,), (1,)), ((), ())),
            preferred_element_type=jnp.float32,
        )

    finish(0)
    q_at = lax.broadcasted_iota(jnp.int32, (rows, rows), 0)
    k_at = lax.broadcasted_iota(jnp.int32, (rows, rows), 1)
    for h in range(heads):
        tile = jnp.where(k_at <= q_at, score(h, 0), HIDDEN_SCORE)
        scores[h, 0] = tile
        peak[h] = narrow(tile)

    def first_pass(slot, carry):
        finish(slot)
        for h in range(heads):
            tile = score(h, slot)
            scores[h, slot] = tile
            peak[h] = jnp.maximum(peak[h], narrow(tile))
        return carry

    lax.fori_loop(1, last + 1, first_pass, 0)
    for h in range(heads):
        best = jnp.max(peak[h], axis=1, keepdims=True)
        peak[h] = jnp.broadcast_to(best, (rows, LANES))
        total[h] = jnp.zeros_like(total[h])

    def second_pass(slot, carry):
        for h in range(heads):
            best = peak[h]
            wide = jnp.concatenate([best] * (rows // LANES), axis=1)
            weight = jnp.exp(scores[h, slot] - wide).astype(jnp.bfloat16)
            total[h] += dot_f32(weight, v_buf[slot])
        return carry

    lax.fori_loop(0, last + 1, second_pass, 0)
    result = total[0, :, :width] / total[0, :, width:]
    for h in range(1, heads):
        result = jnp.where(lane // HD == h, total[h, :, :width] / total[h, :, width:], result)
    out[...] = result.astype(jnp.bfloat16)


def attend(lengths, queries, query_marks, pieces, heads, reach):
    rows, width = queries.shape
    slots = reach + 1
    return pl.pallas_call(
        functools.partial(attend_kernel, len(pieces), heads, reach),
        out_shape=jax.ShapeDtypeStruct((rows, width), jnp.bfloat16),
        in_specs=[SMEM, VMEM, VMEM] + [ANY] * len(pieces),
        out_specs=VMEM,
        scratch_shapes=[
            pltpu.VMEM((heads * rows, width + LANES), jnp.bfloat16),
            pltpu.VMEM((slots, rows, width + LANES), jnp.bfloat16),
            pltpu.VMEM((slots, rows, width + LANES), jnp.bfloat16),
            pltpu.VMEM((slots, pieces[0].shape[-2] - rows, pieces[0].shape[-1]), jnp.bfloat16),
            pltpu.VMEM((heads, slots, rows, rows), jnp.float32),
            pltpu.VMEM((heads, rows, LANES), jnp.float32),
            pltpu.VMEM((heads, rows, width + LANES), jnp.float32),
            pltpu.SemaphoreType.DMA((slots, 3)),
        ],
        compiler_params=params(8 + 2 * slots),
        cost_estimate=cost(
            4 * heads * rows * rows * slots * 256, 4 << 20, heads * rows * rows * slots
        ),
        name="attend",
    )(lengths, queries, query_marks, *pieces)


def cache_kernel(count, window, lengths, page_table, *refs):
    pieces = refs[:count]
    out, rows_buf, logical, sems = refs[count:]
    rows = rows_buf.shape[1]
    blocks = rows_buf.shape[0]
    width = out.shape[2]
    pages = out.shape[0] // PAGE
    me = lax.axis_index("seq")
    started = []

    def begin(source, block):
        copy = pltpu.make_async_copy(
            source.at[pl.ds(0, rows), :], rows_buf.at[block], sems.at[len(started)]
        )
        copy.start()
        started.append(copy)

    piece_copies(pieces, me, begin)

    def place_page(page, carry):
        local = page_table[page] - me * pages

        @pl.when((local >= 0) & (local < pages))
        def _():
            logical[local] = page

        return carry

    lax.fori_loop(0, page_table.shape[0], place_page, 0)
    starts, _ = request_bounds(lengths)
    for copy in started:
        copy.wait()
    row = lax.broadcasted_iota(jnp.int32, (PAGE, window), 0)
    column = lax.broadcasted_iota(jnp.int32, (PAGE, window), 1)

    def one_page(page, carry):
        first, amount, base = 0, 0, 0
        for r, start in enumerate(starts):
            count_r = (lengths[r] + PAGE - 1) // PAGE
            ahead = (logical[page] - base) * PAGE
            within = (ahead >= 0) & (ahead < lengths[r])
            first = jnp.where(within, start + ahead, first)
            amount = jnp.where(within, jnp.minimum(lengths[r] - ahead, PAGE), amount)
            base = base + count_r
        block = first // rows
        total = None
        for ahead in range(2):
            at = jnp.minimum(block + ahead, blocks - 1)
            inside = first - block * rows
            if ahead == 0:
                start = jnp.minimum(inside // 16 * 16, rows - window)
                offset = inside - start
            else:
                start = 0
                offset = inside - rows
            wanted = (row + offset == column) & (row < amount)
            if ahead == 1:
                wanted = wanted & (block + 1 < blocks)
            chooser = jnp.where(wanted, 1.0, 0.0).astype(jnp.bfloat16)
            found = dot_f32(chooser, rows_buf[at, pl.ds(pl.multiple_of(start, 16), window), :])
            total = found if total is None else total + found
        part = pl.ds(pl.multiple_of(page * PAGE, PAGE), PAGE)
        out[part, 0, :] = total[:, :width].astype(jnp.bfloat16)
        out[part, 1, :] = total[:, width:].astype(jnp.bfloat16)
        return carry

    lax.fori_loop(0, pages, one_page, 0)


def fill_cache(lengths, page_table, pieces, rows):
    width = pieces[0].shape[-1]
    blocks = lax.axis_size("seq")
    pages = page_table.shape[0] // blocks
    return pl.pallas_call(
        functools.partial(cache_kernel, len(pieces), 2 * PAGE),
        out_shape=jax.ShapeDtypeStruct((pages * PAGE, 2, width // 2), jnp.bfloat16),
        in_specs=[SMEM] * 2 + [ANY] * len(pieces),
        out_specs=VMEM,
        scratch_shapes=[
            pltpu.VMEM((blocks, rows, width), jnp.bfloat16),
            pltpu.SMEM((pages,), jnp.int32),
            pltpu.SemaphoreType.DMA((blocks,)),
        ],
        compiler_params=params(8),
        cost_estimate=cost(4 * pages * PAGE * 2 * PAGE * width, 3 << 20),
        name="fill_cache",
    )(lengths, page_table, *pieces)


def fetch_kernel(count, *refs):
    finish_loads(start_loads(refs[:count], refs[count:-1], refs[-1]))


def fetch(arrays):
    return pl.pallas_call(
        functools.partial(fetch_kernel, len(arrays)),
        out_shape=[jax.ShapeDtypeStruct(array.shape, array.dtype) for array in arrays],
        in_specs=[HBM] * len(arrays),
        out_specs=[VMEM] * len(arrays),
        scratch_shapes=[pltpu.SemaphoreType.DMA((len(arrays),))],
        compiler_params=params(10),
        cost_estimate=cost(0, 4 * sum(array.size for array in arrays)),
        name="fetch",
    )(*arrays)


def hidden_kernel(counts, *refs):
    places = len(counts)
    pieces, refs = refs[:places], refs[places:]
    w_out_pieces, refs = refs[: sum(counts)], refs[sum(counts) :]
    tokens, gain, w_gate, w_up, w_down = refs[:5]
    outs, attended, w_out = refs[5:-2], refs[-2], refs[-1]
    hidden, kept = outs[:2]
    place = lax.axis_index("tp")
    core = lax.rem(lax.axis_index("seq"), 2)
    each = pieces[0].shape[1]
    at = 0
    for i, count in enumerate(counts):
        attended[:, i * each : (i + 1) * each] = pieces[i][...]
        part = w_out.shape[1] // count
        for j in range(count):
            columns = pl.ds(pl.multiple_of((core ^ j) * part, part), part) if count > 1 else slice(None)
            w_out[i * each : (i + 1) * each, columns] = w_out_pieces[at][...]
            at += 1
    rows, features = tokens.shape
    width = kept.shape[1]
    step = min(rows, 256)
    gain_row = gain[...].astype(jnp.float32).reshape(1, -1)
    for first in range(0, rows, step):
        part = pl.ds(first, step)
        projected = dot_f32(attended[part, :], w_out[...])
        residual = (tokens[part, :].astype(jnp.float32) + projected).astype(jnp.bfloat16)
        mine = residual[:, :width]
        for i in range(1, places):
            mine = jnp.where(place == i, residual[:, i * width : (i + 1) * width], mine)
        kept[part, :] = mine
        normed = norm_rows(residual.astype(jnp.float32), gain_row)
        gate = dot_f32(normed, w_gate[...])
        up = dot_f32(normed, w_up[...])
        hidden[part, :] = (jax.nn.silu(gate) * up).astype(jnp.bfloat16)
    if len(outs) == 2:
        return
    weights = w_down[:, pl.ds(pl.multiple_of((place ^ 3) * width, width), width)]
    through = dot_f32(hidden[...], weights).astype(jnp.bfloat16)
    outs[2][...] = through[: rows // 2]
    outs[3][...] = through[rows // 2 :]


def hidden_of(pieces, w_out_pieces, tokens, gain, w_gate, w_up, w_down):
    rows, features = tokens.shape
    places = lax.axis_size("tp")
    width = features // places
    units = w_gate.shape[1]
    inner = places * pieces[0].shape[1]
    shapes = [(rows, units), (rows, width)] + [(rows // 2, width)] * (2 * (places == 4))
    counts = [len(piece) for piece in w_out_pieces]
    w_out_pieces = [part for piece in w_out_pieces for part in piece]
    return pl.pallas_call(
        functools.partial(hidden_kernel, counts),
        out_shape=[jax.ShapeDtypeStruct(shape, jnp.bfloat16) for shape in shapes],
        in_specs=[VMEM] * (places + len(w_out_pieces) + 5),
        out_specs=[VMEM] * len(shapes),
        scratch_shapes=[
            pltpu.VMEM((rows, inner), jnp.bfloat16),
            pltpu.VMEM((inner, features), jnp.bfloat16),
        ],
        compiler_params=params(12),
        cost_estimate=cost(6 * rows * features * units, 10 << 20),
        name="hidden",
    )(*pieces, *w_out_pieces, tokens, gain, w_gate, w_up, w_down)


def down_kernel(hidden, kept, w_down, far_top, far_low, near, own):
    place = lax.axis_index("tp")
    rows, width = own.shape

    def product(index):
        weights = w_down[:, pl.ds(pl.multiple_of(index * width, width), width)]
        return dot_f32(hidden[...], weights)

    far = product(place ^ 2)
    far_top[...] = far[: rows // 2]
    far_low[...] = far[rows // 2 :]
    near[...] = product(place ^ 1).astype(jnp.bfloat16)
    own[...] = product(place) + kept[...].astype(jnp.float32)


def down_blocks(hidden, kept, w_down):
    rows, width = kept.shape
    shapes = [((rows // 2, width), jnp.float32)] * 2
    shapes += [((rows, width), jnp.bfloat16), ((rows, width), jnp.float32)]
    return pl.pallas_call(
        down_kernel,
        out_shape=[jax.ShapeDtypeStruct(*shape) for shape in shapes],
        in_specs=[VMEM] * 3,
        out_specs=[VMEM] * 4,
        compiler_params=params(6),
        cost_estimate=cost(2 * rows * w_down.shape[0] * width * 3, 5 << 20),
        name="down_blocks",
    )(hidden, kept, w_down)


def add_kernel(out_parts, *refs):
    whole, parts, out = refs[: -1 - out_parts], refs[-1 - out_parts : -1], refs[-1]
    step = out.shape[0] // max(out_parts, 1)
    for i, first in enumerate(range(0, out.shape[0], step)):
        rows = pl.ds(first, step)
        total = whole[0][rows, :].astype(jnp.float32)
        for ref in whole[1:]:
            total = total + ref[rows, :].astype(jnp.float32)
        if out_parts:
            total = total + parts[i][...].astype(jnp.float32)
        out[rows, :] = total.astype(jnp.bfloat16)


def add_up(whole, parts=()):
    terms = [*whole, *parts]
    size = whole[0].size
    return pl.pallas_call(
        functools.partial(add_kernel, len(parts)),
        out_shape=jax.ShapeDtypeStruct(whole[0].shape, jnp.bfloat16),
        in_specs=[VMEM] * len(terms),
        out_specs=VMEM,
        compiler_params=params(6),
        cost_estimate=cost(size * len(terms), 4 * size * len(terms)),
        name="add_up",
    )(*terms)


def feed_forward(pieces, w_out_pieces, *arrays):
    hidden, kept, *through = hidden_of(pieces, w_out_pieces, *arrays)
    w_down = arrays[-1]
    if lax.axis_size("tp") != 4:
        share = lax.psum_scatter(
            dot_f32(hidden, w_down).astype(jnp.bfloat16), "tp", scatter_dimension=1, tiled=True
        )
        return add_up([kept, share]), hidden
    through = [tp_xor(part, 1) for part in through]
    far_top, far_low, near, own = down_blocks(hidden, kept, w_down)
    joined = [add_up([part, other]) for part, other in zip((far_top, far_low), through)]
    near = tp_xor(near, 1)
    far = [tp_xor(part, 2) for part in joined]
    return add_up([own, near], far), joined[-1]


def per_device(
    tokens,
    variate,
    positions,
    lengths,
    page_table,
    gain_attn,
    w_query,
    w_key,
    w_value,
    var_bias,
    w_out,
    gain_ffn,
    w_gate,
    w_up,
    w_down,
):
    rows = tokens.shape[0]
    width = w_query.shape[1]
    heads = width // HD
    reach = lax.axis_size("seq") // 2

    halve = lax.axis_size("tp") == 4 and lax.axis_size("seq") == 8
    cosine, sine, extra, marks, *weights, w_out_part = tables(
        lengths,
        var_bias,
        positions,
        variate,
        width,
        (tokens, gain_attn, w_query, w_key, w_value, w_out),
        halve,
    )
    pieces = gather_pieces(tokens, 2, extra)
    pieces[0] = weights[0]
    token_rows, queries, pairs = project(pieces, *weights[1:], cosine, sine, extra)
    w_out_part, _ = lax.optimization_barrier((w_out_part, pairs))
    row_pieces = seq_pieces(pairs)
    w_out_pieces = [(piece,) for piece in gather_pieces(w_out_part, 1)]
    if halve:
        twins = [(piece, seq_xor(piece, 1)) for (piece,) in w_out_pieces[1:]]
        w_out_pieces = w_out_pieces[:1] + twins
    marks, w_out_pieces = lax.optimization_barrier((marks, w_out_pieces))
    attended = attend(lengths, queries, marks, row_pieces, heads, reach)
    large = (w_out, token_rows, gain_ffn, w_gate, w_up, w_down)
    large = lax.optimization_barrier((large, attended))[0]
    w_out, *large = fetch(large)
    if halve:
        w_out_pieces[0] = (w_out,)
    attended_pieces = gather_pieces(attended, 1, large[1])
    mixed, joined = feed_forward(attended_pieces, w_out_pieces, *large)
    row_pieces, _ = lax.optimization_barrier((row_pieces, joined))
    cache = fill_cache(lengths, page_table, row_pieces, rows)
    return (mixed, cache)


def solution(mesh):
    placed = (
        P("seq", "tp"),
        P("seq"),
        P("seq"),
        P(),
        P(),
        P(),
        P(None, "tp"),
        P(None, "tp"),
        P(None, "tp"),
        P(None, "tp"),
        P("tp", None),
        P(),
        P(None, "tp"),
        P(None, "tp"),
        P("tp", None),
    )
    return jax.shard_map(
        per_device,
        mesh=mesh,
        in_specs=placed,
        out_specs=(P("seq", "tp"), P("seq", None, "tp")),
        check_vma=False,
    )
```

```python
import functools
import math

import jax
import jax.numpy as jnp
from jax import lax
from jax.experimental import pallas as pl
from jax.experimental.pallas import tpu as pltpu
from jax.sharding import PartitionSpec as P

HD = 64
PAGE = 64
VARS = 4
BIAS_PARTS = 3
LANES = 128
HIDDEN_SCORE = -1e30
EPS = 1e-06

VMEM = pl.BlockSpec(memory_space=pltpu.VMEM)
SMEM = pl.BlockSpec(memory_space=pltpu.SMEM)
ANY = pl.BlockSpec(memory_space=pl.ANY)
HBM = pl.BlockSpec(memory_space=pltpu.HBM)


def params(mib):
    return pltpu.CompilerParams(vmem_limit_bytes=mib << 20)


def cost(flops, nbytes, exps=0):
    return pl.CostEstimate(flops=flops, bytes_accessed=nbytes, transcendentals=exps)


def round_up(amount, unit):
    return (amount + unit - 1) // unit * unit


def dot_f32(left, right):
    return jnp.dot(left, right, preferred_element_type=jnp.float32)


def start_loads(sources, targets, sems):
    loads = [
        pltpu.make_async_copy(source, target, sems.at[i])
        for i, (source, target) in enumerate(zip(sources, targets))
    ]
    for load in loads:
        load.start()
    return loads


def finish_loads(loads):
    for load in loads:
        load.wait()


def tp_xor(value, mask):
    return lax.ppermute(value, "tp", [(i, i ^ mask) for i in range(lax.axis_size("tp"))])


def pair_gather(shard, split, before=()):
    far = [tp_xor(part, 2) for part in split]
    near = tp_xor(shard, 1)
    for i, value in enumerate(before):
        far[i], _ = lax.optimization_barrier((far[i], value))
    return [[shard], [near], far, [tp_xor(part, 1) for part in far]]


def turn_gather(shard):
    count = lax.axis_size("tp")
    pairs = [[(i, (i + turn) % count) for i in range(count)] for turn in range(1, count)]
    return [[shard]] + [[lax.ppermute(shard, "tp", each)] for each in pairs]


def gather_pieces(shard, split, before=()):
    if lax.axis_size("tp") == 4:
        return pair_gather(shard, split, before)
    return turn_gather(shard)


def piece_place(i, place, count):
    return place ^ i if count == 4 else lax.rem(place + count - i, count)


def nested(counts, refs):
    groups, at = [], 0
    for count in counts:
        groups.append(refs[at : at + count])
        at += count
    return groups, refs[at:]


def request_bounds(lengths):
    starts, ends, total = [], [], 0
    for r in range(lengths.shape[0]):
        starts.append(total)
        total = total + lengths[r]
        ends.append(total)
    return starts, ends


def segments_of(index, ends):
    segment = jnp.zeros_like(index)
    for end in ends:
        segment += (index >= end).astype(jnp.int32)
    return segment


def mark_count(requests):
    return round_up(BIAS_PARTS * VARS + requests, 16)


def tables_kernel(count, lengths, bias, positions, variate, *refs):
    cosine, sine, extra, marks = refs[count : count + 4]
    sources, targets, sems = list(refs[:count]), refs[count + 4 : -1], refs[-1]
    if targets[-1].shape != sources[-1].shape:
        part = targets[-1].shape[1]
        columns = pl.ds(pl.multiple_of(lax.rem(lax.axis_index("seq"), 2) * part, part), part)
        sources[-1] = sources[-1].at[:, columns]
    loads = start_loads(sources, targets, sems)
    rows = positions.shape[1]
    width = cosine.shape[1]
    half = HD // 2
    step = lax.broadcasted_iota(jnp.int32, (half, rows), 0).astype(jnp.float32) / half
    angles = jnp.exp(-math.log(10000.0) * step) * positions[...].astype(jnp.float32)
    cos_rows, sin_rows = jnp.cos(angles), jnp.sin(angles)
    copies = width // HD
    cosine[...] = jnp.transpose(jnp.concatenate([cos_rows, cos_rows] * copies, axis=0))
    sine[...] = jnp.transpose(jnp.concatenate([-sin_rows, sin_rows] * copies, axis=0))

    ids = variate[...].astype(jnp.float32)
    row = lax.broadcasted_iota(jnp.int32, extra.shape, 0)
    below = jnp.zeros(extra.shape, jnp.float32)
    for i in range(rows // extra.shape[1]):
        below = jnp.where(row == i, ids[:, i * extra.shape[1] : (i + 1) * extra.shape[1]], below)
    extra[...] = below.astype(jnp.bfloat16)

    requests = lengths.shape[0]
    shape = (mark_count(requests), rows)
    _, ends = request_bounds(lengths)
    me = lax.axis_index("seq")
    index = lax.broadcasted_iota(jnp.int32, shape, 1) + me * rows
    mark = lax.broadcasted_iota(jnp.int32, shape, 0)
    request = mark - BIAS_PARTS * VARS
    other = (segments_of(index, ends) != request) & (request >= 0) & (request < requests)
    same = (mark % VARS).astype(jnp.float32) == ids
    part = mark // VARS
    for h in range(marks.shape[0]):
        value = jnp.where(same, bias[0, h], bias[1, h])
        high = value.astype(jnp.bfloat16).astype(jnp.float32)
        middle = (value - high).astype(jnp.bfloat16).astype(jnp.float32)
        low = value - high - middle
        column = jnp.where(part == 0, high, jnp.where(part == 1, middle, low))
        column = jnp.where(part < BIAS_PARTS, column, 0.0)
        column = jnp.where(other, HIDDEN_SCORE, column)
        rest = jnp.zeros((LANES - shape[0], rows), jnp.float32)
        marks[h] = jnp.transpose(jnp.concatenate([column, rest], axis=0)).astype(jnp.bfloat16)
    finish_loads(loads)


def tables(lengths, bias, positions, variate, width, arrays, halve):
    rows = positions.shape[0]
    heads = width // HD
    extra = round_up(rows // (2 * width), 16)
    kept = [array.shape for array in arrays]
    if halve:
        kept[-1] = (kept[-1][0], kept[-1][1] // 2)
    return pl.pallas_call(
        functools.partial(tables_kernel, len(arrays)),
        out_shape=[
            jax.ShapeDtypeStruct((rows, width), jnp.float32),
            jax.ShapeDtypeStruct((rows, width), jnp.float32),
            jax.ShapeDtypeStruct((extra, 2 * width), jnp.bfloat16),
            jax.ShapeDtypeStruct((heads, rows, LANES), jnp.bfloat16),
        ]
        + [jax.ShapeDtypeStruct(shape, array.dtype) for shape, array in zip(kept, arrays)],
        in_specs=[SMEM, SMEM, VMEM, VMEM] + [ANY] * len(arrays),
        out_specs=[VMEM] * (4 + len(arrays)),
        scratch_shapes=[pltpu.SemaphoreType.DMA((len(arrays),))],
        compiler_params=params(6),
        cost_estimate=cost(rows * 1024, 1 << 20, rows * 64),
        name="tables",
    )(
        lengths,
        bias,
        positions.reshape(1, rows),
        variate.reshape(1, rows),
        *arrays,
    )


def rotate_lanes(vectors, cosine, signed_sine):
    lane = lax.broadcasted_iota(jnp.int32, vectors.shape, 1)
    half = HD // 2
    ahead = pltpu.roll(vectors, vectors.shape[1] - half, 1)
    behind = pltpu.roll(vectors, half, 1)
    partner = jnp.where(lane % HD < half, ahead, behind)
    return vectors * cosine + partner * signed_sine


def norm_rows(values, gain):
    scale = lax.rsqrt(jnp.mean(values * values, axis=-1, keepdims=True) + EPS)
    return (values * scale * gain).astype(jnp.bfloat16)


def project_kernel(counts, *refs):
    pieces, refs = nested(counts, refs)
    gain, w_q, w_k, w_v, cosine, sine, extra, tokens_out, queries, pairs, tokens, sem = refs
    pairs[tokens.shape[0] :, :] = extra[...]
    place = lax.axis_index("tp")
    part_width = pieces[0][0].shape[1]
    for i, piece in enumerate(pieces):
        block = piece_place(i, place, len(counts))
        columns = pl.ds(pl.multiple_of(block * part_width, part_width), part_width)
        step = tokens.shape[0] // len(piece)
        for j, part in enumerate(piece):
            tokens[j * step : (j + 1) * step, columns] = part[...]
    keep = pltpu.make_async_copy(tokens, tokens_out, sem)
    keep.start()
    rows = tokens.shape[0]
    width = w_q.shape[1]
    step = min(rows, 256)
    gain_row = gain[...].astype(jnp.float32).reshape(1, -1)
    for first in range(0, rows, step):
        part = pl.ds(first, step)
        normed = norm_rows(tokens[part, :].astype(jnp.float32), gain_row)
        cos_part, sin_part = cosine[part, :], sine[part, :]
        query = rotate_lanes(dot_f32(normed, w_q[...]), cos_part, sin_part)
        queries[part, :] = query.astype(jnp.bfloat16) * jnp.bfloat16(HD**-0.5)
        key = rotate_lanes(dot_f32(normed, w_k[...]), cos_part, sin_part)
        pairs[part, :width] = key.astype(jnp.bfloat16)
        pairs[part, width:] = dot_f32(normed, w_v[...]).astype(jnp.bfloat16)
    keep.wait()


def project(pieces, gain, w_query, w_key, w_value, cosine, sine, extra):
    rows = pieces[0][0].shape[0]
    counts = [len(piece) for piece in pieces]
    pieces = [part for piece in pieces for part in piece]
    width = w_query.shape[1]
    features = w_query.shape[0]
    return pl.pallas_call(
        functools.partial(project_kernel, counts),
        out_shape=[
            jax.ShapeDtypeStruct((rows, features), jnp.bfloat16),
            jax.ShapeDtypeStruct((rows, width), jnp.bfloat16),
            jax.ShapeDtypeStruct((rows + extra.shape[0], 2 * width), jnp.bfloat16),
        ],
        in_specs=[VMEM] * (len(pieces) + 7),
        out_specs=[HBM, VMEM, VMEM],
        scratch_shapes=[pltpu.VMEM((rows, features), jnp.bfloat16), pltpu.SemaphoreType.DMA],
        compiler_params=params(5),
        cost_estimate=cost(6 * rows * features * width, 4 << 20),
        name="project",
    )(*pieces, gain, w_query, w_key, w_value, cosine, sine, extra)


def seq_xor(value, mask):
    return lax.ppermute(value, "seq", [(i, i ^ mask) for i in range(lax.axis_size("seq"))])


def seq_pieces(pairs):
    if lax.axis_size("seq") == 8:
        diagonal = seq_xor(pairs, 6)
        across = seq_xor(pairs, 2)
        down = seq_xor(pairs, 4)
        twin = seq_xor(pairs, 1)
        across_twin = seq_xor(across, 1)
        down_twin = seq_xor(down, 1)
        diagonal_twin = seq_xor(diagonal, 1)
        return [pairs, twin, across, across_twin, down, down_twin, diagonal, diagonal_twin]
    return [lax.all_gather(pairs, "seq", axis=0)]


def piece_copies(pieces, me, wanted):
    if len(pieces) > 1:
        for m, piece in enumerate(pieces):
            wanted(piece, me ^ m)
    else:
        for j in range(pieces[0].shape[0]):
            wanted(pieces[0].at[j], j)


def attend_kernel(count, heads, reach, lengths, queries, query_marks, *refs):
    pieces = refs[:count]
    outs, scratch = refs[count:-8], refs[-8:]
    q_buf, k_buf, v_buf, extra_buf, scores, peak, total, sems = scratch
    me = lax.axis_index("seq")
    rows = queries.shape[0]
    _, ends = request_bounds(lengths)
    request_start = 0
    for end in ends:
        request_start = jnp.where(end <= me * rows, end, request_start)
    last = me - request_start // rows
    width = queries.shape[1]

    def copies(source, slot):
        return [
            pltpu.make_async_copy(
                source.at[pl.ds(0, rows), pl.ds(0, width)],
                k_buf.at[slot, :, pl.ds(0, width)],
                sems.at[slot, 0],
            ),
            pltpu.make_async_copy(
                source.at[pl.ds(0, rows), pl.ds(width, width)],
                v_buf.at[slot, :, pl.ds(0, width)],
                sems.at[slot, 1],
            ),
            pltpu.make_async_copy(
                source.at[pl.ds(rows, extra_buf.shape[1]), :], extra_buf.at[slot], sems.at[slot, 2]
            ),
        ]

    def begin(source, block):
        distance = me - block

        @pl.when((distance >= 0) & (distance <= last))
        def _():
            for copy in copies(source, distance):
                copy.start()

    piece_copies(pieces, me, begin)
    example = pieces[0] if count > 1 else pieces[0].at[0]

    marks = mark_count(lengths.shape[0])

    def finish(slot):
        for copy in copies(example, slot):
            copy.wait()
        extra = extra_buf[slot].astype(jnp.float32)
        pair_width = extra.shape[1]
        variates = jnp.concatenate([extra[i : i + 1] for i in range(rows // pair_width)], axis=1)
        mark = lax.broadcasted_iota(jnp.int32, (marks, rows), 0)
        key = lax.broadcasted_iota(jnp.int32, (marks, rows), 1) + (me - slot) * rows
        segment = segments_of(key, ends)
        same_variate = (mark % VARS).astype(jnp.float32) == variates
        same_segment = mark - BIAS_PARTS * VARS == segment
        marked = (same_variate & (mark < BIAS_PARTS * VARS)) | (
            same_segment & (mark >= BIAS_PARTS * VARS)
        )
        columns = jnp.transpose(jnp.where(marked, 1.0, 0.0))
        k_buf[slot, :, width : width + marks] = columns.astype(jnp.bfloat16)

    lane = lax.broadcasted_iota(jnp.int32, (rows, width), 1)
    for h in range(heads):
        part = pl.ds(h * rows, rows)
        q_buf[part, :width] = jnp.where(lane // HD == h, queries[...], jnp.bfloat16(0))
        q_buf[part, width:] = query_marks[h]
    for slot in range(reach + 1):
        v_buf[slot, :, width:] = jnp.ones((rows, LANES), jnp.bfloat16)
        k_buf[slot, :, width:] = jnp.zeros((rows, LANES), jnp.bfloat16)

    def narrow(tile):
        best = tile[:, :LANES]
        for first in range(LANES, rows, LANES):
            best = jnp.maximum(best, tile[:, first : first + LANES])
        return best

    def score(h, slot):
        return lax.dot_general(
            q_buf[pl.ds(h * rows, rows), :],
            k_buf[slot],
            (((1,), (1,)), ((), ())),
            preferred_element_type=jnp.float32,
        )

    finish(0)
    q_at = lax.broadcasted_iota(jnp.int32, (rows, rows), 0)
    k_at = lax.broadcasted_iota(jnp.int32, (rows, rows), 1)
    for h in range(heads):
        tile = jnp.where(k_at <= q_at, score(h, 0), HIDDEN_SCORE)
        scores[h, 0] = tile
        peak[h] = narrow(tile)

    def first_pass(slot, carry):
        finish(slot)
        for h in range(heads):
            tile = score(h, slot)
            scores[h, slot] = tile
            peak[h] = jnp.maximum(peak[h], narrow(tile))
        return carry

    lax.fori_loop(1, last + 1, first_pass, 0)
    for h in range(heads):
        best = jnp.max(peak[h], axis=1, keepdims=True)
        peak[h] = jnp.broadcast_to(best, (rows, LANES))
        total[h] = jnp.zeros_like(total[h])

    def second_pass(slot, carry):
        for h in range(heads):
            best = peak[h]
            wide = jnp.concatenate([best] * (rows // LANES), axis=1)
            weight = jnp.exp(scores[h, slot] - wide).astype(jnp.bfloat16)
            total[h] += dot_f32(weight, v_buf[slot])
        return carry

    lax.fori_loop(0, last + 1, second_pass, 0)
    result = total[0, :, :width] / total[0, :, width:]
    for h in range(1, heads):
        result = jnp.where(lane // HD == h, total[h, :, :width] / total[h, :, width:], result)
    result = result.astype(jnp.bfloat16)
    outs[0][...] = result
    for i, out in enumerate(outs[1:]):
        step = out.shape[0]
        out[...] = result[i * step : (i + 1) * step]


def attend(lengths, queries, query_marks, pieces, heads, reach):
    rows, width = queries.shape
    slots = reach + 1
    return pl.pallas_call(
        functools.partial(attend_kernel, len(pieces), heads, reach),
        out_shape=[
            jax.ShapeDtypeStruct((each, width), jnp.bfloat16)
            for each in (rows, rows // 2, rows // 2)
        ],
        in_specs=[SMEM, VMEM, VMEM] + [ANY] * len(pieces),
        out_specs=[VMEM] * 3,
        scratch_shapes=[
            pltpu.VMEM((heads * rows, width + LANES), jnp.bfloat16),
            pltpu.VMEM((slots, rows, width + LANES), jnp.bfloat16),
            pltpu.VMEM((slots, rows, width + LANES), jnp.bfloat16),
            pltpu.VMEM((slots, pieces[0].shape[-2] - rows, pieces[0].shape[-1]), jnp.bfloat16),
            pltpu.VMEM((heads, slots, rows, rows), jnp.float32),
            pltpu.VMEM((heads, rows, LANES), jnp.float32),
            pltpu.VMEM((heads, rows, width + LANES), jnp.float32),
            pltpu.SemaphoreType.DMA((slots, 3)),
        ],
        compiler_params=params(8 + 2 * slots),
        cost_estimate=cost(
            4 * heads * rows * rows * slots * 256, 4 << 20, heads * rows * rows * slots
        ),
        name="attend",
    )(lengths, queries, query_marks, *pieces)


def cache_kernel(count, window, lengths, page_table, *refs):
    pieces = refs[:count]
    out, rows_buf, logical, sems = refs[count:]
    rows = rows_buf.shape[1]
    blocks = rows_buf.shape[0]
    width = out.shape[2]
    pages = out.shape[0] // PAGE
    me = lax.axis_index("seq")
    started = []

    def begin(source, block):
        copy = pltpu.make_async_copy(
            source.at[pl.ds(0, rows), :], rows_buf.at[block], sems.at[len(started)]
        )
        copy.start()
        started.append(copy)

    piece_copies(pieces, me, begin)

    def place_page(page, carry):
        local = page_table[page] - me * pages

        @pl.when((local >= 0) & (local < pages))
        def _():
            logical[local] = page

        return carry

    lax.fori_loop(0, page_table.shape[0], place_page, 0)
    starts, _ = request_bounds(lengths)
    for copy in started:
        copy.wait()
    row = lax.broadcasted_iota(jnp.int32, (PAGE, window), 0)
    column = lax.broadcasted_iota(jnp.int32, (PAGE, window), 1)

    def one_page(page, carry):
        first, amount, base = 0, 0, 0
        for r, start in enumerate(starts):
            count_r = (lengths[r] + PAGE - 1) // PAGE
            ahead = (logical[page] - base) * PAGE
            within = (ahead >= 0) & (ahead < lengths[r])
            first = jnp.where(within, start + ahead, first)
            amount = jnp.where(within, jnp.minimum(lengths[r] - ahead, PAGE), amount)
            base = base + count_r
        block = first // rows
        total = None
        for ahead in range(2):
            at = jnp.minimum(block + ahead, blocks - 1)
            inside = first - block * rows
            if ahead == 0:
                start = jnp.minimum(inside // 16 * 16, rows - window)
                offset = inside - start
            else:
                start = 0
                offset = inside - rows
            wanted = (row + offset == column) & (row < amount)
            if ahead == 1:
                wanted = wanted & (block + 1 < blocks)
            chooser = jnp.where(wanted, 1.0, 0.0).astype(jnp.bfloat16)
            found = dot_f32(chooser, rows_buf[at, pl.ds(pl.multiple_of(start, 16), window), :])
            total = found if total is None else total + found
        part = pl.ds(pl.multiple_of(page * PAGE, PAGE), PAGE)
        out[part, 0, :] = total[:, :width].astype(jnp.bfloat16)
        out[part, 1, :] = total[:, width:].astype(jnp.bfloat16)
        return carry

    lax.fori_loop(0, pages, one_page, 0)


def fill_cache(lengths, page_table, pieces, rows):
    width = pieces[0].shape[-1]
    blocks = lax.axis_size("seq")
    pages = page_table.shape[0] // blocks
    return pl.pallas_call(
        functools.partial(cache_kernel, len(pieces), 2 * PAGE),
        out_shape=jax.ShapeDtypeStruct((pages * PAGE, 2, width // 2), jnp.bfloat16),
        in_specs=[SMEM] * 2 + [ANY] * len(pieces),
        out_specs=VMEM,
        scratch_shapes=[
            pltpu.VMEM((blocks, rows, width), jnp.bfloat16),
            pltpu.SMEM((pages,), jnp.int32),
            pltpu.SemaphoreType.DMA((blocks,)),
        ],
        compiler_params=params(8),
        cost_estimate=cost(4 * pages * PAGE * 2 * PAGE * width, 3 << 20),
        name="fill_cache",
    )(lengths, page_table, *pieces)


def fetch_kernel(count, *refs):
    finish_loads(start_loads(refs[:count], refs[count:-1], refs[-1]))


def fetch(arrays):
    return pl.pallas_call(
        functools.partial(fetch_kernel, len(arrays)),
        out_shape=[jax.ShapeDtypeStruct(array.shape, array.dtype) for array in arrays],
        in_specs=[HBM] * len(arrays),
        out_specs=[VMEM] * len(arrays),
        scratch_shapes=[pltpu.SemaphoreType.DMA((len(arrays),))],
        compiler_params=params(10),
        cost_estimate=cost(0, 4 * sum(array.size for array in arrays)),
        name="fetch",
    )(*arrays)


def hidden_kernel(counts, w_counts, *refs):
    pieces, refs = nested(counts, refs)
    w_out_pieces, refs = nested(w_counts, refs)
    tokens, gain, w_gate, w_up, w_down = refs[:5]
    outs, attended, w_out = refs[5:-2], refs[-2], refs[-1]
    hidden, kept = outs[:2]
    places = len(counts)
    place = lax.axis_index("tp")
    core = lax.rem(lax.axis_index("seq"), 2)
    each = pieces[0][0].shape[1]
    for i in range(places):
        inner = slice(i * each, (i + 1) * each)
        step = attended.shape[0] // counts[i]
        for j, part in enumerate(pieces[i]):
            attended[j * step : (j + 1) * step, inner] = part[...]
        if w_counts[i] == 1:
            w_out[inner, :] = w_out_pieces[i][0][...]
            continue
        step = w_out.shape[1] // w_counts[i]
        for j, part in enumerate(w_out_pieces[i]):
            w_out[inner, pl.ds(pl.multiple_of((core ^ j) * step, step), step)] = part[...]
    rows, features = tokens.shape
    width = kept.shape[1]
    step = min(rows, 256)
    gain_row = gain[...].astype(jnp.float32).reshape(1, -1)
    for first in range(0, rows, step):
        part = pl.ds(first, step)
        projected = dot_f32(attended[part, :], w_out[...])
        residual = (tokens[part, :].astype(jnp.float32) + projected).astype(jnp.bfloat16)
        mine = residual[:, :width]
        for i in range(1, places):
            mine = jnp.where(place == i, residual[:, i * width : (i + 1) * width], mine)
        kept[part, :] = mine
        normed = norm_rows(residual.astype(jnp.float32), gain_row)
        gate = dot_f32(normed, w_gate[...])
        up = dot_f32(normed, w_up[...])
        hidden[part, :] = (jax.nn.silu(gate) * up).astype(jnp.bfloat16)
    if len(outs) == 2:
        return
    weights = w_down[:, pl.ds(pl.multiple_of((place ^ 3) * width, width), width)]
    through = dot_f32(hidden[...], weights).astype(jnp.bfloat16)
    outs[2][...] = through[: rows // 2]
    outs[3][...] = through[rows // 2 :]


def hidden_of(pieces, w_out_pieces, tokens, gain, w_gate, w_up, w_down):
    rows, features = tokens.shape
    places = lax.axis_size("tp")
    width = features // places
    units = w_gate.shape[1]
    inner = places * pieces[0][0].shape[1]
    shapes = [(rows, units), (rows, width)] + [(rows // 2, width)] * (2 * (places == 4))
    counts = [[len(piece) for piece in group] for group in (pieces, w_out_pieces)]
    parts = [part for group in (pieces, w_out_pieces) for piece in group for part in piece]
    return pl.pallas_call(
        functools.partial(hidden_kernel, *counts),
        out_shape=[jax.ShapeDtypeStruct(shape, jnp.bfloat16) for shape in shapes],
        in_specs=[VMEM] * (len(parts) + 5),
        out_specs=[VMEM] * len(shapes),
        scratch_shapes=[
            pltpu.VMEM((rows, inner), jnp.bfloat16),
            pltpu.VMEM((inner, features), jnp.bfloat16),
        ],
        compiler_params=params(12),
        cost_estimate=cost(6 * rows * features * units, 10 << 20),
        name="hidden",
    )(*parts, tokens, gain, w_gate, w_up, w_down)


def down_kernel(hidden, kept, w_down, far_top, far_low, near, own):
    place = lax.axis_index("tp")
    rows, width = own.shape

    def product(index):
        weights = w_down[:, pl.ds(pl.multiple_of(index * width, width), width)]
        return dot_f32(hidden[...], weights)

    far = product(place ^ 2)
    far_top[...] = far[: rows // 2]
    far_low[...] = far[rows // 2 :]
    near[...] = product(place ^ 1).astype(jnp.bfloat16)
    own[...] = product(place) + kept[...].astype(jnp.float32)


def down_blocks(hidden, kept, w_down):
    rows, width = kept.shape
    shapes = [((rows // 2, width), jnp.float32)] * 2
    shapes += [((rows, width), jnp.bfloat16), ((rows, width), jnp.float32)]
    return pl.pallas_call(
        down_kernel,
        out_shape=[jax.ShapeDtypeStruct(*shape) for shape in shapes],
        in_specs=[VMEM] * 3,
        out_specs=[VMEM] * 4,
        compiler_params=params(6),
        cost_estimate=cost(2 * rows * w_down.shape[0] * width * 3, 5 << 20),
        name="down_blocks",
    )(hidden, kept, w_down)


def add_kernel(out_parts, *refs):
    whole, parts, out = refs[: -1 - out_parts], refs[-1 - out_parts : -1], refs[-1]
    step = out.shape[0] // max(out_parts, 1)
    for i, first in enumerate(range(0, out.shape[0], step)):
        rows = pl.ds(first, step)
        total = whole[0][rows, :].astype(jnp.float32)
        for ref in whole[1:]:
            total = total + ref[rows, :].astype(jnp.float32)
        if out_parts:
            total = total + parts[i][...].astype(jnp.float32)
        out[rows, :] = total.astype(jnp.bfloat16)


def add_up(whole, parts=()):
    terms = [*whole, *parts]
    size = whole[0].size
    return pl.pallas_call(
        functools.partial(add_kernel, len(parts)),
        out_shape=jax.ShapeDtypeStruct(whole[0].shape, jnp.bfloat16),
        in_specs=[VMEM] * len(terms),
        out_specs=VMEM,
        compiler_params=params(6),
        cost_estimate=cost(size * len(terms), 4 * size * len(terms)),
        name="add_up",
    )(*terms)


def feed_forward(pieces, w_out_pieces, *arrays):
    hidden, kept, *through = hidden_of(pieces, w_out_pieces, *arrays)
    w_down = arrays[-1]
    if lax.axis_size("tp") != 4:
        share = lax.psum_scatter(
            dot_f32(hidden, w_down).astype(jnp.bfloat16), "tp", scatter_dimension=1, tiled=True
        )
        return add_up([kept, share]), hidden
    through = [tp_xor(part, 1) for part in through]
    far_top, far_low, near, own = down_blocks(hidden, kept, w_down)
    joined = [add_up([part, other]) for part, other in zip((far_top, far_low), through)]
    near = tp_xor(near, 1)
    far = [tp_xor(part, 2) for part in joined]
    return add_up([own, near], far), joined[-1]


def per_device(
    tokens,
    variate,
    positions,
    lengths,
    page_table,
    gain_attn,
    w_query,
    w_key,
    w_value,
    var_bias,
    w_out,
    gain_ffn,
    w_gate,
    w_up,
    w_down,
):
    rows = tokens.shape[0]
    width = w_query.shape[1]
    heads = width // HD
    reach = lax.axis_size("seq") // 2

    halve = lax.axis_size("tp") == 4 and lax.axis_size("seq") == 8
    cosine, sine, extra, marks, w_query, w_key, w_out_part = tables(
        lengths, var_bias, positions, variate, width, (w_query, w_key, w_out), halve
    )
    own_tokens, gain_attn, w_value = fetch((tokens, gain_attn, w_value))
    step = rows // 2
    halves = lax.optimization_barrier((tokens[:step], tokens[step:], tokens))
    pieces = gather_pieces(halves[2], halves[:2], (extra, gain_attn))
    pieces[0] = [own_tokens]
    token_rows, queries, pairs = project(
        pieces, gain_attn, w_query, w_key, w_value, cosine, sine, extra
    )
    w_out_part, _ = lax.optimization_barrier((w_out_part, pairs))
    row_pieces = seq_pieces(pairs)
    w_out_pieces = gather_pieces(w_out_part, [w_out_part])
    marks, w_out_pieces = lax.optimization_barrier((marks, w_out_pieces))
    attended, *halves = attend(lengths, queries, marks, row_pieces, heads, reach)
    large = (w_out, token_rows, gain_ffn, w_gate, w_up, w_down)
    large, w_out_pieces = lax.optimization_barrier((large, w_out_pieces, attended))[:2]
    w_out, *large = fetch(large)
    if halve:
        twins = [[piece, seq_xor(piece, 1)] for (piece,) in w_out_pieces[1:]]
        w_out_pieces = [[w_out]] + twins
    attended_pieces = gather_pieces(attended, halves, large[1:2])
    mixed, joined = feed_forward(attended_pieces, w_out_pieces, *large)
    row_pieces, _ = lax.optimization_barrier((row_pieces, joined))
    cache = fill_cache(lengths, page_table, row_pieces, rows)
    return (mixed, cache)


def solution(mesh):
    placed = (
        P("seq", "tp"),
        P("seq"),
        P("seq"),
        P(),
        P(),
        P(),
        P(None, "tp"),
        P(None, "tp"),
        P(None, "tp"),
        P(None, "tp"),
        P("tp", None),
        P(),
        P(None, "tp"),
        P(None, "tp"),
        P("tp", None),
    )
    return jax.shard_map(
        per_device,
        mesh=mesh,
        in_specs=placed,
        out_specs=(P("seq", "tp"), P("seq", None, "tp")),
        check_vma=False,
    )
```

```python
import functools
import math

import jax
import jax.numpy as jnp
from jax import lax
from jax.experimental import pallas as pl
from jax.experimental.pallas import tpu as pltpu
from jax.sharding import PartitionSpec as P

HD = 64
PAGE = 64
VARS = 4
BIAS_PARTS = 3
LANES = 128
HIDDEN_SCORE = -1e30
EPS = 1e-06

VMEM = pl.BlockSpec(memory_space=pltpu.VMEM)
SMEM = pl.BlockSpec(memory_space=pltpu.SMEM)
ANY = pl.BlockSpec(memory_space=pl.ANY)
HBM = pl.BlockSpec(memory_space=pltpu.HBM)


def params(mib):
    return pltpu.CompilerParams(vmem_limit_bytes=mib << 20)


def cost(flops, nbytes, exps=0):
    return pl.CostEstimate(flops=flops, bytes_accessed=nbytes, transcendentals=exps)


def round_up(amount, unit):
    return (amount + unit - 1) // unit * unit


def dot_f32(left, right):
    return jnp.dot(left, right, preferred_element_type=jnp.float32)


def start_loads(sources, targets, sems):
    loads = [
        pltpu.make_async_copy(source, target, sems.at[i])
        for i, (source, target) in enumerate(zip(sources, targets))
    ]
    for load in loads:
        load.start()
    return loads


def finish_loads(loads):
    for load in loads:
        load.wait()


def tp_xor(value, mask):
    return lax.ppermute(value, "tp", [(i, i ^ mask) for i in range(lax.axis_size("tp"))])


def pair_gather(shard, split, before=(), near_first=False):
    far = [tp_xor(part, 2) for part in split]
    near = tp_xor(shard, 1)
    if near_first:
        far[0], _ = lax.optimization_barrier((far[0], near))
    for i, value in enumerate(before):
        far[i], _ = lax.optimization_barrier((far[i], value))
    return [[shard], [near], far, [tp_xor(part, 1) for part in far]]


def turn_gather(shard):
    count = lax.axis_size("tp")
    pairs = [[(i, (i + turn) % count) for i in range(count)] for turn in range(1, count)]
    return [[shard]] + [[lax.ppermute(shard, "tp", each)] for each in pairs]


def gather_pieces(shard, split, before=(), near_first=False):
    if lax.axis_size("tp") == 4:
        return pair_gather(shard, split, before, near_first)
    return turn_gather(shard)


def piece_place(i, place, count):
    return place ^ i if count == 4 else lax.rem(place + count - i, count)


def nested(counts, refs):
    groups, at = [], 0
    for count in counts:
        groups.append(refs[at : at + count])
        at += count
    return groups, refs[at:]


def request_bounds(lengths):
    starts, ends, total = [], [], 0
    for r in range(lengths.shape[0]):
        starts.append(total)
        total = total + lengths[r]
        ends.append(total)
    return starts, ends


def segments_of(index, ends):
    segment = jnp.zeros_like(index)
    for end in ends:
        segment += (index >= end).astype(jnp.int32)
    return segment


def mark_count(requests):
    return round_up(BIAS_PARTS * VARS + requests, 16)


def tables_kernel(count, lengths, bias, positions, variate, *refs):
    cosine, sine, extra, marks = refs[count : count + 4]
    sources, targets, sems = list(refs[:count]), refs[count + 4 : -1], refs[-1]
    if targets[-1].shape != sources[-1].shape:
        part = targets[-1].shape[1]
        columns = pl.ds(pl.multiple_of(lax.rem(lax.axis_index("seq"), 2) * part, part), part)
        sources[-1] = sources[-1].at[:, columns]
    loads = start_loads(sources, targets, sems)
    rows = positions.shape[1]
    width = cosine.shape[1]
    half = HD // 2
    step = lax.broadcasted_iota(jnp.int32, (half, rows), 0).astype(jnp.float32) / half
    angles = jnp.exp(-math.log(10000.0) * step) * positions[...].astype(jnp.float32)
    cos_rows, sin_rows = jnp.cos(angles), jnp.sin(angles)
    copies = width // HD
    cosine[...] = jnp.transpose(jnp.concatenate([cos_rows, cos_rows] * copies, axis=0))
    sine[...] = jnp.transpose(jnp.concatenate([-sin_rows, sin_rows] * copies, axis=0))

    ids = variate[...].astype(jnp.float32)
    row = lax.broadcasted_iota(jnp.int32, extra.shape, 0)
    below = jnp.zeros(extra.shape, jnp.float32)
    for i in range(rows // extra.shape[1]):
        below = jnp.where(row == i, ids[:, i * extra.shape[1] : (i + 1) * extra.shape[1]], below)
    extra[...] = below.astype(jnp.bfloat16)

    requests = lengths.shape[0]
    shape = (mark_count(requests), rows)
    _, ends = request_bounds(lengths)
    me = lax.axis_index("seq")
    index = lax.broadcasted_iota(jnp.int32, shape, 1) + me * rows
    mark = lax.broadcasted_iota(jnp.int32, shape, 0)
    request = mark - BIAS_PARTS * VARS
    other = (segments_of(index, ends) != request) & (request >= 0) & (request < requests)
    same = (mark % VARS).astype(jnp.float32) == ids
    part = mark // VARS
    for h in range(marks.shape[0]):
        value = jnp.where(same, bias[0, h], bias[1, h])
        high = value.astype(jnp.bfloat16).astype(jnp.float32)
        middle = (value - high).astype(jnp.bfloat16).astype(jnp.float32)
        low = value - high - middle
        column = jnp.where(part == 0, high, jnp.where(part == 1, middle, low))
        column = jnp.where(part < BIAS_PARTS, column, 0.0)
        column = jnp.where(other, HIDDEN_SCORE, column)
        rest = jnp.zeros((LANES - shape[0], rows), jnp.float32)
        marks[h] = jnp.transpose(jnp.concatenate([column, rest], axis=0)).astype(jnp.bfloat16)
    finish_loads(loads)


def tables(lengths, bias, positions, variate, width, arrays, halve):
    rows = positions.shape[0]
    heads = width // HD
    extra = round_up(rows // (2 * width), 16)
    kept = [array.shape for array in arrays]
    if halve:
        kept[-1] = (kept[-1][0], kept[-1][1] // 2)
    return pl.pallas_call(
        functools.partial(tables_kernel, len(arrays)),
        out_shape=[
            jax.ShapeDtypeStruct((rows, width), jnp.float32),
            jax.ShapeDtypeStruct((rows, width), jnp.float32),
            jax.ShapeDtypeStruct((extra, 2 * width), jnp.bfloat16),
            jax.ShapeDtypeStruct((heads, rows, LANES), jnp.bfloat16),
        ]
        + [jax.ShapeDtypeStruct(shape, array.dtype) for shape, array in zip(kept, arrays)],
        in_specs=[SMEM, SMEM, VMEM, VMEM] + [ANY] * len(arrays),
        out_specs=[VMEM] * (4 + len(arrays)),
        scratch_shapes=[pltpu.SemaphoreType.DMA((len(arrays),))],
        compiler_params=params(6),
        cost_estimate=cost(rows * 1024, 1 << 20, rows * 64),
        name="tables",
    )(
        lengths,
        bias,
        positions.reshape(1, rows),
        variate.reshape(1, rows),
        *arrays,
    )


def rotate_lanes(vectors, cosine, signed_sine):
    lane = lax.broadcasted_iota(jnp.int32, vectors.shape, 1)
    half = HD // 2
    ahead = pltpu.roll(vectors, vectors.shape[1] - half, 1)
    behind = pltpu.roll(vectors, half, 1)
    partner = jnp.where(lane % HD < half, ahead, behind)
    return vectors * cosine + partner * signed_sine


def norm_rows(values, gain):
    scale = lax.rsqrt(jnp.mean(values * values, axis=-1, keepdims=True) + EPS)
    return (values * scale * gain).astype(jnp.bfloat16)


def project_kernel(counts, *refs):
    pieces, refs = nested(counts, refs)
    gain, w_q, w_k, w_v, cosine, sine, extra, tokens_out, queries, pairs, tokens, sem = refs
    pairs[tokens.shape[0] :, :] = extra[...]
    place = lax.axis_index("tp")
    part_width = pieces[0][0].shape[1]
    for i, piece in enumerate(pieces):
        block = piece_place(i, place, len(counts))
        columns = pl.ds(pl.multiple_of(block * part_width, part_width), part_width)
        step = tokens.shape[0] // len(piece)
        for j, part in enumerate(piece):
            tokens[j * step : (j + 1) * step, columns] = part[...]
    keep = pltpu.make_async_copy(tokens, tokens_out, sem)
    keep.start()
    rows = tokens.shape[0]
    width = w_q.shape[1]
    step = min(rows, 256)
    gain_row = gain[...].astype(jnp.float32).reshape(1, -1)
    for first in range(0, rows, step):
        part = pl.ds(first, step)
        normed = norm_rows(tokens[part, :].astype(jnp.float32), gain_row)
        cos_part, sin_part = cosine[part, :], sine[part, :]
        query = rotate_lanes(dot_f32(normed, w_q[...]), cos_part, sin_part)
        queries[part, :] = query.astype(jnp.bfloat16) * jnp.bfloat16(HD**-0.5)
        key = rotate_lanes(dot_f32(normed, w_k[...]), cos_part, sin_part)
        pairs[part, :width] = key.astype(jnp.bfloat16)
        pairs[part, width:] = dot_f32(normed, w_v[...]).astype(jnp.bfloat16)
    keep.wait()


def project(pieces, gain, w_query, w_key, w_value, cosine, sine, extra):
    rows = pieces[0][0].shape[0]
    counts = [len(piece) for piece in pieces]
    pieces = [part for piece in pieces for part in piece]
    width = w_query.shape[1]
    features = w_query.shape[0]
    return pl.pallas_call(
        functools.partial(project_kernel, counts),
        out_shape=[
            jax.ShapeDtypeStruct((rows, features), jnp.bfloat16),
            jax.ShapeDtypeStruct((rows, width), jnp.bfloat16),
            jax.ShapeDtypeStruct((rows + extra.shape[0], 2 * width), jnp.bfloat16),
        ],
        in_specs=[VMEM] * (len(pieces) + 7),
        out_specs=[HBM, VMEM, VMEM],
        scratch_shapes=[pltpu.VMEM((rows, features), jnp.bfloat16), pltpu.SemaphoreType.DMA],
        compiler_params=params(5),
        cost_estimate=cost(6 * rows * features * width, 4 << 20),
        name="project",
    )(*pieces, gain, w_query, w_key, w_value, cosine, sine, extra)


def seq_xor(value, mask):
    return lax.ppermute(value, "seq", [(i, i ^ mask) for i in range(lax.axis_size("seq"))])


def seq_pieces(pairs, before):
    if lax.axis_size("seq") == 8:
        diagonal = seq_xor(pairs, 6)
        across = seq_xor(pairs, 2)
        down = seq_xor(pairs, 4)
        twin = seq_xor(pairs, 1)
        (across, down, diagonal), _ = lax.optimization_barrier(((across, down, diagonal), before))
        across_twin = seq_xor(across, 1)
        down_twin = seq_xor(down, 1)
        diagonal_twin = seq_xor(diagonal, 1)
        return [pairs, twin, across, across_twin, down, down_twin, diagonal, diagonal_twin]
    return [lax.all_gather(pairs, "seq", axis=0)]


def piece_copies(pieces, me, wanted):
    if len(pieces) > 1:
        for m, piece in enumerate(pieces):
            wanted(piece, me ^ m)
    else:
        for j in range(pieces[0].shape[0]):
            wanted(pieces[0].at[j], j)


def attend_kernel(count, heads, reach, lengths, queries, query_marks, *refs):
    pieces = refs[:count]
    outs, scratch = refs[count:-8], refs[-8:]
    q_buf, k_buf, v_buf, extra_buf, scores, peak, total, sems = scratch
    me = lax.axis_index("seq")
    rows = queries.shape[0]
    _, ends = request_bounds(lengths)
    request_start = 0
    for end in ends:
        request_start = jnp.where(end <= me * rows, end, request_start)
    last = me - request_start // rows
    width = queries.shape[1]

    def copies(source, slot):
        return [
            pltpu.make_async_copy(
                source.at[pl.ds(0, rows), pl.ds(0, width)],
                k_buf.at[slot, :, pl.ds(0, width)],
                sems.at[slot, 0],
            ),
            pltpu.make_async_copy(
                source.at[pl.ds(0, rows), pl.ds(width, width)],
                v_buf.at[slot, :, pl.ds(0, width)],
                sems.at[slot, 1],
            ),
            pltpu.make_async_copy(
                source.at[pl.ds(rows, extra_buf.shape[1]), :], extra_buf.at[slot], sems.at[slot, 2]
            ),
        ]

    def begin(source, block):
        distance = me - block

        @pl.when((distance >= 0) & (distance <= last))
        def _():
            for copy in copies(source, distance):
                copy.start()

    piece_copies(pieces, me, begin)
    example = pieces[0] if count > 1 else pieces[0].at[0]

    marks = mark_count(lengths.shape[0])

    def finish(slot):
        for copy in copies(example, slot):
            copy.wait()
        extra = extra_buf[slot].astype(jnp.float32)
        pair_width = extra.shape[1]
        variates = jnp.concatenate([extra[i : i + 1] for i in range(rows // pair_width)], axis=1)
        mark = lax.broadcasted_iota(jnp.int32, (marks, rows), 0)
        key = lax.broadcasted_iota(jnp.int32, (marks, rows), 1) + (me - slot) * rows
        segment = segments_of(key, ends)
        same_variate = (mark % VARS).astype(jnp.float32) == variates
        same_segment = mark - BIAS_PARTS * VARS == segment
        marked = (same_variate & (mark < BIAS_PARTS * VARS)) | (
            same_segment & (mark >= BIAS_PARTS * VARS)
        )
        columns = jnp.transpose(jnp.where(marked, 1.0, 0.0))
        k_buf[slot, :, width : width + marks] = columns.astype(jnp.bfloat16)

    lane = lax.broadcasted_iota(jnp.int32, (rows, width), 1)
    for h in range(heads):
        part = pl.ds(h * rows, rows)
        q_buf[part, :width] = jnp.where(lane // HD == h, queries[...], jnp.bfloat16(0))
        q_buf[part, width:] = query_marks[h]
    for slot in range(reach + 1):
        v_buf[slot, :, width:] = jnp.ones((rows, LANES), jnp.bfloat16)
        k_buf[slot, :, width:] = jnp.zeros((rows, LANES), jnp.bfloat16)

    def narrow(tile):
        best = tile[:, :LANES]
        for first in range(LANES, rows, LANES):
            best = jnp.maximum(best, tile[:, first : first + LANES])
        return best

    def score(h, slot):
        return lax.dot_general(
            q_buf[pl.ds(h * rows, rows), :],
            k_buf[slot],
            (((1,), (1,)), ((), ())),
            preferred_element_type=jnp.float32,
        )

    finish(0)
    q_at = lax.broadcasted_iota(jnp.int32, (rows, rows), 0)
    k_at = lax.broadcasted_iota(jnp.int32, (rows, rows), 1)
    for h in range(heads):
        tile = jnp.where(k_at <= q_at, score(h, 0), HIDDEN_SCORE)
        scores[h, 0] = tile
        peak[h] = narrow(tile)

    def first_pass(slot, carry):
        finish(slot)
        for h in range(heads):
            tile = score(h, slot)
            scores[h, slot] = tile
            peak[h] = jnp.maximum(peak[h], narrow(tile))
        return carry

    lax.fori_loop(1, last + 1, first_pass, 0)
    for h in range(heads):
        best = jnp.max(peak[h], axis=1, keepdims=True)
        peak[h] = jnp.broadcast_to(best, (rows, LANES))
        total[h] = jnp.zeros_like(total[h])

    def second_pass(slot, carry):
        for h in range(heads):
            best = peak[h]
            wide = jnp.concatenate([best] * (rows // LANES), axis=1)
            weight = jnp.exp(scores[h, slot] - wide).astype(jnp.bfloat16)
            total[h] += dot_f32(weight, v_buf[slot])
        return carry

    lax.fori_loop(0, last + 1, second_pass, 0)
    result = total[0, :, :width] / total[0, :, width:]
    for h in range(1, heads):
        result = jnp.where(lane // HD == h, total[h, :, :width] / total[h, :, width:], result)
    result = result.astype(jnp.bfloat16)
    outs[0][...] = result
    for i, out in enumerate(outs[1:]):
        step = out.shape[0]
        out[...] = result[i * step : (i + 1) * step]


def attend(lengths, queries, query_marks, pieces, heads, reach):
    rows, width = queries.shape
    slots = reach + 1
    return pl.pallas_call(
        functools.partial(attend_kernel, len(pieces), heads, reach),
        out_shape=[
            jax.ShapeDtypeStruct((each, width), jnp.bfloat16)
            for each in (rows, rows // 2, rows // 2)
        ],
        in_specs=[SMEM, VMEM, VMEM] + [ANY] * len(pieces),
        out_specs=[VMEM] * 3,
        scratch_shapes=[
            pltpu.VMEM((heads * rows, width + LANES), jnp.bfloat16),
            pltpu.VMEM((slots, rows, width + LANES), jnp.bfloat16),
            pltpu.VMEM((slots, rows, width + LANES), jnp.bfloat16),
            pltpu.VMEM((slots, pieces[0].shape[-2] - rows, pieces[0].shape[-1]), jnp.bfloat16),
            pltpu.VMEM((heads, slots, rows, rows), jnp.float32),
            pltpu.VMEM((heads, rows, LANES), jnp.float32),
            pltpu.VMEM((heads, rows, width + LANES), jnp.float32),
            pltpu.SemaphoreType.DMA((slots, 3)),
        ],
        compiler_params=params(8 + 2 * slots),
        cost_estimate=cost(
            4 * heads * rows * rows * slots * 256, 4 << 20, heads * rows * rows * slots
        ),
        name="attend",
    )(lengths, queries, query_marks, *pieces)


def cache_kernel(count, window, lengths, page_table, *refs):
    pieces = refs[:count]
    out, rows_buf, logical, sems = refs[count:]
    rows = rows_buf.shape[1]
    blocks = rows_buf.shape[0]
    width = out.shape[2]
    pages = out.shape[0] // PAGE
    me = lax.axis_index("seq")
    started = []

    def begin(source, block):
        copy = pltpu.make_async_copy(
            source.at[pl.ds(0, rows), :], rows_buf.at[block], sems.at[len(started)]
        )
        copy.start()
        started.append(copy)

    piece_copies(pieces, me, begin)

    def place_page(page, carry):
        local = page_table[page] - me * pages

        @pl.when((local >= 0) & (local < pages))
        def _():
            logical[local] = page

        return carry

    lax.fori_loop(0, page_table.shape[0], place_page, 0)
    starts, _ = request_bounds(lengths)
    for copy in started:
        copy.wait()
    row = lax.broadcasted_iota(jnp.int32, (PAGE, window), 0)
    column = lax.broadcasted_iota(jnp.int32, (PAGE, window), 1)

    def one_page(page, carry):
        first, amount, base = 0, 0, 0
        for r, start in enumerate(starts):
            count_r = (lengths[r] + PAGE - 1) // PAGE
            ahead = (logical[page] - base) * PAGE
            within = (ahead >= 0) & (ahead < lengths[r])
            first = jnp.where(within, start + ahead, first)
            amount = jnp.where(within, jnp.minimum(lengths[r] - ahead, PAGE), amount)
            base = base + count_r
        block = first // rows
        total = None
        for ahead in range(2):
            at = jnp.minimum(block + ahead, blocks - 1)
            inside = first - block * rows
            if ahead == 0:
                start = jnp.minimum(inside // 16 * 16, rows - window)
                offset = inside - start
            else:
                start = 0
                offset = inside - rows
            wanted = (row + offset == column) & (row < amount)
            if ahead == 1:
                wanted = wanted & (block + 1 < blocks)
            chooser = jnp.where(wanted, 1.0, 0.0).astype(jnp.bfloat16)
            found = dot_f32(chooser, rows_buf[at, pl.ds(pl.multiple_of(start, 16), window), :])
            total = found if total is None else total + found
        part = pl.ds(pl.multiple_of(page * PAGE, PAGE), PAGE)
        out[part, 0, :] = total[:, :width].astype(jnp.bfloat16)
        out[part, 1, :] = total[:, width:].astype(jnp.bfloat16)
        return carry

    lax.fori_loop(0, pages, one_page, 0)


def fill_cache(lengths, page_table, pieces, rows):
    width = pieces[0].shape[-1]
    blocks = lax.axis_size("seq")
    pages = page_table.shape[0] // blocks
    return pl.pallas_call(
        functools.partial(cache_kernel, len(pieces), 2 * PAGE),
        out_shape=jax.ShapeDtypeStruct((pages * PAGE, 2, width // 2), jnp.bfloat16),
        in_specs=[SMEM] * 2 + [ANY] * len(pieces),
        out_specs=VMEM,
        scratch_shapes=[
            pltpu.VMEM((blocks, rows, width), jnp.bfloat16),
            pltpu.SMEM((pages,), jnp.int32),
            pltpu.SemaphoreType.DMA((blocks,)),
        ],
        compiler_params=params(8),
        cost_estimate=cost(4 * pages * PAGE * 2 * PAGE * width, 3 << 20),
        name="fill_cache",
    )(lengths, page_table, *pieces)


def fetch_kernel(count, *refs):
    finish_loads(start_loads(refs[:count], refs[count:-1], refs[-1]))


def fetch(arrays):
    return pl.pallas_call(
        functools.partial(fetch_kernel, len(arrays)),
        out_shape=[jax.ShapeDtypeStruct(array.shape, array.dtype) for array in arrays],
        in_specs=[HBM] * len(arrays),
        out_specs=[VMEM] * len(arrays),
        scratch_shapes=[pltpu.SemaphoreType.DMA((len(arrays),))],
        compiler_params=params(10),
        cost_estimate=cost(0, 4 * sum(array.size for array in arrays)),
        name="fetch",
    )(*arrays)


def hidden_kernel(counts, w_counts, *refs):
    pieces, refs = nested(counts, refs)
    w_out_pieces, refs = nested(w_counts, refs)
    tokens, gain, w_gate, w_up, w_down = refs[:5]
    outs, attended, w_out = refs[5:-2], refs[-2], refs[-1]
    hidden, kept = outs[:2]
    places = len(counts)
    place = lax.axis_index("tp")
    core = lax.rem(lax.axis_index("seq"), 2)
    each = pieces[0][0].shape[1]
    for i in range(places):
        inner = slice(i * each, (i + 1) * each)
        step = attended.shape[0] // counts[i]
        for j, part in enumerate(pieces[i]):
            attended[j * step : (j + 1) * step, inner] = part[...]
        if w_counts[i] == 1:
            w_out[inner, :] = w_out_pieces[i][0][...]
            continue
        step = w_out.shape[1] // w_counts[i]
        for j, part in enumerate(w_out_pieces[i]):
            w_out[inner, pl.ds(pl.multiple_of((core ^ j) * step, step), step)] = part[...]
    rows, features = tokens.shape
    width = kept.shape[1]
    step = min(rows, 256)
    gain_row = gain[...].astype(jnp.float32).reshape(1, -1)
    for first in range(0, rows, step):
        part = pl.ds(first, step)
        projected = dot_f32(attended[part, :], w_out[...])
        residual = (tokens[part, :].astype(jnp.float32) + projected).astype(jnp.bfloat16)
        mine = residual[:, :width]
        for i in range(1, places):
            mine = jnp.where(place == i, residual[:, i * width : (i + 1) * width], mine)
        kept[part, :] = mine
        normed = norm_rows(residual.astype(jnp.float32), gain_row)
        gate = dot_f32(normed, w_gate[...])
        up = dot_f32(normed, w_up[...])
        hidden[part, :] = (jax.nn.silu(gate) * up).astype(jnp.bfloat16)
    if len(outs) == 2:
        return
    weights = w_down[:, pl.ds(pl.multiple_of((place ^ 3) * width, width), width)]
    through = dot_f32(hidden[...], weights).astype(jnp.bfloat16)
    outs[2][...] = through[: rows // 2]
    outs[3][...] = through[rows // 2 :]


def hidden_of(pieces, w_out_pieces, tokens, gain, w_gate, w_up, w_down):
    rows, features = tokens.shape
    places = lax.axis_size("tp")
    width = features // places
    units = w_gate.shape[1]
    inner = places * pieces[0][0].shape[1]
    shapes = [(rows, units), (rows, width)] + [(rows // 2, width)] * (2 * (places == 4))
    counts = [[len(piece) for piece in group] for group in (pieces, w_out_pieces)]
    parts = [part for group in (pieces, w_out_pieces) for piece in group for part in piece]
    return pl.pallas_call(
        functools.partial(hidden_kernel, *counts),
        out_shape=[jax.ShapeDtypeStruct(shape, jnp.bfloat16) for shape in shapes],
        in_specs=[VMEM] * (len(parts) + 5),
        out_specs=[VMEM] * len(shapes),
        scratch_shapes=[
            pltpu.VMEM((rows, inner), jnp.bfloat16),
            pltpu.VMEM((inner, features), jnp.bfloat16),
        ],
        compiler_params=params(12),
        cost_estimate=cost(6 * rows * features * units, 10 << 20),
        name="hidden",
    )(*parts, tokens, gain, w_gate, w_up, w_down)


def down_kernel(hidden, kept, w_down, far_top, far_low, near, own):
    place = lax.axis_index("tp")
    rows, width = own.shape

    def product(index):
        weights = w_down[:, pl.ds(pl.multiple_of(index * width, width), width)]
        return dot_f32(hidden[...], weights)

    far = product(place ^ 2)
    far_top[...] = far[: rows // 2]
    far_low[...] = far[rows // 2 :]
    near[...] = product(place ^ 1).astype(jnp.bfloat16)
    own[...] = product(place) + kept[...].astype(jnp.float32)


def down_blocks(hidden, kept, w_down):
    rows, width = kept.shape
    shapes = [((rows // 2, width), jnp.float32)] * 2
    shapes += [((rows, width), jnp.bfloat16), ((rows, width), jnp.float32)]
    return pl.pallas_call(
        down_kernel,
        out_shape=[jax.ShapeDtypeStruct(*shape) for shape in shapes],
        in_specs=[VMEM] * 3,
        out_specs=[VMEM] * 4,
        compiler_params=params(6),
        cost_estimate=cost(2 * rows * w_down.shape[0] * width * 3, 5 << 20),
        name="down_blocks",
    )(hidden, kept, w_down)


def add_kernel(out_parts, *refs):
    whole, parts, out = refs[: -1 - out_parts], refs[-1 - out_parts : -1], refs[-1]
    step = out.shape[0] // max(out_parts, 1)
    for i, first in enumerate(range(0, out.shape[0], step)):
        rows = pl.ds(first, step)
        total = whole[0][rows, :].astype(jnp.float32)
        for ref in whole[1:]:
            total = total + ref[rows, :].astype(jnp.float32)
        if out_parts:
            total = total + parts[i][...].astype(jnp.float32)
        out[rows, :] = total.astype(jnp.bfloat16)


def add_up(whole, parts=()):
    terms = [*whole, *parts]
    size = whole[0].size
    return pl.pallas_call(
        functools.partial(add_kernel, len(parts)),
        out_shape=jax.ShapeDtypeStruct(whole[0].shape, jnp.bfloat16),
        in_specs=[VMEM] * len(terms),
        out_specs=VMEM,
        compiler_params=params(6),
        cost_estimate=cost(size * len(terms), 4 * size * len(terms)),
        name="add_up",
    )(*terms)


def feed_forward(pieces, w_out_pieces, *arrays):
    hidden, kept, *through = hidden_of(pieces, w_out_pieces, *arrays)
    w_down = arrays[-1]
    if lax.axis_size("tp") != 4:
        share = lax.psum_scatter(
            dot_f32(hidden, w_down).astype(jnp.bfloat16), "tp", scatter_dimension=1, tiled=True
        )
        return add_up([kept, share]), hidden
    through = [tp_xor(part, 1) for part in through]
    far_top, far_low, near, own = down_blocks(hidden, kept, w_down)
    joined = [add_up([part, other]) for part, other in zip((far_top, far_low), through)]
    near = tp_xor(near, 1)
    far = [tp_xor(part, 2) for part in joined]
    return add_up([own, near], far), joined[-1]


def per_device(
    tokens,
    variate,
    positions,
    lengths,
    page_table,
    gain_attn,
    w_query,
    w_key,
    w_value,
    var_bias,
    w_out,
    gain_ffn,
    w_gate,
    w_up,
    w_down,
):
    rows = tokens.shape[0]
    width = w_query.shape[1]
    heads = width // HD
    reach = lax.axis_size("seq") // 2

    halve = lax.axis_size("tp") == 4 and lax.axis_size("seq") == 8
    cosine, sine, extra, marks, w_query, w_key, w_out_part = tables(
        lengths, var_bias, positions, variate, width, (w_query, w_key, w_out), halve
    )
    own_tokens, gain_attn, w_value = fetch((tokens, gain_attn, w_value))
    step = rows // 2
    halves = lax.optimization_barrier((tokens[:step], tokens[step:], tokens))
    pieces = gather_pieces(halves[2], halves[:2], (extra, gain_attn))
    pieces[0] = [own_tokens]
    token_rows, queries, pairs = project(
        pieces, gain_attn, w_query, w_key, w_value, cosine, sine, extra
    )
    w_out_part, _ = lax.optimization_barrier((w_out_part, pairs))
    w_out_pieces = gather_pieces(w_out_part, [w_out_part], (), True)
    if halve:
        twins = [[piece, seq_xor(piece, 1)] for (piece,) in w_out_pieces[1:-1]]
        w_out_pieces = w_out_pieces[:1] + twins + w_out_pieces[-1:]
    row_pieces = seq_pieces(pairs, w_out_pieces[1:-1])
    marks, w_out_pieces = lax.optimization_barrier((marks, w_out_pieces))
    attended, *halves = attend(lengths, queries, marks, row_pieces, heads, reach)
    large = (w_out, token_rows, gain_ffn, w_gate, w_up, w_down)
    large, last = lax.optimization_barrier((large, w_out_pieces[-1], attended))[:2]
    w_out, *large = fetch(large)
    if halve:
        w_out_pieces[0] = [w_out]
        w_out_pieces[-1] = [last[0], seq_xor(last[0], 1)]
    attended_pieces = gather_pieces(attended, halves, large[1:2], True)
    mixed, joined = feed_forward(attended_pieces, w_out_pieces, *large)
    row_pieces, _ = lax.optimization_barrier((row_pieces, joined))
    cache = fill_cache(lengths, page_table, row_pieces, rows)
    return (mixed, cache)


def solution(mesh):
    placed = (
        P("seq", "tp"),
        P("seq"),
        P("seq"),
        P(),
        P(),
        P(),
        P(None, "tp"),
        P(None, "tp"),
        P(None, "tp"),
        P(None, "tp"),
        P("tp", None),
        P(),
        P(None, "tp"),
        P(None, "tp"),
        P("tp", None),
    )
    return jax.shard_map(
        per_device,
        mesh=mesh,
        in_specs=placed,
        out_specs=(P("seq", "tp"), P("seq", None, "tp")),
        check_vma=False,
    )
```

```python
import functools
import math

import jax
import jax.numpy as jnp
from jax import lax
from jax.experimental import pallas as pl
from jax.experimental.pallas import tpu as pltpu
from jax.sharding import PartitionSpec as P

HD = 64
PAGE = 64
VARS = 4
BIAS_PARTS = 3
LANES = 128
HIDDEN_SCORE = -1e30
EPS = 1e-06

VMEM = pl.BlockSpec(memory_space=pltpu.VMEM)
SMEM = pl.BlockSpec(memory_space=pltpu.SMEM)
ANY = pl.BlockSpec(memory_space=pl.ANY)
HBM = pl.BlockSpec(memory_space=pltpu.HBM)


def params(mib):
    return pltpu.CompilerParams(vmem_limit_bytes=mib << 20)


def cost(flops, nbytes, exps=0):
    return pl.CostEstimate(flops=flops, bytes_accessed=nbytes, transcendentals=exps)


def round_up(amount, unit):
    return (amount + unit - 1) // unit * unit


def dot_f32(left, right):
    return jnp.dot(left, right, preferred_element_type=jnp.float32)


def start_loads(sources, targets, sems):
    loads = [
        pltpu.make_async_copy(source, target, sems.at[i])
        for i, (source, target) in enumerate(zip(sources, targets))
    ]
    for load in loads:
        load.start()
    return loads


def finish_loads(loads):
    for load in loads:
        load.wait()


def tp_xor(value, mask):
    return lax.ppermute(value, "tp", [(i, i ^ mask) for i in range(lax.axis_size("tp"))])


def pair_gather(shard, split, before=(), near_first=False):
    far = [tp_xor(part, 2) for part in split]
    near = tp_xor(shard, 1)
    if near_first:
        far[0], _ = lax.optimization_barrier((far[0], near))
    for i, value in enumerate(before):
        far[i], _ = lax.optimization_barrier((far[i], value))
    return [[shard], [near], far, [tp_xor(part, 1) for part in far]]


def turn_gather(shard):
    count = lax.axis_size("tp")
    pairs = [[(i, (i + turn) % count) for i in range(count)] for turn in range(1, count)]
    return [[shard]] + [[lax.ppermute(shard, "tp", each)] for each in pairs]


def direct_gather(shard):
    if lax.axis_size("tp") != 4:
        return turn_gather(shard)
    moved = {mask: tp_xor(shard, mask) for mask in (3, 2, 1)}
    return [[shard]] + [[moved[mask]] for mask in (1, 2, 3)]


def gather_pieces(shard, split, before=(), near_first=False):
    if lax.axis_size("tp") == 4:
        return pair_gather(shard, split, before, near_first)
    return turn_gather(shard)


def piece_place(i, place, count):
    return place ^ i if count == 4 else lax.rem(place + count - i, count)


def nested(counts, refs):
    groups, at = [], 0
    for count in counts:
        groups.append(refs[at : at + count])
        at += count
    return groups, refs[at:]


def request_bounds(lengths):
    starts, ends, total = [], [], 0
    for r in range(lengths.shape[0]):
        starts.append(total)
        total = total + lengths[r]
        ends.append(total)
    return starts, ends


def segments_of(index, ends):
    segment = jnp.zeros_like(index)
    for end in ends:
        segment += (index >= end).astype(jnp.int32)
    return segment


def mark_count(requests):
    return round_up(BIAS_PARTS * VARS + requests, 16)


def tables_kernel(count, lengths, bias, positions, variate, *refs):
    cosine, sine, extra, marks = refs[count : count + 4]
    sources, targets, sems = list(refs[:count]), refs[count + 4 : -1], refs[-1]
    if targets[-1].shape != sources[-1].shape:
        part = targets[-1].shape[1]
        columns = pl.ds(pl.multiple_of(lax.rem(lax.axis_index("seq"), 2) * part, part), part)
        sources[-1] = sources[-1].at[:, columns]
    loads = start_loads(sources, targets, sems)
    rows = positions.shape[1]
    width = cosine.shape[1]
    half = HD // 2
    step = lax.broadcasted_iota(jnp.int32, (half, rows), 0).astype(jnp.float32) / half
    angles = jnp.exp(-math.log(10000.0) * step) * positions[...].astype(jnp.float32)
    cos_rows, sin_rows = jnp.cos(angles), jnp.sin(angles)
    copies = width // HD
    cosine[...] = jnp.transpose(jnp.concatenate([cos_rows, cos_rows] * copies, axis=0))
    sine[...] = jnp.transpose(jnp.concatenate([-sin_rows, sin_rows] * copies, axis=0))

    ids = variate[...].astype(jnp.float32)
    row = lax.broadcasted_iota(jnp.int32, extra.shape, 0)
    below = jnp.zeros(extra.shape, jnp.float32)
    for i in range(rows // extra.shape[1]):
        below = jnp.where(row == i, ids[:, i * extra.shape[1] : (i + 1) * extra.shape[1]], below)
    extra[...] = below.astype(jnp.bfloat16)

    requests = lengths.shape[0]
    shape = (mark_count(requests), rows)
    _, ends = request_bounds(lengths)
    me = lax.axis_index("seq")
    index = lax.broadcasted_iota(jnp.int32, shape, 1) + me * rows
    mark = lax.broadcasted_iota(jnp.int32, shape, 0)
    request = mark - BIAS_PARTS * VARS
    other = (segments_of(index, ends) != request) & (request >= 0) & (request < requests)
    same = (mark % VARS).astype(jnp.float32) == ids
    part = mark // VARS
    for h in range(marks.shape[0]):
        value = jnp.where(same, bias[0, h], bias[1, h])
        high = value.astype(jnp.bfloat16).astype(jnp.float32)
        middle = (value - high).astype(jnp.bfloat16).astype(jnp.float32)
        low = value - high - middle
        column = jnp.where(part == 0, high, jnp.where(part == 1, middle, low))
        column = jnp.where(part < BIAS_PARTS, column, 0.0)
        column = jnp.where(other, HIDDEN_SCORE, column)
        rest = jnp.zeros((LANES - shape[0], rows), jnp.float32)
        marks[h] = jnp.transpose(jnp.concatenate([column, rest], axis=0)).astype(jnp.bfloat16)
    finish_loads(loads)


def tables(lengths, bias, positions, variate, width, arrays, halve):
    rows = positions.shape[0]
    heads = width // HD
    extra = round_up(rows // (2 * width), 16)
    kept = [array.shape for array in arrays]
    if halve:
        kept[-1] = (kept[-1][0], kept[-1][1] // 2)
    return pl.pallas_call(
        functools.partial(tables_kernel, len(arrays)),
        out_shape=[
            jax.ShapeDtypeStruct((rows, width), jnp.float32),
            jax.ShapeDtypeStruct((rows, width), jnp.float32),
            jax.ShapeDtypeStruct((extra, 2 * width), jnp.bfloat16),
            jax.ShapeDtypeStruct((heads, rows, LANES), jnp.bfloat16),
        ]
        + [jax.ShapeDtypeStruct(shape, array.dtype) for shape, array in zip(kept, arrays)],
        in_specs=[SMEM, SMEM, VMEM, VMEM] + [ANY] * len(arrays),
        out_specs=[VMEM] * (4 + len(arrays)),
        scratch_shapes=[pltpu.SemaphoreType.DMA((len(arrays),))],
        compiler_params=params(6),
        cost_estimate=cost(rows * 1024, 1 << 20, rows * 64),
        name="tables",
    )(
        lengths,
        bias,
        positions.reshape(1, rows),
        variate.reshape(1, rows),
        *arrays,
    )


def rotate_lanes(vectors, cosine, signed_sine):
    lane = lax.broadcasted_iota(jnp.int32, vectors.shape, 1)
    half = HD // 2
    ahead = pltpu.roll(vectors, vectors.shape[1] - half, 1)
    behind = pltpu.roll(vectors, half, 1)
    partner = jnp.where(lane % HD < half, ahead, behind)
    return vectors * cosine + partner * signed_sine


def norm_rows(values, gain):
    scale = lax.rsqrt(jnp.mean(values * values, axis=-1, keepdims=True) + EPS)
    return (values * scale * gain).astype(jnp.bfloat16)


def project_kernel(counts, *refs):
    pieces, refs = nested(counts, refs)
    gain, w_q, w_k, w_v, cosine, sine, extra, tokens_out, queries, pairs, tokens, sem = refs
    pairs[tokens.shape[0] :, :] = extra[...]
    place = lax.axis_index("tp")
    part_width = pieces[0][0].shape[1]
    for i, piece in enumerate(pieces):
        block = piece_place(i, place, len(counts))
        columns = pl.ds(pl.multiple_of(block * part_width, part_width), part_width)
        step = tokens.shape[0] // len(piece)
        for j, part in enumerate(piece):
            tokens[j * step : (j + 1) * step, columns] = part[...]
    keep = pltpu.make_async_copy(tokens, tokens_out, sem)
    keep.start()
    rows = tokens.shape[0]
    width = w_q.shape[1]
    step = min(rows, 256)
    gain_row = gain[...].astype(jnp.float32).reshape(1, -1)
    for first in range(0, rows, step):
        part = pl.ds(first, step)
        normed = norm_rows(tokens[part, :].astype(jnp.float32), gain_row)
        cos_part, sin_part = cosine[part, :], sine[part, :]
        query = rotate_lanes(dot_f32(normed, w_q[...]), cos_part, sin_part)
        queries[part, :] = query.astype(jnp.bfloat16) * jnp.bfloat16(HD**-0.5)
        key = rotate_lanes(dot_f32(normed, w_k[...]), cos_part, sin_part)
        pairs[part, :width] = key.astype(jnp.bfloat16)
        pairs[part, width:] = dot_f32(normed, w_v[...]).astype(jnp.bfloat16)
    keep.wait()


def project(pieces, gain, w_query, w_key, w_value, cosine, sine, extra):
    rows = pieces[0][0].shape[0]
    counts = [len(piece) for piece in pieces]
    pieces = [part for piece in pieces for part in piece]
    width = w_query.shape[1]
    features = w_query.shape[0]
    return pl.pallas_call(
        functools.partial(project_kernel, counts),
        out_shape=[
            jax.ShapeDtypeStruct((rows, features), jnp.bfloat16),
            jax.ShapeDtypeStruct((rows, width), jnp.bfloat16),
            jax.ShapeDtypeStruct((rows + extra.shape[0], 2 * width), jnp.bfloat16),
        ],
        in_specs=[VMEM] * (len(pieces) + 7),
        out_specs=[HBM, VMEM, VMEM],
        scratch_shapes=[pltpu.VMEM((rows, features), jnp.bfloat16), pltpu.SemaphoreType.DMA],
        compiler_params=params(5),
        cost_estimate=cost(6 * rows * features * width, 4 << 20),
        name="project",
    )(*pieces, gain, w_query, w_key, w_value, cosine, sine, extra)


def seq_xor(value, mask):
    return lax.ppermute(value, "seq", [(i, i ^ mask) for i in range(lax.axis_size("seq"))])


def seq_pieces(pairs, before):
    if lax.axis_size("seq") == 8:
        diagonal = seq_xor(pairs, 6)
        across = seq_xor(pairs, 2)
        down = seq_xor(pairs, 4)
        twin = seq_xor(pairs, 1)
        (across, down, diagonal), _ = lax.optimization_barrier(((across, down, diagonal), before))
        across_twin = seq_xor(across, 1)
        down_twin = seq_xor(down, 1)
        diagonal_twin = seq_xor(diagonal, 1)
        return [pairs, twin, across, across_twin, down, down_twin, diagonal, diagonal_twin]
    return [lax.all_gather(pairs, "seq", axis=0)]


def piece_copies(pieces, me, wanted):
    if len(pieces) > 1:
        for m, piece in enumerate(pieces):
            wanted(piece, me ^ m)
    else:
        for j in range(pieces[0].shape[0]):
            wanted(pieces[0].at[j], j)


def attend_kernel(count, heads, reach, lengths, queries, query_marks, *refs):
    pieces = refs[:count]
    out, q_buf, k_buf, v_buf, extra_buf, scores, peak, total, sems = refs[count:]
    me = lax.axis_index("seq")
    rows = queries.shape[0]
    _, ends = request_bounds(lengths)
    request_start = 0
    for end in ends:
        request_start = jnp.where(end <= me * rows, end, request_start)
    last = me - request_start // rows
    width = queries.shape[1]

    def copies(source, slot):
        return [
            pltpu.make_async_copy(
                source.at[pl.ds(0, rows), pl.ds(0, width)],
                k_buf.at[slot, :, pl.ds(0, width)],
                sems.at[slot, 0],
            ),
            pltpu.make_async_copy(
                source.at[pl.ds(0, rows), pl.ds(width, width)],
                v_buf.at[slot, :, pl.ds(0, width)],
                sems.at[slot, 1],
            ),
            pltpu.make_async_copy(
                source.at[pl.ds(rows, extra_buf.shape[1]), :], extra_buf.at[slot], sems.at[slot, 2]
            ),
        ]

    def begin(source, block):
        distance = me - block

        @pl.when((distance >= 0) & (distance <= last))
        def _():
            for copy in copies(source, distance):
                copy.start()

    piece_copies(pieces, me, begin)
    example = pieces[0] if count > 1 else pieces[0].at[0]

    marks = mark_count(lengths.shape[0])

    def finish(slot):
        for copy in copies(example, slot):
            copy.wait()
        extra = extra_buf[slot].astype(jnp.float32)
        pair_width = extra.shape[1]
        variates = jnp.concatenate([extra[i : i + 1] for i in range(rows // pair_width)], axis=1)
        mark = lax.broadcasted_iota(jnp.int32, (marks, rows), 0)
        key = lax.broadcasted_iota(jnp.int32, (marks, rows), 1) + (me - slot) * rows
        segment = segments_of(key, ends)
        same_variate = (mark % VARS).astype(jnp.float32) == variates
        same_segment = mark - BIAS_PARTS * VARS == segment
        marked = (same_variate & (mark < BIAS_PARTS * VARS)) | (
            same_segment & (mark >= BIAS_PARTS * VARS)
        )
        columns = jnp.transpose(jnp.where(marked, 1.0, 0.0))
        k_buf[slot, :, width : width + marks] = columns.astype(jnp.bfloat16)

    lane = lax.broadcasted_iota(jnp.int32, (rows, width), 1)
    for h in range(heads):
        part = pl.ds(h * rows, rows)
        q_buf[part, :width] = jnp.where(lane // HD == h, queries[...], jnp.bfloat16(0))
        q_buf[part, width:] = query_marks[h]
    for slot in range(reach + 1):
        v_buf[slot, :, width:] = jnp.ones((rows, LANES), jnp.bfloat16)
        k_buf[slot, :, width:] = jnp.zeros((rows, LANES), jnp.bfloat16)

    def narrow(tile):
        best = tile[:, :LANES]
        for first in range(LANES, rows, LANES):
            best = jnp.maximum(best, tile[:, first : first + LANES])
        return best

    def score(h, slot):
        return lax.dot_general(
            q_buf[pl.ds(h * rows, rows), :],
            k_buf[slot],
            (((1,), (1,)), ((), ())),
            preferred_element_type=jnp.float32,
        )

    finish(0)
    q_at = lax.broadcasted_iota(jnp.int32, (rows, rows), 0)
    k_at = lax.broadcasted_iota(jnp.int32, (rows, rows), 1)
    for h in range(heads):
        tile = jnp.where(k_at <= q_at, score(h, 0), HIDDEN_SCORE)
        scores[h, 0] = tile
        peak[h] = narrow(tile)

    def first_pass(slot, carry):
        finish(slot)
        for h in range(heads):
            tile = score(h, slot)
            scores[h, slot] = tile
            peak[h] = jnp.maximum(peak[h], narrow(tile))
        return carry

    lax.fori_loop(1, last + 1, first_pass, 0)
    for h in range(heads):
        best = jnp.max(peak[h], axis=1, keepdims=True)
        peak[h] = jnp.broadcast_to(best, (rows, LANES))
        total[h] = jnp.zeros_like(total[h])

    def second_pass(slot, carry):
        for h in range(heads):
            best = peak[h]
            wide = jnp.concatenate([best] * (rows // LANES), axis=1)
            weight = jnp.exp(scores[h, slot] - wide).astype(jnp.bfloat16)
            total[h] += dot_f32(weight, v_buf[slot])
        return carry

    lax.fori_loop(0, last + 1, second_pass, 0)
    result = total[0, :, :width] / total[0, :, width:]
    for h in range(1, heads):
        result = jnp.where(lane // HD == h, total[h, :, :width] / total[h, :, width:], result)
    out[...] = result.astype(jnp.bfloat16)


def attend(lengths, queries, query_marks, pieces, heads, reach):
    rows, width = queries.shape
    slots = reach + 1
    return pl.pallas_call(
        functools.partial(attend_kernel, len(pieces), heads, reach),
        out_shape=jax.ShapeDtypeStruct((rows, width), jnp.bfloat16),
        in_specs=[SMEM, VMEM, VMEM] + [ANY] * len(pieces),
        out_specs=VMEM,
        scratch_shapes=[
            pltpu.VMEM((heads * rows, width + LANES), jnp.bfloat16),
            pltpu.VMEM((slots, rows, width + LANES), jnp.bfloat16),
            pltpu.VMEM((slots, rows, width + LANES), jnp.bfloat16),
            pltpu.VMEM((slots, pieces[0].shape[-2] - rows, pieces[0].shape[-1]), jnp.bfloat16),
            pltpu.VMEM((heads, slots, rows, rows), jnp.float32),
            pltpu.VMEM((heads, rows, LANES), jnp.float32),
            pltpu.VMEM((heads, rows, width + LANES), jnp.float32),
            pltpu.SemaphoreType.DMA((slots, 3)),
        ],
        compiler_params=params(8 + 2 * slots),
        cost_estimate=cost(
            4 * heads * rows * rows * slots * 256, 4 << 20, heads * rows * rows * slots
        ),
        name="attend",
    )(lengths, queries, query_marks, *pieces)


def cache_kernel(count, window, lengths, page_table, *refs):
    pieces = refs[:count]
    out, rows_buf, logical, sems = refs[count:]
    rows = rows_buf.shape[1]
    blocks = rows_buf.shape[0]
    width = out.shape[2]
    pages = out.shape[0] // PAGE
    me = lax.axis_index("seq")
    started = []

    def begin(source, block):
        copy = pltpu.make_async_copy(
            source.at[pl.ds(0, rows), :], rows_buf.at[block], sems.at[len(started)]
        )
        copy.start()
        started.append(copy)

    piece_copies(pieces, me, begin)

    def place_page(page, carry):
        local = page_table[page] - me * pages

        @pl.when((local >= 0) & (local < pages))
        def _():
            logical[local] = page

        return carry

    lax.fori_loop(0, page_table.shape[0], place_page, 0)
    starts, _ = request_bounds(lengths)
    for copy in started:
        copy.wait()
    row = lax.broadcasted_iota(jnp.int32, (PAGE, window), 0)
    column = lax.broadcasted_iota(jnp.int32, (PAGE, window), 1)

    def one_page(page, carry):
        first, amount, base = 0, 0, 0
        for r, start in enumerate(starts):
            count_r = (lengths[r] + PAGE - 1) // PAGE
            ahead = (logical[page] - base) * PAGE
            within = (ahead >= 0) & (ahead < lengths[r])
            first = jnp.where(within, start + ahead, first)
            amount = jnp.where(within, jnp.minimum(lengths[r] - ahead, PAGE), amount)
            base = base + count_r
        block = first // rows
        total = None
        for ahead in range(2):
            at = jnp.minimum(block + ahead, blocks - 1)
            inside = first - block * rows
            if ahead == 0:
                start = jnp.minimum(inside // 16 * 16, rows - window)
                offset = inside - start
            else:
                start = 0
                offset = inside - rows
            wanted = (row + offset == column) & (row < amount)
            if ahead == 1:
                wanted = wanted & (block + 1 < blocks)
            chooser = jnp.where(wanted, 1.0, 0.0).astype(jnp.bfloat16)
            found = dot_f32(chooser, rows_buf[at, pl.ds(pl.multiple_of(start, 16), window), :])
            total = found if total is None else total + found
        part = pl.ds(pl.multiple_of(page * PAGE, PAGE), PAGE)
        out[part, 0, :] = total[:, :width].astype(jnp.bfloat16)
        out[part, 1, :] = total[:, width:].astype(jnp.bfloat16)
        return carry

    lax.fori_loop(0, pages, one_page, 0)


def fill_cache(lengths, page_table, pieces, rows):
    width = pieces[0].shape[-1]
    blocks = lax.axis_size("seq")
    pages = page_table.shape[0] // blocks
    return pl.pallas_call(
        functools.partial(cache_kernel, len(pieces), 2 * PAGE),
        out_shape=jax.ShapeDtypeStruct((pages * PAGE, 2, width // 2), jnp.bfloat16),
        in_specs=[SMEM] * 2 + [ANY] * len(pieces),
        out_specs=VMEM,
        scratch_shapes=[
            pltpu.VMEM((blocks, rows, width), jnp.bfloat16),
            pltpu.SMEM((pages,), jnp.int32),
            pltpu.SemaphoreType.DMA((blocks,)),
        ],
        compiler_params=params(8),
        cost_estimate=cost(4 * pages * PAGE * 2 * PAGE * width, 3 << 20),
        name="fill_cache",
    )(lengths, page_table, *pieces)


def fetch_kernel(count, *refs):
    finish_loads(start_loads(refs[:count], refs[count:-1], refs[-1]))


def fetch(arrays):
    return pl.pallas_call(
        functools.partial(fetch_kernel, len(arrays)),
        out_shape=[jax.ShapeDtypeStruct(array.shape, array.dtype) for array in arrays],
        in_specs=[HBM] * len(arrays),
        out_specs=[VMEM] * len(arrays),
        scratch_shapes=[pltpu.SemaphoreType.DMA((len(arrays),))],
        compiler_params=params(10),
        cost_estimate=cost(0, 4 * sum(array.size for array in arrays)),
        name="fetch",
    )(*arrays)


def hidden_kernel(counts, w_counts, *refs):
    pieces, refs = nested(counts, refs)
    w_out_pieces, refs = nested(w_counts, refs)
    tokens, gain, w_gate, w_up, w_down = refs[:5]
    outs, attended, w_out = refs[5:-2], refs[-2], refs[-1]
    hidden, kept = outs[:2]
    places = len(counts)
    place = lax.axis_index("tp")
    core = lax.rem(lax.axis_index("seq"), 2)
    each = pieces[0][0].shape[1]
    for i in range(places):
        inner = slice(i * each, (i + 1) * each)
        step = attended.shape[0] // counts[i]
        for j, part in enumerate(pieces[i]):
            attended[j * step : (j + 1) * step, inner] = part[...]
        if w_counts[i] == 1:
            w_out[inner, :] = w_out_pieces[i][0][...]
            continue
        step = w_out.shape[1] // w_counts[i]
        for j, part in enumerate(w_out_pieces[i]):
            w_out[inner, pl.ds(pl.multiple_of((core ^ j) * step, step), step)] = part[...]
    rows, features = tokens.shape
    width = kept.shape[1]
    step = min(rows, 256)
    gain_row = gain[...].astype(jnp.float32).reshape(1, -1)
    for first in range(0, rows, step):
        part = pl.ds(first, step)
        projected = dot_f32(attended[part, :], w_out[...])
        residual = (tokens[part, :].astype(jnp.float32) + projected).astype(jnp.bfloat16)
        mine = residual[:, :width]
        for i in range(1, places):
            mine = jnp.where(place == i, residual[:, i * width : (i + 1) * width], mine)
        kept[part, :] = mine
        normed = norm_rows(residual.astype(jnp.float32), gain_row)
        gate = dot_f32(normed, w_gate[...])
        up = dot_f32(normed, w_up[...])
        hidden[part, :] = (jax.nn.silu(gate) * up).astype(jnp.bfloat16)
    if len(outs) == 2:
        return
    weights = w_down[:, pl.ds(pl.multiple_of((place ^ 3) * width, width), width)]
    through = dot_f32(hidden[...], weights).astype(jnp.bfloat16)
    outs[2][...] = through[: rows // 2]
    outs[3][...] = through[rows // 2 :]


def hidden_of(pieces, w_out_pieces, tokens, gain, w_gate, w_up, w_down):
    rows, features = tokens.shape
    places = lax.axis_size("tp")
    width = features // places
    units = w_gate.shape[1]
    inner = places * pieces[0][0].shape[1]
    shapes = [(rows, units), (rows, width)] + [(rows // 2, width)] * (2 * (places == 4))
    counts = [[len(piece) for piece in group] for group in (pieces, w_out_pieces)]
    parts = [part for group in (pieces, w_out_pieces) for piece in group for part in piece]
    return pl.pallas_call(
        functools.partial(hidden_kernel, *counts),
        out_shape=[jax.ShapeDtypeStruct(shape, jnp.bfloat16) for shape in shapes],
        in_specs=[VMEM] * (len(parts) + 5),
        out_specs=[VMEM] * len(shapes),
        scratch_shapes=[
            pltpu.VMEM((rows, inner), jnp.bfloat16),
            pltpu.VMEM((inner, features), jnp.bfloat16),
        ],
        compiler_params=params(12),
        cost_estimate=cost(6 * rows * features * units, 10 << 20),
        name="hidden",
    )(*parts, tokens, gain, w_gate, w_up, w_down)


def down_kernel(hidden, kept, w_down, far_top, far_low, near, own):
    place = lax.axis_index("tp")
    rows, width = own.shape

    def product(index):
        weights = w_down[:, pl.ds(pl.multiple_of(index * width, width), width)]
        return dot_f32(hidden[...], weights)

    far = product(place ^ 2)
    far_top[...] = far[: rows // 2]
    far_low[...] = far[rows // 2 :]
    near[...] = product(place ^ 1).astype(jnp.bfloat16)
    own[...] = product(place) + kept[...].astype(jnp.float32)


def down_blocks(hidden, kept, w_down):
    rows, width = kept.shape
    shapes = [((rows // 2, width), jnp.float32)] * 2
    shapes += [((rows, width), jnp.bfloat16), ((rows, width), jnp.float32)]
    return pl.pallas_call(
        down_kernel,
        out_shape=[jax.ShapeDtypeStruct(*shape) for shape in shapes],
        in_specs=[VMEM] * 3,
        out_specs=[VMEM] * 4,
        compiler_params=params(6),
        cost_estimate=cost(2 * rows * w_down.shape[0] * width * 3, 5 << 20),
        name="down_blocks",
    )(hidden, kept, w_down)


def add_kernel(out_parts, *refs):
    whole, parts, out = refs[: -1 - out_parts], refs[-1 - out_parts : -1], refs[-1]
    step = out.shape[0] // max(out_parts, 1)
    for i, first in enumerate(range(0, out.shape[0], step)):
        rows = pl.ds(first, step)
        total = whole[0][rows, :].astype(jnp.float32)
        for ref in whole[1:]:
            total = total + ref[rows, :].astype(jnp.float32)
        if out_parts:
            total = total + parts[i][...].astype(jnp.float32)
        out[rows, :] = total.astype(jnp.bfloat16)


def add_up(whole, parts=()):
    terms = [*whole, *parts]
    size = whole[0].size
    return pl.pallas_call(
        functools.partial(add_kernel, len(parts)),
        out_shape=jax.ShapeDtypeStruct(whole[0].shape, jnp.bfloat16),
        in_specs=[VMEM] * len(terms),
        out_specs=VMEM,
        compiler_params=params(6),
        cost_estimate=cost(size * len(terms), 4 * size * len(terms)),
        name="add_up",
    )(*terms)


def feed_forward(pieces, w_out_pieces, *arrays):
    hidden, kept, *through = hidden_of(pieces, w_out_pieces, *arrays)
    w_down = arrays[-1]
    if lax.axis_size("tp") != 4:
        share = lax.psum_scatter(
            dot_f32(hidden, w_down).astype(jnp.bfloat16), "tp", scatter_dimension=1, tiled=True
        )
        return add_up([kept, share]), hidden
    through = [tp_xor(part, 1) for part in through]
    far_top, far_low, near, own = down_blocks(hidden, kept, w_down)
    joined = [add_up([part, other]) for part, other in zip((far_top, far_low), through)]
    near = tp_xor(near, 1)
    far = [tp_xor(part, 2) for part in joined]
    return add_up([own, near], far), joined[-1]


def per_device(
    tokens,
    variate,
    positions,
    lengths,
    page_table,
    gain_attn,
    w_query,
    w_key,
    w_value,
    var_bias,
    w_out,
    gain_ffn,
    w_gate,
    w_up,
    w_down,
):
    rows = tokens.shape[0]
    width = w_query.shape[1]
    heads = width // HD
    reach = lax.axis_size("seq") // 2

    halve = lax.axis_size("tp") == 4 and lax.axis_size("seq") == 8
    cosine, sine, extra, marks, w_query, w_key, w_out_part = tables(
        lengths, var_bias, positions, variate, width, (w_query, w_key, w_out), halve
    )
    own_tokens, gain_attn, w_value = fetch((tokens, gain_attn, w_value))
    step = rows // 2
    halves = lax.optimization_barrier((tokens[:step], tokens[step:], tokens))
    pieces = gather_pieces(halves[2], halves[:2], (extra, gain_attn))
    pieces[0] = [own_tokens]
    token_rows, queries, pairs = project(
        pieces, gain_attn, w_query, w_key, w_value, cosine, sine, extra
    )
    w_out_part, _ = lax.optimization_barrier((w_out_part, pairs))
    w_out_pieces = gather_pieces(w_out_part, [w_out_part], (), True)
    if halve:
        twins = [[piece, seq_xor(piece, 1)] for (piece,) in w_out_pieces[1:-1]]
        w_out_pieces = w_out_pieces[:1] + twins + w_out_pieces[-1:]
    row_pieces = seq_pieces(pairs, w_out_pieces[1:])
    marks, w_out_pieces = lax.optimization_barrier((marks, w_out_pieces))
    attended = attend(lengths, queries, marks, row_pieces, heads, reach)
    large = (w_out, token_rows, gain_ffn, w_gate, w_up, w_down)
    large, last = lax.optimization_barrier((large, w_out_pieces[-1], attended))[:2]
    w_out, *large = fetch(large)
    if halve:
        w_out_pieces[0] = [w_out]
        w_out_pieces[-1] = [last[0], seq_xor(last[0], 1)]
    attended_pieces = direct_gather(attended)
    mixed, joined = feed_forward(attended_pieces, w_out_pieces, *large)
    row_pieces, _ = lax.optimization_barrier((row_pieces, joined))
    cache = fill_cache(lengths, page_table, row_pieces, rows)
    return (mixed, cache)


def solution(mesh):
    placed = (
        P("seq", "tp"),
        P("seq"),
        P("seq"),
        P(),
        P(),
        P(),
        P(None, "tp"),
        P(None, "tp"),
        P(None, "tp"),
        P(None, "tp"),
        P("tp", None),
        P(),
        P(None, "tp"),
        P(None, "tp"),
        P("tp", None),
    )
    return jax.shard_map(
        per_device,
        mesh=mesh,
        in_specs=placed,
        out_specs=(P("seq", "tp"), P("seq", None, "tp")),
        check_vma=False,
    )
```

```python
import functools
import math

import jax
import jax.numpy as jnp
from jax import lax
from jax.experimental import pallas as pl
from jax.experimental.pallas import tpu as pltpu
from jax.sharding import PartitionSpec as P

HD = 64
PAGE = 64
VARS = 4
BIAS_PARTS = 3
LANES = 128
HIDDEN_SCORE = -1e30
EPS = 1e-06

VMEM = pl.BlockSpec(memory_space=pltpu.VMEM)
SMEM = pl.BlockSpec(memory_space=pltpu.SMEM)
ANY = pl.BlockSpec(memory_space=pl.ANY)
HBM = pl.BlockSpec(memory_space=pltpu.HBM)


def params(mib):
    return pltpu.CompilerParams(vmem_limit_bytes=mib << 20)


def cost(flops, nbytes, exps=0):
    return pl.CostEstimate(flops=flops, bytes_accessed=nbytes, transcendentals=exps)


def round_up(amount, unit):
    return (amount + unit - 1) // unit * unit


def dot_f32(left, right):
    return jnp.dot(left, right, preferred_element_type=jnp.float32)


def start_loads(sources, targets, sems):
    loads = [
        pltpu.make_async_copy(source, target, sems.at[i])
        for i, (source, target) in enumerate(zip(sources, targets))
    ]
    for load in loads:
        load.start()
    return loads


def finish_loads(loads):
    for load in loads:
        load.wait()


def tp_xor(value, mask):
    return lax.ppermute(value, "tp", [(i, i ^ mask) for i in range(lax.axis_size("tp"))])


def pair_gather(shard, split, before=(), near_first=False):
    far = [tp_xor(part, 2) for part in split]
    near = tp_xor(shard, 1)
    if near_first:
        far[0], _ = lax.optimization_barrier((far[0], near))
    for i, value in enumerate(before):
        value = value(far) if callable(value) else value
        far[i], _ = lax.optimization_barrier((far[i], value))
    return [[shard], [near], far, [tp_xor(part, 1) for part in far]]


def turn_gather(shard):
    count = lax.axis_size("tp")
    pairs = [[(i, (i + turn) % count) for i in range(count)] for turn in range(1, count)]
    return [[shard]] + [[lax.ppermute(shard, "tp", each)] for each in pairs]


def direct_gather(shard):
    if lax.axis_size("tp") != 4:
        return turn_gather(shard)
    moved = {mask: tp_xor(shard, mask) for mask in (3, 2, 1)}
    return [[shard]] + [[moved[mask]] for mask in (1, 2, 3)]


def gather_pieces(shard, split, before=(), near_first=False):
    if lax.axis_size("tp") == 4:
        return pair_gather(shard, split, before, near_first)
    return turn_gather(shard)


def piece_place(i, place, count):
    return place ^ i if count == 4 else lax.rem(place + count - i, count)


def nested(counts, refs):
    groups, at = [], 0
    for count in counts:
        groups.append(refs[at : at + count])
        at += count
    return groups, refs[at:]


def request_bounds(lengths):
    starts, ends, total = [], [], 0
    for r in range(lengths.shape[0]):
        starts.append(total)
        total = total + lengths[r]
        ends.append(total)
    return starts, ends


def segments_of(index, ends):
    segment = jnp.zeros_like(index)
    for end in ends:
        segment += (index >= end).astype(jnp.int32)
    return segment


def mark_count(requests):
    return round_up(BIAS_PARTS * VARS + requests, 16)


def tables_kernel(count, lengths, bias, positions, variate, *refs):
    cosine, sine, extra, marks = refs[count : count + 4]
    sources, targets, sems = list(refs[:count]), refs[count + 4 : -1], refs[-1]
    if targets[-1].shape != sources[-1].shape:
        part = targets[-1].shape[1]
        columns = pl.ds(pl.multiple_of(lax.rem(lax.axis_index("seq"), 2) * part, part), part)
        sources[-1] = sources[-1].at[:, columns]
    loads = start_loads(sources, targets, sems)
    rows = positions.shape[1]
    width = cosine.shape[1]
    half = HD // 2
    step = lax.broadcasted_iota(jnp.int32, (half, rows), 0).astype(jnp.float32) / half
    angles = jnp.exp(-math.log(10000.0) * step) * positions[...].astype(jnp.float32)
    cos_rows, sin_rows = jnp.cos(angles), jnp.sin(angles)
    copies = width // HD
    cosine[...] = jnp.transpose(jnp.concatenate([cos_rows, cos_rows] * copies, axis=0))
    sine[...] = jnp.transpose(jnp.concatenate([-sin_rows, sin_rows] * copies, axis=0))

    ids = variate[...].astype(jnp.float32)
    row = lax.broadcasted_iota(jnp.int32, extra.shape, 0)
    below = jnp.zeros(extra.shape, jnp.float32)
    for i in range(rows // extra.shape[1]):
        below = jnp.where(row == i, ids[:, i * extra.shape[1] : (i + 1) * extra.shape[1]], below)
    extra[...] = below.astype(jnp.bfloat16)

    requests = lengths.shape[0]
    shape = (mark_count(requests), rows)
    _, ends = request_bounds(lengths)
    me = lax.axis_index("seq")
    index = lax.broadcasted_iota(jnp.int32, shape, 1) + me * rows
    mark = lax.broadcasted_iota(jnp.int32, shape, 0)
    request = mark - BIAS_PARTS * VARS
    other = (segments_of(index, ends) != request) & (request >= 0) & (request < requests)
    same = (mark % VARS).astype(jnp.float32) == ids
    part = mark // VARS
    for h in range(marks.shape[0]):
        value = jnp.where(same, bias[0, h], bias[1, h])
        high = value.astype(jnp.bfloat16).astype(jnp.float32)
        middle = (value - high).astype(jnp.bfloat16).astype(jnp.float32)
        low = value - high - middle
        column = jnp.where(part == 0, high, jnp.where(part == 1, middle, low))
        column = jnp.where(part < BIAS_PARTS, column, 0.0)
        column = jnp.where(other, HIDDEN_SCORE, column)
        rest = jnp.zeros((LANES - shape[0], rows), jnp.float32)
        marks[h] = jnp.transpose(jnp.concatenate([column, rest], axis=0)).astype(jnp.bfloat16)
    finish_loads(loads)


def tables(lengths, bias, positions, variate, width, arrays, halve):
    rows = positions.shape[0]
    heads = width // HD
    extra = round_up(rows // (2 * width), 16)
    kept = [array.shape for array in arrays]
    if halve:
        kept[-1] = (kept[-1][0], kept[-1][1] // 2)
    return pl.pallas_call(
        functools.partial(tables_kernel, len(arrays)),
        out_shape=[
            jax.ShapeDtypeStruct((rows, width), jnp.float32),
            jax.ShapeDtypeStruct((rows, width), jnp.float32),
            jax.ShapeDtypeStruct((extra, 2 * width), jnp.bfloat16),
            jax.ShapeDtypeStruct((heads, rows, LANES), jnp.bfloat16),
        ]
        + [jax.ShapeDtypeStruct(shape, array.dtype) for shape, array in zip(kept, arrays)],
        in_specs=[SMEM, SMEM, VMEM, VMEM] + [ANY] * len(arrays),
        out_specs=[VMEM] * (4 + len(arrays)),
        scratch_shapes=[pltpu.SemaphoreType.DMA((len(arrays),))],
        compiler_params=params(6),
        cost_estimate=cost(rows * 1024, 1 << 20, rows * 64),
        name="tables",
    )(
        lengths,
        bias,
        positions.reshape(1, rows),
        variate.reshape(1, rows),
        *arrays,
    )


def rotate_lanes(vectors, cosine, signed_sine):
    lane = lax.broadcasted_iota(jnp.int32, vectors.shape, 1)
    half = HD // 2
    ahead = pltpu.roll(vectors, vectors.shape[1] - half, 1)
    behind = pltpu.roll(vectors, half, 1)
    partner = jnp.where(lane % HD < half, ahead, behind)
    return vectors * cosine + partner * signed_sine


def norm_rows(values, gain):
    scale = lax.rsqrt(jnp.mean(values * values, axis=-1, keepdims=True) + EPS)
    return (values * scale * gain).astype(jnp.bfloat16)


def project_kernel(counts, *refs):
    pieces, refs = nested(counts, refs)
    gain, w_q, w_k, w_v, cosine, sine, extra, tokens_out, queries, pairs, tokens, sem = refs
    pairs[tokens.shape[0] :, :] = extra[...]
    place = lax.axis_index("tp")
    part_width = pieces[0][0].shape[1]
    for i, piece in enumerate(pieces):
        block = piece_place(i, place, len(counts))
        columns = pl.ds(pl.multiple_of(block * part_width, part_width), part_width)
        step = tokens.shape[0] // len(piece)
        for j, part in enumerate(piece):
            tokens[j * step : (j + 1) * step, columns] = part[...]
    keep = pltpu.make_async_copy(tokens, tokens_out, sem)
    keep.start()
    rows = tokens.shape[0]
    width = w_q.shape[1]
    step = min(rows, 256)
    gain_row = gain[...].astype(jnp.float32).reshape(1, -1)
    for first in range(0, rows, step):
        part = pl.ds(first, step)
        normed = norm_rows(tokens[part, :].astype(jnp.float32), gain_row)
        cos_part, sin_part = cosine[part, :], sine[part, :]
        query = rotate_lanes(dot_f32(normed, w_q[...]), cos_part, sin_part)
        queries[part, :] = query.astype(jnp.bfloat16) * jnp.bfloat16(HD**-0.5)
        key = rotate_lanes(dot_f32(normed, w_k[...]), cos_part, sin_part)
        pairs[part, :width] = key.astype(jnp.bfloat16)
        pairs[part, width:] = dot_f32(normed, w_v[...]).astype(jnp.bfloat16)
    keep.wait()


def project(pieces, gain, w_query, w_key, w_value, cosine, sine, extra):
    rows = pieces[0][0].shape[0]
    counts = [len(piece) for piece in pieces]
    pieces = [part for piece in pieces for part in piece]
    width = w_query.shape[1]
    features = w_query.shape[0]
    return pl.pallas_call(
        functools.partial(project_kernel, counts),
        out_shape=[
            jax.ShapeDtypeStruct((rows, features), jnp.bfloat16),
            jax.ShapeDtypeStruct((rows, width), jnp.bfloat16),
            jax.ShapeDtypeStruct((rows + extra.shape[0], 2 * width), jnp.bfloat16),
        ],
        in_specs=[VMEM] * (len(pieces) + 7),
        out_specs=[HBM, VMEM, VMEM],
        scratch_shapes=[pltpu.VMEM((rows, features), jnp.bfloat16), pltpu.SemaphoreType.DMA],
        compiler_params=params(5),
        cost_estimate=cost(6 * rows * features * width, 4 << 20),
        name="project",
    )(*pieces, gain, w_query, w_key, w_value, cosine, sine, extra)


def seq_xor(value, mask):
    return lax.ppermute(value, "seq", [(i, i ^ mask) for i in range(lax.axis_size("seq"))])


def seq_pieces(pairs, before):
    if lax.axis_size("seq") == 8:
        diagonal = seq_xor(pairs, 6)
        across = seq_xor(pairs, 2)
        down = seq_xor(pairs, 4)
        twin = seq_xor(pairs, 1)
        (across, down, diagonal), _ = lax.optimization_barrier(((across, down, diagonal), before))
        across_twin = seq_xor(across, 1)
        down_twin = seq_xor(down, 1)
        diagonal_twin = seq_xor(diagonal, 1)
        return [pairs, twin, across, across_twin, down, down_twin, diagonal, diagonal_twin]
    return [lax.all_gather(pairs, "seq", axis=0)]


def piece_copies(pieces, me, wanted):
    if len(pieces) > 1:
        for m, piece in enumerate(pieces):
            wanted(piece, me ^ m)
    else:
        for j in range(pieces[0].shape[0]):
            wanted(pieces[0].at[j], j)


def attend_kernel(count, heads, reach, lengths, queries, query_marks, *refs):
    pieces = refs[:count]
    out, q_buf, k_buf, v_buf, extra_buf, scores, peak, total, sems = refs[count:]
    me = lax.axis_index("seq")
    rows = queries.shape[0]
    _, ends = request_bounds(lengths)
    request_start = 0
    for end in ends:
        request_start = jnp.where(end <= me * rows, end, request_start)
    last = me - request_start // rows
    width = queries.shape[1]

    def copies(source, slot):
        return [
            pltpu.make_async_copy(
                source.at[pl.ds(0, rows), pl.ds(0, width)],
                k_buf.at[slot, :, pl.ds(0, width)],
                sems.at[slot, 0],
            ),
            pltpu.make_async_copy(
                source.at[pl.ds(0, rows), pl.ds(width, width)],
                v_buf.at[slot, :, pl.ds(0, width)],
                sems.at[slot, 1],
            ),
            pltpu.make_async_copy(
                source.at[pl.ds(rows, extra_buf.shape[1]), :], extra_buf.at[slot], sems.at[slot, 2]
            ),
        ]

    def begin(source, block):
        distance = me - block

        @pl.when((distance >= 0) & (distance <= last))
        def _():
            for copy in copies(source, distance):
                copy.start()

    piece_copies(pieces, me, begin)
    example = pieces[0] if count > 1 else pieces[0].at[0]

    marks = mark_count(lengths.shape[0])

    def finish(slot):
        for copy in copies(example, slot):
            copy.wait()
        extra = extra_buf[slot].astype(jnp.float32)
        pair_width = extra.shape[1]
        variates = jnp.concatenate([extra[i : i + 1] for i in range(rows // pair_width)], axis=1)
        mark = lax.broadcasted_iota(jnp.int32, (marks, rows), 0)
        key = lax.broadcasted_iota(jnp.int32, (marks, rows), 1) + (me - slot) * rows
        segment = segments_of(key, ends)
        same_variate = (mark % VARS).astype(jnp.float32) == variates
        same_segment = mark - BIAS_PARTS * VARS == segment
        marked = (same_variate & (mark < BIAS_PARTS * VARS)) | (
            same_segment & (mark >= BIAS_PARTS * VARS)
        )
        columns = jnp.transpose(jnp.where(marked, 1.0, 0.0))
        k_buf[slot, :, width : width + marks] = columns.astype(jnp.bfloat16)

    lane = lax.broadcasted_iota(jnp.int32, (rows, width), 1)
    for h in range(heads):
        part = pl.ds(h * rows, rows)
        q_buf[part, :width] = jnp.where(lane // HD == h, queries[...], jnp.bfloat16(0))
        q_buf[part, width:] = query_marks[h]
    for slot in range(reach + 1):
        v_buf[slot, :, width:] = jnp.ones((rows, LANES), jnp.bfloat16)
        k_buf[slot, :, width:] = jnp.zeros((rows, LANES), jnp.bfloat16)

    def narrow(tile):
        best = tile[:, :LANES]
        for first in range(LANES, rows, LANES):
            best = jnp.maximum(best, tile[:, first : first + LANES])
        return best

    def score(h, slot):
        return lax.dot_general(
            q_buf[pl.ds(h * rows, rows), :],
            k_buf[slot],
            (((1,), (1,)), ((), ())),
            preferred_element_type=jnp.float32,
        )

    finish(0)
    q_at = lax.broadcasted_iota(jnp.int32, (rows, rows), 0)
    k_at = lax.broadcasted_iota(jnp.int32, (rows, rows), 1)
    for h in range(heads):
        tile = jnp.where(k_at <= q_at, score(h, 0), HIDDEN_SCORE)
        scores[h, 0] = tile
        peak[h] = narrow(tile)

    def first_pass(slot, carry):
        finish(slot)
        for h in range(heads):
            tile = score(h, slot)
            scores[h, slot] = tile
            peak[h] = jnp.maximum(peak[h], narrow(tile))
        return carry

    lax.fori_loop(1, last + 1, first_pass, 0)
    for h in range(heads):
        best = jnp.max(peak[h], axis=1, keepdims=True)
        peak[h] = jnp.broadcast_to(best, (rows, LANES))
        total[h] = jnp.zeros_like(total[h])

    def second_pass(slot, carry):
        for h in range(heads):
            best = peak[h]
            wide = jnp.concatenate([best] * (rows // LANES), axis=1)
            weight = jnp.exp(scores[h, slot] - wide).astype(jnp.bfloat16)
            total[h] += dot_f32(weight, v_buf[slot])
        return carry

    lax.fori_loop(0, last + 1, second_pass, 0)
    result = total[0, :, :width] / total[0, :, width:]
    for h in range(1, heads):
        result = jnp.where(lane // HD == h, total[h, :, :width] / total[h, :, width:], result)
    out[...] = result.astype(jnp.bfloat16)


def attend(lengths, queries, query_marks, pieces, heads, reach):
    rows, width = queries.shape
    slots = reach + 1
    return pl.pallas_call(
        functools.partial(attend_kernel, len(pieces), heads, reach),
        out_shape=jax.ShapeDtypeStruct((rows, width), jnp.bfloat16),
        in_specs=[SMEM, VMEM, VMEM] + [ANY] * len(pieces),
        out_specs=VMEM,
        scratch_shapes=[
            pltpu.VMEM((heads * rows, width + LANES), jnp.bfloat16),
            pltpu.VMEM((slots, rows, width + LANES), jnp.bfloat16),
            pltpu.VMEM((slots, rows, width + LANES), jnp.bfloat16),
            pltpu.VMEM((slots, pieces[0].shape[-2] - rows, pieces[0].shape[-1]), jnp.bfloat16),
            pltpu.VMEM((heads, slots, rows, rows), jnp.float32),
            pltpu.VMEM((heads, rows, LANES), jnp.float32),
            pltpu.VMEM((heads, rows, width + LANES), jnp.float32),
            pltpu.SemaphoreType.DMA((slots, 3)),
        ],
        compiler_params=params(8 + 2 * slots),
        cost_estimate=cost(
            4 * heads * rows * rows * slots * 256, 4 << 20, heads * rows * rows * slots
        ),
        name="attend",
    )(lengths, queries, query_marks, *pieces)


def cache_kernel(count, window, lengths, page_table, *refs):
    pieces = refs[:count]
    out, rows_buf, logical, sems = refs[count:]
    rows = rows_buf.shape[1]
    blocks = rows_buf.shape[0]
    width = out.shape[2]
    pages = out.shape[0] // PAGE
    me = lax.axis_index("seq")
    started = []

    def begin(source, block):
        copy = pltpu.make_async_copy(
            source.at[pl.ds(0, rows), :], rows_buf.at[block], sems.at[len(started)]
        )
        copy.start()
        started.append(copy)

    piece_copies(pieces, me, begin)

    def place_page(page, carry):
        local = page_table[page] - me * pages

        @pl.when((local >= 0) & (local < pages))
        def _():
            logical[local] = page

        return carry

    lax.fori_loop(0, page_table.shape[0], place_page, 0)
    starts, _ = request_bounds(lengths)
    for copy in started:
        copy.wait()
    row = lax.broadcasted_iota(jnp.int32, (PAGE, window), 0)
    column = lax.broadcasted_iota(jnp.int32, (PAGE, window), 1)

    def one_page(page, carry):
        first, amount, base = 0, 0, 0
        for r, start in enumerate(starts):
            count_r = (lengths[r] + PAGE - 1) // PAGE
            ahead = (logical[page] - base) * PAGE
            within = (ahead >= 0) & (ahead < lengths[r])
            first = jnp.where(within, start + ahead, first)
            amount = jnp.where(within, jnp.minimum(lengths[r] - ahead, PAGE), amount)
            base = base + count_r
        block = first // rows
        total = None
        for ahead in range(2):
            at = jnp.minimum(block + ahead, blocks - 1)
            inside = first - block * rows
            if ahead == 0:
                start = jnp.minimum(inside // 16 * 16, rows - window)
                offset = inside - start
            else:
                start = 0
                offset = inside - rows
            wanted = (row + offset == column) & (row < amount)
            if ahead == 1:
                wanted = wanted & (block + 1 < blocks)
            chooser = jnp.where(wanted, 1.0, 0.0).astype(jnp.bfloat16)
            found = dot_f32(chooser, rows_buf[at, pl.ds(pl.multiple_of(start, 16), window), :])
            total = found if total is None else total + found
        part = pl.ds(pl.multiple_of(page * PAGE, PAGE), PAGE)
        out[part, 0, :] = total[:, :width].astype(jnp.bfloat16)
        out[part, 1, :] = total[:, width:].astype(jnp.bfloat16)
        return carry

    lax.fori_loop(0, pages, one_page, 0)


def fill_cache(lengths, page_table, pieces, rows):
    width = pieces[0].shape[-1]
    blocks = lax.axis_size("seq")
    pages = page_table.shape[0] // blocks
    return pl.pallas_call(
        functools.partial(cache_kernel, len(pieces), 2 * PAGE),
        out_shape=jax.ShapeDtypeStruct((pages * PAGE, 2, width // 2), jnp.bfloat16),
        in_specs=[SMEM] * 2 + [ANY] * len(pieces),
        out_specs=VMEM,
        scratch_shapes=[
            pltpu.VMEM((blocks, rows, width), jnp.bfloat16),
            pltpu.SMEM((pages,), jnp.int32),
            pltpu.SemaphoreType.DMA((blocks,)),
        ],
        compiler_params=params(8),
        cost_estimate=cost(4 * pages * PAGE * 2 * PAGE * width, 3 << 20),
        name="fill_cache",
    )(lengths, page_table, *pieces)


def fetch_kernel(count, *refs):
    finish_loads(start_loads(refs[:count], refs[count:-1], refs[-1]))


def fetch(arrays):
    return pl.pallas_call(
        functools.partial(fetch_kernel, len(arrays)),
        out_shape=[jax.ShapeDtypeStruct(array.shape, array.dtype) for array in arrays],
        in_specs=[HBM] * len(arrays),
        out_specs=[VMEM] * len(arrays),
        scratch_shapes=[pltpu.SemaphoreType.DMA((len(arrays),))],
        compiler_params=params(10),
        cost_estimate=cost(0, 4 * sum(array.size for array in arrays)),
        name="fetch",
    )(*arrays)


def hidden_kernel(counts, w_counts, *refs):
    pieces, refs = nested(counts, refs)
    w_out_pieces, refs = nested(w_counts, refs)
    tokens, gain, w_gate, w_up, w_down = refs[:5]
    outs, attended, w_out = refs[5:-2], refs[-2], refs[-1]
    hidden, kept = outs[:2]
    places = len(counts)
    place = lax.axis_index("tp")
    core = lax.rem(lax.axis_index("seq"), 2)
    each = pieces[0][0].shape[1]
    for i in range(places):
        inner = slice(i * each, (i + 1) * each)
        step = attended.shape[0] // counts[i]
        for j, part in enumerate(pieces[i]):
            attended[j * step : (j + 1) * step, inner] = part[...]
        if w_counts[i] == 1:
            w_out[inner, :] = w_out_pieces[i][0][...]
            continue
        step = w_out.shape[1] // w_counts[i]
        for j, part in enumerate(w_out_pieces[i]):
            w_out[inner, pl.ds(pl.multiple_of((core ^ j) * step, step), step)] = part[...]
    rows, features = tokens.shape
    width = kept.shape[1]
    step = min(rows, 256)
    gain_row = gain[...].astype(jnp.float32).reshape(1, -1)
    for first in range(0, rows, step):
        part = pl.ds(first, step)
        projected = dot_f32(attended[part, :], w_out[...])
        residual = (tokens[part, :].astype(jnp.float32) + projected).astype(jnp.bfloat16)
        mine = residual[:, :width]
        for i in range(1, places):
            mine = jnp.where(place == i, residual[:, i * width : (i + 1) * width], mine)
        kept[part, :] = mine
        normed = norm_rows(residual.astype(jnp.float32), gain_row)
        gate = dot_f32(normed, w_gate[...])
        up = dot_f32(normed, w_up[...])
        hidden[part, :] = (jax.nn.silu(gate) * up).astype(jnp.bfloat16)
    if len(outs) == 2:
        return
    weights = w_down[:, pl.ds(pl.multiple_of((place ^ 3) * width, width), width)]
    through = dot_f32(hidden[...], weights).astype(jnp.bfloat16)
    outs[2][...] = through[: rows // 2]
    outs[3][...] = through[rows // 2 :]


def hidden_of(pieces, w_out_pieces, tokens, gain, w_gate, w_up, w_down):
    rows, features = tokens.shape
    places = lax.axis_size("tp")
    width = features // places
    units = w_gate.shape[1]
    inner = places * pieces[0][0].shape[1]
    shapes = [(rows, units), (rows, width)] + [(rows // 2, width)] * (2 * (places == 4))
    counts = [[len(piece) for piece in group] for group in (pieces, w_out_pieces)]
    parts = [part for group in (pieces, w_out_pieces) for piece in group for part in piece]
    return pl.pallas_call(
        functools.partial(hidden_kernel, *counts),
        out_shape=[jax.ShapeDtypeStruct(shape, jnp.bfloat16) for shape in shapes],
        in_specs=[VMEM] * (len(parts) + 5),
        out_specs=[VMEM] * len(shapes),
        scratch_shapes=[
            pltpu.VMEM((rows, inner), jnp.bfloat16),
            pltpu.VMEM((inner, features), jnp.bfloat16),
        ],
        compiler_params=params(12),
        cost_estimate=cost(6 * rows * features * units, 10 << 20),
        name="hidden",
    )(*parts, tokens, gain, w_gate, w_up, w_down)


def down_kernel(hidden, kept, w_down, far_top, far_low, near, own):
    place = lax.axis_index("tp")
    rows, width = own.shape

    def product(index):
        weights = w_down[:, pl.ds(pl.multiple_of(index * width, width), width)]
        return dot_f32(hidden[...], weights)

    far = product(place ^ 2)
    far_top[...] = far[: rows // 2]
    far_low[...] = far[rows // 2 :]
    near[...] = product(place ^ 1).astype(jnp.bfloat16)
    own[...] = product(place) + kept[...].astype(jnp.float32)


def down_blocks(hidden, kept, w_down):
    rows, width = kept.shape
    shapes = [((rows // 2, width), jnp.float32)] * 2
    shapes += [((rows, width), jnp.bfloat16), ((rows, width), jnp.float32)]
    return pl.pallas_call(
        down_kernel,
        out_shape=[jax.ShapeDtypeStruct(*shape) for shape in shapes],
        in_specs=[VMEM] * 3,
        out_specs=[VMEM] * 4,
        compiler_params=params(6),
        cost_estimate=cost(2 * rows * w_down.shape[0] * width * 3, 5 << 20),
        name="down_blocks",
    )(hidden, kept, w_down)


def add_kernel(out_parts, *refs):
    whole, parts, out = refs[: -1 - out_parts], refs[-1 - out_parts : -1], refs[-1]
    step = out.shape[0] // max(out_parts, 1)
    for i, first in enumerate(range(0, out.shape[0], step)):
        rows = pl.ds(first, step)
        total = whole[0][rows, :].astype(jnp.float32)
        for ref in whole[1:]:
            total = total + ref[rows, :].astype(jnp.float32)
        if out_parts:
            total = total + parts[i][...].astype(jnp.float32)
        out[rows, :] = total.astype(jnp.bfloat16)


def add_up(whole, parts=()):
    terms = [*whole, *parts]
    size = whole[0].size
    return pl.pallas_call(
        functools.partial(add_kernel, len(parts)),
        out_shape=jax.ShapeDtypeStruct(whole[0].shape, jnp.bfloat16),
        in_specs=[VMEM] * len(terms),
        out_specs=VMEM,
        compiler_params=params(6),
        cost_estimate=cost(size * len(terms), 4 * size * len(terms)),
        name="add_up",
    )(*terms)


def feed_forward(pieces, w_out_pieces, *arrays):
    hidden, kept, *through = hidden_of(pieces, w_out_pieces, *arrays)
    w_down = arrays[-1]
    if lax.axis_size("tp") != 4:
        share = lax.psum_scatter(
            dot_f32(hidden, w_down).astype(jnp.bfloat16), "tp", scatter_dimension=1, tiled=True
        )
        return add_up([kept, share]), hidden
    through = [tp_xor(part, 1) for part in through]
    far_top, far_low, near, own = down_blocks(hidden, kept, w_down)
    joined = [add_up([part, other]) for part, other in zip((far_top, far_low), through)]
    near = tp_xor(near, 1)
    far = [tp_xor(part, 2) for part in joined]
    return add_up([own, near], far), joined[-1]


def per_device(
    tokens,
    variate,
    positions,
    lengths,
    page_table,
    gain_attn,
    w_query,
    w_key,
    w_value,
    var_bias,
    w_out,
    gain_ffn,
    w_gate,
    w_up,
    w_down,
):
    rows = tokens.shape[0]
    width = w_query.shape[1]
    heads = width // HD
    reach = lax.axis_size("seq") // 2

    halve = lax.axis_size("tp") == 4 and lax.axis_size("seq") == 8
    cosine, sine, extra, marks, w_query, w_key, w_out_part = tables(
        lengths, var_bias, positions, variate, width, (w_query, w_key, w_out), halve
    )
    loaded = []

    def load(far):
        operands = lax.optimization_barrier(((tokens, gain_attn, w_value), far[0]))[0]
        loaded.extend(fetch(operands))
        return loaded[1]

    step = rows // 2
    halves = lax.optimization_barrier((tokens[:step], tokens[step:], tokens))
    pieces = gather_pieces(halves[2], halves[:2], (extra, load))
    if loaded:
        own_tokens, gain_attn, w_value = loaded
        pieces[0] = [own_tokens]
    token_rows, queries, pairs = project(
        pieces, gain_attn, w_query, w_key, w_value, cosine, sine, extra
    )
    w_out_part, _ = lax.optimization_barrier((w_out_part, pairs))
    w_out_pieces = gather_pieces(w_out_part, [w_out_part], (), True)
    if halve:
        twins = [[piece, seq_xor(piece, 1)] for (piece,) in w_out_pieces[1:-1]]
        w_out_pieces = w_out_pieces[:1] + twins + w_out_pieces[-1:]
    row_pieces = seq_pieces(pairs, w_out_pieces[1:])
    marks, w_out_pieces = lax.optimization_barrier((marks, w_out_pieces))
    attended = attend(lengths, queries, marks, row_pieces, heads, reach)
    large = (w_out, token_rows, gain_ffn, w_gate, w_up, w_down)
    large, last = lax.optimization_barrier((large, w_out_pieces[-1], attended))[:2]
    w_out, *large = fetch(large)
    if halve:
        w_out_pieces[0] = [w_out]
        w_out_pieces[-1] = [last[0], seq_xor(last[0], 1)]
    attended_pieces = direct_gather(attended)
    mixed, joined = feed_forward(attended_pieces, w_out_pieces, *large)
    row_pieces, _ = lax.optimization_barrier((row_pieces, joined))
    cache = fill_cache(lengths, page_table, row_pieces, rows)
    return (mixed, cache)


def solution(mesh):
    placed = (
        P("seq", "tp"),
        P("seq"),
        P("seq"),
        P(),
        P(),
        P(),
        P(None, "tp"),
        P(None, "tp"),
        P(None, "tp"),
        P(None, "tp"),
        P("tp", None),
        P(),
        P(None, "tp"),
        P(None, "tp"),
        P("tp", None),
    )
    return jax.shard_map(
        per_device,
        mesh=mesh,
        in_specs=placed,
        out_specs=(P("seq", "tp"), P("seq", None, "tp")),
        check_vma=False,
    )
```
